512 devices in a mesh: bx: 16 (over x, z_lo), by: 32 (over z_hi, y, core).
Axes of the slice: x: 4, y: 4, z: 16 (z_hi: 4, z_lo: 4; z = z_hi * 4 + z_lo), core: 2. Of those that a mesh axis runs over, the one named last changes fastest.
Arguments:
- cells_in: float32 [2048, 5, 4096], P(('bx', 'by')), may hold values from -0.5 to 2, as said below
- block_levels: int32 [2048], P(('bx', 'by')), may hold values from 0 to 2
- send_x: int32 [512, 1], P(('bx', 'by')), may hold values from 0 to 3, as said below
- send_y: int32 [512, 1], P(('bx', 'by')), may hold values from 0 to 3, as said below
- layout: int32 [512, 3], P(('bx', 'by')), may hold values from -1 to 5, as said below
- face_out: int32 [512, 4, 4], P(('bx', 'by')), may hold values from 0 to 23, as said below
- ghost_src: int32 [512, 4, 6], P(('bx', 'by')), may hold values from 0 to 39
Outputs:
- cells_out: float32 [1536, 5, 4096], P(('bx', 'by'))
The draws below stay inside these ranges and needn't reach their ends.
Inputs may be any that keep to these rules, and one draw needn't show every extreme that they name: `cells_in`: fields 0 and 4 (density, pressure) lie in 1 to 2, fields 1 to 3 (velocities) in -0.5 to 0.5. Per device, send_x and send_y together name 2 distinct slots. Per device, send_x and send_y together name 2 distinct slots. `layout`: each device's codes name each of 4 to 5 once, at most 1 distinct own slots that neither send list names, and -1 for empty slots; some device keeps 1 own slots and some keeps none. `face_out`: entries are face numbers slot * 6 + face of the sending device, distinct within one device and direction.
All inputs are finite; a program needn't handle non-finite values.
Results may differ from the reference program's by a relative error of at most 0.0003.
Values sent between devices are 32-bit elements; how exact they have to be, the bound alone decides.
No kernel may reach another device: no remote copies, remote signals or barrier semaphores. Data moves between devices by JAX's collectives and lax.ppermute only.
A program may use at most 64 MiB of HBM per device.

```python
import jax
import jax.numpy as jnp
from jax import lax

B = 16
CAP_IN = 4
MOVE = 1
CAP_OUT = 3
GMAX = 4
BLOCKS_IN = 2048
N_BX = 16
N_BY = 32


def draw_cells_in(key, part):
    lower_ends = jnp.array([1.0, -0.5, -0.5, -0.5, 1.0], jnp.float32)[None, :, None]
    upper_ends = jnp.array([2.0, 0.5, 0.5, 0.5, 2.0], jnp.float32)[None, :, None]
    rough = jax.random.uniform(key, (BLOCKS_IN, 5, B * B * B), jnp.float32)
    mixed = rough
    return lower_ends + (upper_ends - lower_ends) * mixed


def migration_lists(key):
    devices = BLOCKS_IN // CAP_IN
    keys_all = jax.random.split(jax.random.fold_in(key, 101), 4)
    perms = jax.vmap(lambda one_key: jax.random.permutation(one_key, CAP_IN))(jax.random.split(keys_all[0], devices)).astype(jnp.int32)
    sent_x = perms[:, :MOVE]
    sent_y = perms[:, MOVE:2 * MOVE]
    spare = perms[:, 2 * MOVE:3 * MOVE]
    device_ids = jnp.arange(devices, dtype=jnp.int32)
    kept = jax.random.randint(keys_all[1], (devices,), 0, MOVE + 1).astype(jnp.int32)
    busiest = jax.random.randint(keys_all[2], (), 0, devices).astype(jnp.int32)
    kept = jnp.where(device_ids == busiest, MOVE, kept)
    kept = jnp.where(device_ids == (busiest + 1) % devices, 0, kept)
    received = jnp.broadcast_to(CAP_IN + jnp.arange(2 * MOVE, dtype=jnp.int32)[None, :], (devices, 2 * MOVE))
    kept_codes = jnp.where(jnp.arange(MOVE, dtype=jnp.int32)[None, :] < kept[:, None], spare, -1)
    slot_codes = jnp.concatenate([received, kept_codes], axis=1)
    orders = jax.vmap(lambda one_key: jax.random.permutation(one_key, CAP_OUT))(jax.random.split(keys_all[3], devices)).astype(jnp.int32)
    placed = jnp.take_along_axis(slot_codes, orders, axis=1).astype(jnp.int32)
    return (sent_x, sent_y, placed)


def draw_send_x(key, part):
    return migration_lists(key)[0]


def draw_send_y(key, part):
    return migration_lists(key)[1]


def draw_layout(key, part):
    return migration_lists(key)[2]


def draw_face_out(key, part):
    devices = BLOCKS_IN // CAP_IN
    perms = jax.vmap(lambda one_key: jax.random.permutation(one_key, 6 * CAP_IN))(jax.random.split(jax.random.fold_in(key, 202), devices * 4))
    return perms[:, :GMAX].reshape(devices, 4, GMAX).astype(jnp.int32)


def draw_ghost_src(key, part):
    devices = BLOCKS_IN // CAP_IN
    keys_all = jax.random.split(jax.random.fold_in(key, 303), 4)
    shape = (devices, CAP_IN, 6)
    chooser = jax.random.randint(keys_all[0], shape, 0, 3)
    local_face = jax.random.randint(keys_all[1], shape, 0, 6 * CAP_IN)
    direction = jax.random.randint(keys_all[2], shape, 0, 4)
    position = jax.random.randint(keys_all[3], shape, 0, GMAX)
    return jnp.where(chooser == 0, local_face, 6 * CAP_IN + direction * GMAX + position).astype(jnp.int32)


def set_ends(entries, rng, smallest, top_value):
    longest = entries.shape.index(max(entries.shape))
    spots = []
    for shift in (0, 1):
        where = [jax.random.randint(jax.random.fold_in(rng, axis), (), 0, length) for axis, length in enumerate(entries.shape)]
        where[longest] = (where[longest] + shift) % entries.shape[longest]
        spots.append(tuple(where))
    return entries.at[spots[0]].set(smallest).at[spots[1]].set(top_value)


def setup_inputs(seed: int = 0) -> dict:
    seeds = jax.random.split(jax.random.key(seed), 8)
    return {
        "cells_in": draw_cells_in(jax.random.fold_in(seeds[7], 71), 0),
        "block_levels": set_ends(jax.random.randint(seeds[1], (BLOCKS_IN,), 0, 3), jax.random.fold_in(seeds[1], 1), 0, 2).astype(jnp.int32),
        "send_x": draw_send_x(jax.random.fold_in(seeds[7], 71), 0),
        "send_y": draw_send_y(jax.random.fold_in(seeds[7], 71), 0),
        "layout": draw_layout(jax.random.fold_in(seeds[7], 71), 0),
        "face_out": draw_face_out(jax.random.fold_in(seeds[7], 71), 0),
        "ghost_src": draw_ghost_src(jax.random.fold_in(seeds[7], 71), 0),
    }


gamma_gas = 1.4
step_base = 0.05

def face_table(blocks):
    number = blocks.shape[0]
    cube_cells = blocks.reshape(number, 5, B, B, B)
    layer_pairs = [(cube_cells[:, :, 0], cube_cells[:, :, 1]), (cube_cells[:, :, B - 1], cube_cells[:, :, B - 2]), (cube_cells[:, :, :, 0], cube_cells[:, :, :, 1]), (cube_cells[:, :, :, B - 1], cube_cells[:, :, :, B - 2]), (cube_cells[:, :, :, :, 0], cube_cells[:, :, :, :, 1]), (cube_cells[:, :, :, :, B - 1], cube_cells[:, :, :, :, B - 2])]
    face_set = jnp.stack([jnp.stack(layer_pair, axis=2) for layer_pair in layer_pairs], axis=1)
    return face_set.reshape(number * 6, 5, 2 * B * B)

def minmod_slope(left_diff, right_diff):
    return 0.5 * (jnp.sign(left_diff) + jnp.sign(right_diff)) * jnp.minimum(jnp.abs(left_diff), jnp.abs(right_diff))

def euler_flux(states, normal):
    density = states[0]
    pressure = states[4]
    normal_vel = states[normal]
    kinetic = 0.5 * density * (states[1] * states[1] + states[2] * states[2] + states[3] * states[3])
    energy = pressure / (gamma_gas - 1.0) + kinetic
    cons_rows = [density] + [density * states[column] for column in range(1, 4)] + [energy]
    flux_rows = [density * normal_vel]
    for column in range(1, 4):
        update_term = density * states[column] * normal_vel
        if column == normal:
            update_term = update_term + pressure
        flux_rows.append(update_term)
    flux_rows.append(normal_vel * (energy + pressure))
    signal = jnp.abs(normal_vel) + jnp.sqrt(gamma_gas * pressure / density)
    return (jnp.stack(flux_rows), jnp.stack(cons_rows), signal)

def sweep(extended, normal, ratio_dt):
    length = extended.shape[1] - 4
    deltas = extended[:, 1:] - extended[:, :-1]
    slopes = minmod_slope(deltas[:, :-1], deltas[:, 1:])
    centre = extended[:, 1:length + 3]
    density = centre[0]
    normal_vel = centre[normal]
    pressure = centre[4]
    advance = [-(normal_vel * slopes[0] + density * slopes[normal])]
    for column in range(1, 4):
        update_term = normal_vel * slopes[column]
        if column == normal:
            update_term = update_term + slopes[4] / density
        advance.append(-update_term)
    advance.append(-(normal_vel * slopes[4] + gamma_gas * pressure * slopes[normal]))
    half_step = 0.5 * ratio_dt * jnp.stack(advance)
    lower_face = centre - 0.5 * slopes + half_step
    upper_face = centre + 0.5 * slopes + half_step
    left_flux, left_cons, left_signal = euler_flux(upper_face[:, :length + 1], normal)
    right_flux, right_cons, right_signal = euler_flux(lower_face[:, 1:length + 2], normal)
    face_flux = 0.5 * (left_flux + right_flux) - 0.5 * jnp.maximum(left_signal, right_signal) * (right_cons - left_cons)
    return face_flux[:, 1:] - face_flux[:, :-1]

def extend_cells(interior, low_side, high_side):
    return jnp.concatenate([low_side[:, 1:2], low_side[:, 0:1], interior, high_side[:, 0:1], high_side[:, 1:2]], axis=1)

def update_block(cells, ghosts, ratio_dt):
    cube_cells = cells.reshape(5, B, B, B)
    ghost_cube = ghosts.reshape(6, 5, 2, B, B)
    along_x = extend_cells(cube_cells, ghost_cube[0], ghost_cube[1]).reshape(5, B + 4, B * B)
    along_y = extend_cells(cube_cells.transpose(0, 2, 1, 3), ghost_cube[2], ghost_cube[3]).reshape(5, B + 4, B * B)
    along_z = extend_cells(cube_cells.transpose(0, 3, 1, 2), ghost_cube[4], ghost_cube[5]).reshape(5, B + 4, B * B)
    change_x = sweep(along_x, 1, ratio_dt).reshape(5, B, B, B)
    change_y = sweep(along_y, 2, ratio_dt).reshape(5, B, B, B).transpose(0, 2, 1, 3)
    change_z = sweep(along_z, 3, ratio_dt).reshape(5, B, B, B).transpose(0, 2, 3, 1)
    flat = cube_cells.reshape(5, B * B * B)
    density = flat[0]
    kinetic = 0.5 * density * (flat[1] * flat[1] + flat[2] * flat[2] + flat[3] * flat[3])
    initial = jnp.stack([density, density * flat[1], density * flat[2], density * flat[3], flat[4] / (gamma_gas - 1.0) + kinetic])
    total = (change_x + change_y + change_z).reshape(5, B * B * B)
    return initial - ratio_dt * total

def reference(cells_in, block_levels, send_x, send_y, layout, face_out, ghost_src):
    devices = N_BX * N_BY
    per_device = 6 * CAP_IN
    device_ids = jnp.arange(devices, dtype=jnp.int32)
    row_index = device_ids // N_BY
    col_index = device_ids % N_BY
    neighbours = jnp.stack([(row_index - 1) % N_BX * N_BY + col_index, (row_index + 1) % N_BX * N_BY + col_index, row_index * N_BY + (col_index - 1) % N_BY, row_index * N_BY + (col_index + 1) % N_BY], axis=1).astype(jnp.int32)
    remote = jnp.maximum(ghost_src - per_device, 0)
    direction = jnp.minimum(remote // GMAX, 3)
    position = remote % GMAX
    sender = neighbours[device_ids[:, None, None], direction]
    remote_face = sender * per_device + face_out[sender, direction, position]
    local_face = device_ids[:, None, None] * per_device + ghost_src
    face_ids = jnp.where(ghost_src < per_device, local_face, remote_face).astype(jnp.int32).reshape(devices * CAP_IN, 6)
    flip_x = N_BX // 2 * N_BY
    flip_y = N_BY // 2
    partner_x = jnp.where(row_index >= N_BX // 2, device_ids - flip_x, device_ids + flip_x).astype(jnp.int32)
    partner_y = jnp.where(col_index >= N_BY // 2, device_ids - flip_y, device_ids + flip_y).astype(jnp.int32)
    own_block = device_ids[:, None] * CAP_IN + jnp.clip(layout, 0, CAP_IN - 1)
    from_x = partner_x[:, None] * CAP_IN + send_x[partner_x[:, None], jnp.clip(layout - CAP_IN, 0, MOVE - 1)]
    from_y = partner_y[:, None] * CAP_IN + send_y[partner_y[:, None], jnp.clip(layout - CAP_IN - MOVE, 0, MOVE - 1)]
    source = jnp.where(layout < CAP_IN, own_block, jnp.where(layout < CAP_IN + MOVE, from_x, from_y)).astype(jnp.int32).reshape(-1)
    filled = layout.reshape(-1) >= 0
    step_sizes = step_base * jnp.exp2(block_levels.astype(jnp.float32))

    def update_one(position_now):
        face_row = face_ids[position_now]
        ghost_list = []
        for face_slot in range(6):
            face_id = face_row[face_slot]
            ghost_list.append(face_table(cells_in[face_id // 6][None])[face_id % 6])
        return update_block(cells_in[position_now], jnp.stack(ghost_list), step_sizes[position_now])
    updated = lax.map(update_one, source)
    return jnp.where(filled[:, None, None], updated, jnp.zeros_like(updated))
```

```python
import functools

import jax
import jax.numpy as jnp
from jax import lax
from jax.experimental import pallas as pl
from jax.experimental.pallas import tpu as pltpu
from jax.sharding import PartitionSpec as P

B = 16
GAMMA = 1.4
STEP = 0.05
HALF = 8
FIELD_ROWS = B * 8
SWEEP_ROWS = 5 * FIELD_ROWS
BLOCK_ROWS = 5 * 2 * B
FACE_ROWS = 24
GHOST_ROWS = 4 * 8


def slot_of(field, direction):
    if field == 1:
        return 1 + direction
    if field == 1 + direction:
        return 1
    return field


def lanes(shape=(8, 128)):
    return lax.broadcasted_iota(jnp.int32, shape, 1)


def rows(shape=(8, 128)):
    return lax.broadcasted_iota(jnp.int32, shape, 0)


def take(values, index, axis):
    return jnp.take_along_axis(values, index, axis=axis, mode="promise_in_bounds")


class Turns:
    def __init__(self):
        lane, row = lanes(), rows()
        group, inner = lane // 16, lane % 16
        self.low = inner < 8
        self.skew = ((group + row) % 8) * 16 + inner
        self.shift = (row - group) % 8
        self.back = ((row - group) % 8) * 16 + inner
        source_group = (group + row) % 8
        self.skew_z = (inner % 8) * 16 + (inner // 8) * 8 + source_group
        z_low, z_high = inner % 8, inner // 8
        self.back_z = ((row - z_low) % 8) * 16 + z_high * 8 + group

    def turn(self, v):
        return take(take(take(v, self.skew, 1), self.shift, 0), self.back, 1)

    def to_z(self, v0, v1):
        t0 = take(take(take(v0, self.skew_z, 1), self.shift, 0), self.back, 1)
        t1 = take(take(take(v1, self.skew_z, 1), self.shift, 0), self.back, 1)
        first = jnp.where(self.low, t0, pltpu.roll(t1, 8, 1))
        second = jnp.where(self.low, pltpu.roll(t0, 120, 1), t1)
        return first, second

    def from_z(self, first, second):
        t0 = jnp.where(self.low, first, pltpu.roll(second, 8, 1))
        t1 = jnp.where(self.low, pltpu.roll(first, 120, 1), second)
        return tuple(
            take(take(take(t, self.skew, 1), self.shift, 0), self.back_z, 1) for t in (t0, t1)
        )


def pack_kernel(face_out, lists, cells, sweep, table, *messages):
    turns = Turns()
    for s in range(4):
        for t in range(2 * B):
            x, h = t // 2, t % 2
            sweep[s, pl.ds(x * 8 + h, 5, stride=FIELD_ROWS), :] = cells[
                s, :, t * 128 : (t + 1) * 128
            ]
        for field in range(5):
            base = field * FIELD_ROWS
            to_y = slot_of(field, 1) * FIELD_ROWS
            to_z = slot_of(field, 2) * FIELD_ROWS
            for xh in range(2):
                v = [
                    sweep[s, pl.ds(base + HALF * xh * 8 + h, 8, stride=8), :] for h in range(2)
                ]
                for h in range(2):
                    start = to_y + HALF * h * 8 + 2 + xh
                    sweep[s, pl.ds(start, 8, stride=8), :] = turns.turn(v[h])
                for zh, value in enumerate(turns.to_z(v[0], v[1])):
                    start = to_z + HALF * zh * 8 + 4 + xh
                    sweep[s, pl.ds(start, 8, stride=8), :] = value
        for face in range(6):
            direction, high = face // 2, face % 2
            for layer in range(2):
                i = B - 1 - layer if high else layer
                for h in range(2):
                    row = i * 8 + direction * 2 + h
                    to = (layer * 2 + h) * 5
                    table[s * 6 + face, to : to + 5, :] = sweep[
                        s, pl.ds(row, 5, stride=FIELD_ROWS), :
                    ]
                    if direction:
                        for field, slot in ((1, 1 + direction), (1 + direction, 1)):
                            table[s * 6 + face, to + field : to + field + 1, :] = sweep[
                                s, pl.ds(slot * FIELD_ROWS + row, 1), :
                            ]
    for m in range(4):
        listed = lists[m]
        for k in range(4):
            messages[m][k] = table[face_out[0, listed, k]]


def limited(left, right):
    return jnp.maximum(jnp.minimum(left, right), 0.0) + jnp.minimum(jnp.maximum(left, right), 0.0)


def fluxes_of(q):
    density, normal, second, third, pressure = q
    mass = density * normal
    kinetic = 0.5 * density * (normal * normal + second * second + third * third)
    energy = pressure * (1.0 / (GAMMA - 1.0)) + kinetic
    cons = (density, mass, density * second, density * third, energy)
    flux = (mass, mass * normal + pressure, mass * second, mass * third, normal * (energy + pressure))
    scaled = GAMMA * pressure
    signal = jnp.abs(normal) + scaled * lax.rsqrt(scaled * density)
    return cons, flux, signal


def step_of(level):
    return jnp.where(level == 0, STEP, jnp.where(level == 1, STEP * 2, STEP * 4))


def update_kernel(slot, levels, ghost_src, order, sweep, table, r0, r1, r2, r3, out, remote, ghost, change):
    turns = Turns()
    s = slot[0]
    ratio = step_of(levels[s])
    for m, received in enumerate((r0, r1, r2, r3)):
        for k in range(4):
            remote[m * 4 + k] = received[k]
    for face in range(6):
        direction, high = face // 2, face % 2
        code = ghost_src[0, s, face]
        far = jnp.maximum(code - 24, 0)
        far = order[far // 4] * 4 + far % 4
        near = jnp.minimum(code, 23)
        for layer in range(2):
            i = 2 + layer if high else 1 - layer
            for h in range(2):
                row = i * 8 + direction * 2 + h
                at = (layer * 2 + h) * 5
                moves = [(pl.ds(at, 5), pl.ds(row, 5, stride=GHOST_ROWS))]
                if direction:
                    for field, to in ((1, 1 + direction), (1 + direction, 1)):
                        moves.append((pl.ds(at + field, 1), pl.ds(to * GHOST_ROWS + row, 1)))
                for source, target in moves:
                    ghost[target, :] = jnp.where(
                        code < 24, table[near, source, :], remote[far, source, :]
                    )

    def cells_at(i):
        if 0 <= i < B:
            return [sweep[s, pl.ds(f * FIELD_ROWS + i * 8, 8), :] for f in range(5)]
        k = i + 2 if i < 0 else i - B + 2
        return [ghost[pl.ds(f * GHOST_ROWS + k * 8, 8), :] for f in range(5)]

    here, after = cells_at(-2), cells_at(-1)
    right = [b - a for a, b in zip(here, after)]
    left_face = last_flux = None
    for i in range(-1, B + 1):
        here, after, left = after, cells_at(i + 2 - 1), right
        right = [b - a for a, b in zip(here, after)]
        half = [0.5 * limited(a, b) for a, b in zip(left, right)]
        density, normal, _, _, pressure = here
        carried = ratio * normal
        moved = [carried * a for a in half]
        centre = [
            density - (moved[0] + ratio * density * half[1]),
            normal - (moved[1] + ratio * half[4] / density),
            here[2] - moved[2],
            here[3] - moved[3],
            pressure - (moved[4] + (ratio * GAMMA) * pressure * half[1]),
        ]
        if i >= 0:
            cons, flux, signal = fluxes_of([a - b for a, b in zip(centre, half)])
            old_cons, old_flux, old_signal = left_face
            speed = jnp.maximum(signal, old_signal)
            face_flux = [
                (fa + fb) - speed * (ub - ua)
                for fa, fb, ua, ub in zip(old_flux, flux, old_cons, cons)
            ]
            if i >= 1:
                for f in range(5):
                    change[pl.ds(f * FIELD_ROWS + (i - 1) * 8, 8), :] = face_flux[f] - last_flux[f]
            last_flux = face_flux
        if i < B:
            left_face = fluxes_of([a + b for a, b in zip(centre, half)])

    def in_place(ref, start):
        return ref[pl.ds(start, 8, stride=8), :]

    scale = 0.5 * ratio
    for xh in range(2):
        prims = [
            [sweep[s, pl.ds(f * FIELD_ROWS + HALF * xh * 8 + h, 8, stride=8), :] for h in range(2)]
            for f in range(5)
        ]
        for f in range(5):
            along_y = slot_of(f, 1) * FIELD_ROWS
            along_z = slot_of(f, 2) * FIELD_ROWS
            from_z = turns.from_z(
                *[in_place(change, along_z + HALF * zh * 8 + 4 + xh) for zh in range(2)]
            )
            for h in range(2):
                total = (
                    in_place(change, f * FIELD_ROWS + HALF * xh * 8 + h)
                    + turns.turn(in_place(change, along_y + HALF * h * 8 + 2 + xh))
                    + from_z[h]
                )
                density, u, v, w, pressure = (prims[k][h] for k in range(5))
                if f == 0:
                    initial = density
                elif f < 4:
                    initial = density * prims[f][h]
                else:
                    initial = pressure * (1.0 / (GAMMA - 1.0)) + 0.5 * density * (
                        u * u + v * v + w * w
                    )
                row = f * 2 * B + h * B + HALF * xh
                out[row : row + 8, :] = initial - scale * total


def place_kernel(layout, own, from_x, from_y, out):
    codes = [layout[0, j] for j in range(3)]
    at_x = jnp.where(codes[1] == 4, 1, jnp.where(codes[2] == 4, 2, 0))
    at_y = jnp.where(codes[1] == 5, 1, jnp.where(codes[2] == 5, 2, 0))
    at_own = 3 - at_x - at_y
    empty = codes[0] + codes[1] + codes[2] == 8
    for source, at in ((own, at_own), (from_x, at_x), (from_y, at_y)):
        for t in range(2 * B):
            row = (t % 2) * B + t // 2
            v = source[pl.ds(row, 5, stride=2 * B), :]
            if source is own:
                v = jnp.where(empty, 0.0, v)
            out[at, :, t * 128 : (t + 1) * 128] = v


SMEM = pl.BlockSpec(memory_space=pltpu.SMEM)
VMEM = pl.BlockSpec(memory_space=pltpu.VMEM)
LIMIT = 48 << 20


def struct(*shape):
    return jax.ShapeDtypeStruct(shape, jnp.float32)


def pack(face_out, lists, cells):
    return pl.pallas_call(
        pack_kernel,
        out_shape=(struct(4, SWEEP_ROWS, 128), struct(24, FACE_ROWS, 128))
        + (struct(4, FACE_ROWS, 128),) * 4,
        in_specs=[SMEM, SMEM, VMEM],
        out_specs=(VMEM,) * 6,
        compiler_params=pltpu.CompilerParams(vmem_limit_bytes=LIMIT),
        name="pack",
    )(face_out, lists, cells)


def update(name, slot, levels, ghost_src, order, sweep, table, received):
    return pl.pallas_call(
        update_kernel,
        out_shape=struct(BLOCK_ROWS, 128),
        in_specs=[SMEM] * 4 + [VMEM] * 6,
        out_specs=VMEM,
        scratch_shapes=[
            pltpu.VMEM((16, FACE_ROWS, 128), jnp.float32),
            pltpu.VMEM((5 * GHOST_ROWS, 128), jnp.float32),
            pltpu.VMEM((SWEEP_ROWS, 128), jnp.float32),
        ],
        compiler_params=pltpu.CompilerParams(vmem_limit_bytes=LIMIT),
        name=name,
    )(slot, levels, ghost_src, order, sweep, table, *received)


def place(layout, own, from_x, from_y):
    return pl.pallas_call(
        place_kernel,
        out_shape=struct(3, 5, B * B * B),
        in_specs=[SMEM] + [VMEM] * 3,
        out_specs=VMEM,
        compiler_params=pltpu.CompilerParams(vmem_limit_bytes=LIMIT),
        name="place",
    )(layout, own, from_x, from_y)


def with_pair(values, axis, odd):
    count = lax.axis_size(axis)
    mate = [((i + odd) ^ 1) - odd for i in range(count)]
    return lax.ppermute(values, axis, [(i, j % count) for i, j in enumerate(mate)])


def with_partner(values, axis):
    count = lax.axis_size(axis)
    return lax.ppermute(values, axis, [(i, i ^ (count // 2)) for i in range(count)])


def on_device(cells_in, block_levels, send_x, send_y, layout, face_out, ghost_src):
    odd_x = lax.axis_index("bx") % 2
    odd_y = lax.axis_index("by") % 2
    lists = jnp.stack([odd_x, 1 - odd_x, 2 + odd_y, 3 - odd_y]).astype(jnp.int32)
    order = jnp.stack([1 - odd_x, odd_x, 3 - odd_y, 2 + odd_y]).astype(jnp.int32)
    sweep, table, *messages = pack(face_out, lists, cells_in)
    received = [
        with_pair(messages[0], "bx", 0),
        with_pair(messages[1], "bx", 1),
        with_pair(messages[2], "by", 0),
        with_pair(messages[3], "by", 1),
    ]
    own_slot = jnp.max(jnp.where(layout < 4, layout, 0), axis=1)
    common = (block_levels, ghost_src, order, sweep, table, received)
    from_y = with_partner(update("to_y", send_y[0], *common), "by")
    from_x = with_partner(update("to_x", send_x[0], *common), "bx")
    own = update("own", own_slot, *common)
    return place(layout, own, from_x, from_y)


def solution(mesh):
    return jax.shard_map(
        on_device,
        mesh=mesh,
        in_specs=(
            P(("bx", "by"), None, None),
            P(("bx", "by")),
            P(("bx", "by"), None),
            P(("bx", "by"), None),
            P(("bx", "by"), None),
            P(("bx", "by"), None, None),
            P(("bx", "by"), None, None),
        ),
        out_specs=P(("bx", "by"), None, None),
        check_vma=False,
    )
```

```python
import functools

import jax
import jax.numpy as jnp
from jax import lax
from jax.experimental import pallas as pl
from jax.experimental.pallas import tpu as pltpu
from jax.sharding import PartitionSpec as P

B = 16
GAMMA = 1.4
STEP = 0.05
HALF = 8
FIELD_ROWS = B * 8
SWEEP_ROWS = 5 * FIELD_ROWS
BLOCK_ROWS = 5 * 2 * B
FACE_ROWS = 24
GHOST_ROWS = 4 * 8


def slot_of(field, direction):
    if field == 1:
        return 1 + direction
    if field == 1 + direction:
        return 1
    return field


def lanes(shape=(8, 128)):
    return lax.broadcasted_iota(jnp.int32, shape, 1)


def rows(shape=(8, 128)):
    return lax.broadcasted_iota(jnp.int32, shape, 0)


def take(values, index, axis):
    return jnp.take_along_axis(values, index, axis=axis, mode="promise_in_bounds")


class Turns:
    def __init__(self):
        lane, row = lanes(), rows()
        group, inner = lane // 16, lane % 16
        self.low = inner < 8
        self.skew = ((group + row) % 8) * 16 + inner
        self.shift = (row - group) % 8
        self.back = ((row - group) % 8) * 16 + inner
        self.skew_half = ((group + row) % 8) * 16 + (inner + 8) % 16
        self.back_half = ((row - group) % 8) * 16 + (inner + 8) % 16
        source_group = (group + row) % 8
        self.skew_z = (inner % 8) * 16 + (inner // 8) * 8 + source_group
        z_low, z_high = inner % 8, inner // 8
        self.back_z = ((row - z_low) % 8) * 16 + z_high * 8 + group

    def turn(self, v):
        return take(take(take(v, self.skew, 1), self.shift, 0), self.back, 1)

    def to_z(self, v0, v1):
        t0 = take(take(v0, self.skew_z, 1), self.shift, 0)
        t1 = take(take(v1, self.skew_z, 1), self.shift, 0)
        first = jnp.where(self.low, take(t0, self.back, 1), take(t1, self.back_half, 1))
        second = jnp.where(self.low, take(t0, self.back_half, 1), take(t1, self.back, 1))
        return first, second

    def from_z(self, first, second):
        t0 = jnp.where(self.low, take(first, self.skew, 1), take(second, self.skew_half, 1))
        t1 = jnp.where(self.low, take(first, self.skew_half, 1), take(second, self.skew, 1))
        return tuple(take(take(t, self.shift, 0), self.back_z, 1) for t in (t0, t1))


def parities():
    return lax.axis_index("bx") % 2, lax.axis_index("by") % 2


def pack_kernel(
    send_x, send_y, cells_in, layout_in, levels_in, ghost_src_in, face_out_in, *rest
):
    numbers, sweep, table, *messages = rest[:7]
    cells, layout, levels, ghost_src, face_out, cells_sem, small_sem = rest[7:]
    odd_x, odd_y = parities()
    copies = [
        pltpu.make_async_copy(cells_in.at[f], cells.at[f], cells_sem.at[f]) for f in range(5)
    ]
    small = [
        pltpu.make_async_copy(source, target, small_sem.at[i])
        for i, (source, target) in enumerate(
            (
                (face_out_in, face_out),
                (layout_in, layout),
                (levels_in, levels),
                (ghost_src_in, ghost_src),
            )
        )
    ]
    for copy in copies + small:
        copy.start()
    turns = Turns()
    for field in range(5):
        base = field * FIELD_ROWS
        to_y = slot_of(field, 1) * FIELD_ROWS
        to_z = slot_of(field, 2) * FIELD_ROWS
        copies[field].wait()
        for t in range(2 * B):
            row = base + (t // 2) * 8 + t % 2
            sweep[pl.ds(row, 4, stride=SWEEP_ROWS), :] = cells[
                field, :, t * 128 : (t + 1) * 128
            ]
        for first in range(0, 4 * SWEEP_ROWS, SWEEP_ROWS):
            for xh in range(2):
                v = [
                    sweep[pl.ds(first + base + HALF * xh * 8 + h, 8, stride=8), :]
                    for h in range(2)
                ]
                for h in range(2):
                    start = first + to_y + HALF * h * 8 + 2 + xh
                    sweep[pl.ds(start, 8, stride=8), :] = turns.turn(v[h])
                for zh, value in enumerate(turns.to_z(v[0], v[1])):
                    start = first + to_z + HALF * zh * 8 + 4 + xh
                    sweep[pl.ds(start, 8, stride=8), :] = value
    for s in range(4):
        for face in range(6):
            direction, high = face // 2, face % 2
            for layer in range(2):
                i = B - 1 - layer if high else layer
                for h in range(2):
                    row = s * SWEEP_ROWS + i * 8 + direction * 2 + h
                    to = (layer * 2 + h) * 5
                    table[s * 6 + face, to : to + 5, :] = sweep[
                        pl.ds(row, 5, stride=FIELD_ROWS), :
                    ]
                    if direction:
                        for field, slot in ((1, 1 + direction), (1 + direction, 1)):
                            table[s * 6 + face, to + field : to + field + 1, :] = sweep[
                                pl.ds(slot * FIELD_ROWS + row, 1), :
                            ]
    for copy in small:
        copy.wait()
    for m, one_list in enumerate((2 + (1 - odd_y), 1 - odd_x, odd_x, 2 + odd_y)):
        for k in range(4):
            messages[m][k] = table[face_out[0, one_list, k]]
    codes = [layout[0, j] for j in range(3)]
    kept = functools.reduce(jnp.maximum, [jnp.where(c < 4, c, 0) for c in codes])
    listed = {0: send_x[0, 0], 1: send_y[0, 0], 2: kept}
    listed.update({3 + j: codes[j] for j in range(3)})
    listed.update({8 + j: levels[j] for j in range(4)})
    listed.update({12 + s * 6 + f: ghost_src[0, s, f] for s in range(4) for f in range(6)})
    lane = lanes((1, 128))
    row = jnp.zeros((1, 128), jnp.int32)
    for i, number in listed.items():
        row = jnp.where(lane == i, number, row)
    numbers[...] = row


def limited(left, right):
    return jnp.maximum(jnp.minimum(left, right), 0.0) + jnp.minimum(jnp.maximum(left, right), 0.0)


def fluxes_of(q):
    density, normal, second, third, pressure = q
    mass = density * normal
    kinetic = 0.5 * density * (normal * normal + second * second + third * third)
    energy = pressure * (1.0 / (GAMMA - 1.0)) + kinetic
    cons = (density, mass, density * second, density * third, energy)
    flux = (mass, mass * normal + pressure, mass * second, mass * third, normal * (energy + pressure))
    scaled = GAMMA * pressure
    signal = jnp.abs(normal) + scaled * lax.rsqrt(scaled * density)
    return cons, flux, signal


def step_of(level):
    return jnp.where(level == 0, STEP, jnp.where(level == 1, STEP * 2, STEP * 4))


def update_kernel(which_block, more, numbers, sweep, table, r0, r1, r2, r3, *rest):
    out, remote, ghost, change = rest[-4:]
    turns = Turns()
    odd_x, odd_y = parities()
    s = numbers[0, which_block]
    ratio = step_of(numbers[0, 8 + s])
    for m, received in enumerate((r0, r1, r2, r3)):
        for k in range(4):
            remote[m * 4 + k] = received[k]
    for face in range(6):
        direction, high = face // 2, face % 2
        code = numbers[0, 12 + s * 6 + face]
        far = jnp.maximum(code - 24, 0)
        which = far // 4
        along_x = jnp.where(which == odd_x, 1, 2)
        along_y = jnp.where(which - 2 == odd_y, 0, 3)
        far = jnp.where(which < 2, along_x, along_y) * 4 + far % 4
        near = jnp.minimum(code, 23)
        for layer in range(2):
            i = 2 + layer if high else 1 - layer
            for h in range(2):
                row = i * 8 + direction * 2 + h
                at = (layer * 2 + h) * 5
                moves = [(pl.ds(at, 5), pl.ds(row, 5, stride=GHOST_ROWS))]
                if direction:
                    for field, to in ((1, 1 + direction), (1 + direction, 1)):
                        moves.append((pl.ds(at + field, 1), pl.ds(to * GHOST_ROWS + row, 1)))
                for source, target in moves:
                    ghost[target, :] = jnp.where(
                        code < 24, table[near, source, :], remote[far, source, :]
                    )

    def cells_at(i):
        if 0 <= i < B:
            return [sweep[s, pl.ds(f * FIELD_ROWS + i * 8, 8), :] for f in range(5)]
        k = i + 2 if i < 0 else i - B + 2
        return [ghost[pl.ds(f * GHOST_ROWS + k * 8, 8), :] for f in range(5)]

    here, after = cells_at(-2), cells_at(-1)
    right = [b - a for a, b in zip(here, after)]
    left_face = last_flux = None
    for i in range(-1, B + 1):
        here, after, left = after, cells_at(i + 2 - 1), right
        right = [b - a for a, b in zip(here, after)]
        half = [0.5 * limited(a, b) for a, b in zip(left, right)]
        density, normal, _, _, pressure = here
        carried = ratio * normal
        moved = [carried * a for a in half]
        centre = [
            density - (moved[0] + ratio * density * half[1]),
            normal - (moved[1] + ratio * half[4] / density),
            here[2] - moved[2],
            here[3] - moved[3],
            pressure - (moved[4] + (ratio * GAMMA) * pressure * half[1]),
        ]
        if i >= 0:
            cons, flux, signal = fluxes_of([a - b for a, b in zip(centre, half)])
            old_cons, old_flux, old_signal = left_face
            speed = jnp.maximum(signal, old_signal)
            face_flux = [
                (fa + fb) - speed * (ub - ua)
                for fa, fb, ua, ub in zip(old_flux, flux, old_cons, cons)
            ]
            if i >= 1:
                for f in range(5):
                    change[pl.ds(f * FIELD_ROWS + (i - 1) * 8, 8), :] = face_flux[f] - last_flux[f]
            last_flux = face_flux
        if i < B:
            left_face = fluxes_of([a + b for a, b in zip(centre, half)])

    if more:
        out[BLOCK_ROWS : BLOCK_ROWS + 8, :] = jnp.zeros((8, 128), jnp.float32)

    def in_place(ref, start):
        return ref[pl.ds(start, 8, stride=8), :]

    scale = 0.5 * ratio
    for xh in range(2):
        prims = [
            [sweep[s, pl.ds(f * FIELD_ROWS + HALF * xh * 8 + h, 8, stride=8), :] for h in range(2)]
            for f in range(5)
        ]
        for f in range(5):
            along_y = slot_of(f, 1) * FIELD_ROWS
            along_z = slot_of(f, 2) * FIELD_ROWS
            from_z = turns.from_z(
                *[in_place(change, along_z + HALF * zh * 8 + 4 + xh) for zh in range(2)]
            )
            for h in range(2):
                total = (
                    in_place(change, f * FIELD_ROWS + HALF * xh * 8 + h)
                    + turns.turn(in_place(change, along_y + HALF * h * 8 + 2 + xh))
                    + from_z[h]
                )
                density, u, v, w, pressure = (prims[k][h] for k in range(5))
                if f == 0:
                    initial = density
                elif f < 4:
                    initial = density * prims[f][h]
                else:
                    initial = pressure * (1.0 / (GAMMA - 1.0)) + 0.5 * density * (
                        u * u + v * v + w * w
                    )
                row = f * 2 * B + h * B + HALF * xh
                out[row : row + 8, :] = initial - scale * total


def place_kernel(numbers, from_y, from_x, own, out, slots, staged, sems):
    codes = [numbers[0, 3 + j] for j in range(3)]
    at_x = jnp.where(codes[1] == 4, 1, jnp.where(codes[2] == 4, 2, 0))
    at_y = jnp.where(codes[1] == 5, 1, jnp.where(codes[2] == 5, 2, 0))
    at_own = 3 - at_x - at_y
    empty = codes[0] + codes[1] + codes[2] == 8
    copies = []
    for f in range(5):
        for source, at in ((own, at_own), (from_x, at_x), (from_y, at_y)):
            v = source[f * 2 * B : (f + 1) * 2 * B, :]
            if source is own:
                v = jnp.where(empty, 0.0, v)
            slots[pl.ds(pl.multiple_of(at * BLOCK_ROWS + f * 2 * B, 2 * B), 2 * B), :] = v
        for t in range(2 * B):
            row = f * 2 * B + (t % 2) * B + t // 2
            staged[f, :, t * 128 : (t + 1) * 128] = slots[pl.ds(row, 3, stride=BLOCK_ROWS), :]
        copies.append(pltpu.make_async_copy(staged.at[f], out.at[f], sems.at[f]))
        copies[-1].start()
    for copy in copies:
        copy.wait()


SMEM = pl.BlockSpec(memory_space=pltpu.SMEM)
VMEM = pl.BlockSpec(memory_space=pltpu.VMEM)
HBM = pl.BlockSpec(memory_space=pltpu.HBM)
ANY = pl.BlockSpec(memory_space=pl.ANY)
LIMIT = 48 << 20


def struct(*shape):
    return jax.ShapeDtypeStruct(shape, jnp.float32)


def in_hbm(array):
    return pltpu.with_memory_space_constraint(array, pltpu.HBM)


def pack(send_x, send_y, cells, *small):
    return pl.pallas_call(
        pack_kernel,
        out_shape=(
            jax.ShapeDtypeStruct((1, 128), jnp.int32),
            struct(4 * SWEEP_ROWS, 128),
            struct(24, FACE_ROWS, 128),
        )
        + (struct(4, FACE_ROWS, 128),) * 4,
        in_specs=[SMEM, SMEM, HBM] + [HBM] * len(small),
        out_specs=(VMEM,) * 7,
        scratch_shapes=[
            pltpu.VMEM(cells.shape, jnp.float32),
            *[pltpu.SMEM(array.shape, jnp.int32) for array in small],
            pltpu.SemaphoreType.DMA((5,)),
            pltpu.SemaphoreType.DMA((len(small),)),
        ],
        compiler_params=pltpu.CompilerParams(vmem_limit_bytes=LIMIT),
        name="pack",
    )(send_x, send_y, *[in_hbm(array) for array in (cells, *small)])


def update(name, which_block, more, numbers, sweep, table, received, *after):
    return pl.pallas_call(
        functools.partial(update_kernel, which_block, more),
        out_shape=struct(BLOCK_ROWS + (8 if more else 0), 128),
        in_specs=[SMEM] + [VMEM] * 6 + [ANY] * len(after),
        out_specs=VMEM,
        scratch_shapes=[
            pltpu.VMEM((16, FACE_ROWS, 128), jnp.float32),
            pltpu.VMEM((5 * GHOST_ROWS, 128), jnp.float32),
            pltpu.VMEM((SWEEP_ROWS, 128), jnp.float32),
        ],
        compiler_params=pltpu.CompilerParams(vmem_limit_bytes=LIMIT),
        cost_estimate=pl.CostEstimate(flops=2_000_000, bytes_accessed=4_000_000, transcendentals=40_000),
        name=name,
    )(numbers, sweep.reshape(4, SWEEP_ROWS, 128), table, *received, *after)


def place(numbers, from_y, from_x, own):
    return pl.pallas_call(
        place_kernel,
        out_shape=struct(5, 3, B * B * B),
        in_specs=[SMEM] + [VMEM] * 3,
        out_specs=HBM,
        scratch_shapes=[
            pltpu.VMEM((3 * BLOCK_ROWS, 128), jnp.float32),
            pltpu.VMEM((5, 3, B * B * B), jnp.float32),
            pltpu.SemaphoreType.DMA((5,)),
        ],
        compiler_params=pltpu.CompilerParams(vmem_limit_bytes=LIMIT),
        name="place",
    )(numbers, from_y, from_x, own)


def with_pair(values, axis, odd):
    count = lax.axis_size(axis)
    mate = [((i + odd) ^ 1) - odd for i in range(count)]
    return lax.ppermute(values, axis, [(i, j % count) for i, j in enumerate(mate)])


def with_partner(values, axis):
    count = lax.axis_size(axis)
    return lax.ppermute(values, axis, [(i, i ^ (count // 2)) for i in range(count)])


def on_device(cells_in, block_levels, send_x, send_y, layout, face_out, ghost_src):
    numbers, sweep, table, *messages = pack(
        send_x, send_y, cells_in.transpose(1, 0, 2), layout, block_levels, ghost_src, face_out
    )
    received = [
        with_pair(messages[0], "by", 1),
        with_pair(messages[1], "bx", 1),
        with_pair(messages[2], "bx", 0),
        with_pair(messages[3], "by", 0),
    ]
    common = (numbers, sweep, table, received)
    to_y = update("to_y", 1, True, *common)
    from_y = with_partner(to_y, "by")
    to_x = update("to_x", 0, False, *common, to_y)
    from_x = with_partner(to_x, "bx")
    own = update("own", 2, False, *common, to_x)
    return place(numbers, from_y, from_x, own).transpose(1, 0, 2)


def solution(mesh):
    return jax.shard_map(
        on_device,
        mesh=mesh,
        in_specs=(
            P(("bx", "by"), None, None),
            P(("bx", "by")),
            P(("bx", "by"), None),
            P(("bx", "by"), None),
            P(("bx", "by"), None),
            P(("bx", "by"), None, None),
            P(("bx", "by"), None, None),
        ),
        out_specs=P(("bx", "by"), None, None),
        check_vma=False,
    )
```

```python
import functools

import jax
import jax.numpy as jnp
from jax import lax
from jax.experimental import pallas as pl
from jax.experimental.pallas import tpu as pltpu
from jax.sharding import PartitionSpec as P

B = 16
GAMMA = 1.4
STEP = 0.05
HALF = 8
FIELD_ROWS = B * 8
SWEEP_ROWS = 5 * FIELD_ROWS
BLOCK_ROWS = 5 * 2 * B
FACE_ROWS = 24
GHOST_ROWS = 4 * 8


def slot_of(field, direction):
    if field == 1:
        return 1 + direction
    if field == 1 + direction:
        return 1
    return field


def lanes(shape=(8, 128)):
    return lax.broadcasted_iota(jnp.int32, shape, 1)


def rows(shape=(8, 128)):
    return lax.broadcasted_iota(jnp.int32, shape, 0)


def take(values, index, axis):
    return jnp.take_along_axis(values, index, axis=axis, mode="promise_in_bounds")


class Turns:
    def __init__(self):
        lane, row = lanes(), rows()
        group, inner = lane // 16, lane % 16
        self.low = inner < 8
        self.skew = ((group + row) % 8) * 16 + inner
        self.shift = (row - group) % 8
        self.back = ((row - group) % 8) * 16 + inner
        self.skew_half = ((group + row) % 8) * 16 + (inner + 8) % 16
        self.back_half = ((row - group) % 8) * 16 + (inner + 8) % 16
        source_group = (group + row) % 8
        self.skew_z = (inner % 8) * 16 + (inner // 8) * 8 + source_group
        z_low, z_high = inner % 8, inner // 8
        self.back_z = ((row - z_low) % 8) * 16 + z_high * 8 + group

    def turn(self, v):
        return take(take(take(v, self.skew, 1), self.shift, 0), self.back, 1)

    def to_z(self, v0, v1):
        t0 = take(take(v0, self.skew_z, 1), self.shift, 0)
        t1 = take(take(v1, self.skew_z, 1), self.shift, 0)
        first = jnp.where(self.low, take(t0, self.back, 1), take(t1, self.back_half, 1))
        second = jnp.where(self.low, take(t0, self.back_half, 1), take(t1, self.back, 1))
        return first, second

    def from_z(self, first, second):
        t0 = jnp.where(self.low, take(first, self.skew, 1), take(second, self.skew_half, 1))
        t1 = jnp.where(self.low, take(first, self.skew_half, 1), take(second, self.skew, 1))
        return tuple(take(take(t, self.shift, 0), self.back_z, 1) for t in (t0, t1))


def parities():
    return lax.axis_index("bx") % 2, lax.axis_index("by") % 2


def pack_kernel(
    cells_in, layout_in, levels_in, ghost_src_in, face_out_in, *rest
):
    numbers, sweep, table, *messages = rest[:7]
    cells, layout, levels, ghost_src, face_out, cells_sem, small_sem = rest[7:]
    odd_x, odd_y = parities()
    copies = [
        pltpu.make_async_copy(cells_in.at[f], cells.at[f], cells_sem.at[f]) for f in range(5)
    ]
    small = [
        pltpu.make_async_copy(source, target, small_sem.at[i])
        for i, (source, target) in enumerate(
            (
                (face_out_in, face_out),
                (layout_in, layout),
                (levels_in, levels),
                (ghost_src_in, ghost_src),
            )
        )
    ]
    for copy in copies + small:
        copy.start()
    turns = Turns()
    for field in range(5):
        base = field * FIELD_ROWS
        to_y = slot_of(field, 1) * FIELD_ROWS
        to_z = slot_of(field, 2) * FIELD_ROWS
        copies[field].wait()
        for t in range(2 * B):
            row = base + (t // 2) * 8 + t % 2
            sweep[pl.ds(row, 4, stride=SWEEP_ROWS), :] = cells[
                field, :, t * 128 : (t + 1) * 128
            ]
        for first in range(0, 4 * SWEEP_ROWS, SWEEP_ROWS):
            for xh in range(2):
                v = [
                    sweep[pl.ds(first + base + HALF * xh * 8 + h, 8, stride=8), :]
                    for h in range(2)
                ]
                for h in range(2):
                    start = first + to_y + HALF * h * 8 + 2 + xh
                    sweep[pl.ds(start, 8, stride=8), :] = turns.turn(v[h])
                for zh, value in enumerate(turns.to_z(v[0], v[1])):
                    start = first + to_z + HALF * zh * 8 + 4 + xh
                    sweep[pl.ds(start, 8, stride=8), :] = value
    for s in range(4):
        for face in range(6):
            direction, high = face // 2, face % 2
            for layer in range(2):
                i = B - 1 - layer if high else layer
                for h in range(2):
                    row = s * SWEEP_ROWS + i * 8 + direction * 2 + h
                    to = (layer * 2 + h) * 5
                    table[s * 6 + face, to : to + 5, :] = sweep[
                        pl.ds(row, 5, stride=FIELD_ROWS), :
                    ]
                    if direction:
                        for field, slot in ((1, 1 + direction), (1 + direction, 1)):
                            table[s * 6 + face, to + field : to + field + 1, :] = sweep[
                                pl.ds(slot * FIELD_ROWS + row, 1), :
                            ]
    for copy in small:
        copy.wait()
    for m, one_list in enumerate((2 + (1 - odd_y), 1 - odd_x, odd_x, 2 + odd_y)):
        for k in range(4):
            messages[m][k] = table[face_out[0, one_list, k]]
    codes = [layout[0, j] for j in range(3)]
    kept = functools.reduce(jnp.maximum, [jnp.where(c < 4, c, 0) for c in codes])
    listed = {2: kept}
    listed.update({3 + j: codes[j] for j in range(3)})
    listed.update({8 + j: levels[j] for j in range(4)})
    listed.update({12 + s * 6 + f: ghost_src[0, s, f] for s in range(4) for f in range(6)})
    lane = lanes((1, 128))
    row = jnp.zeros((1, 128), jnp.int32)
    for i, number in listed.items():
        row = jnp.where(lane == i, number, row)
    numbers[...] = row


def limited(left, right):
    return jnp.maximum(jnp.minimum(left, right), 0.0) + jnp.minimum(jnp.maximum(left, right), 0.0)


def fluxes_of(q):
    density, normal, second, third, pressure = q
    mass = density * normal
    kinetic = 0.5 * density * (normal * normal + second * second + third * third)
    energy = pressure * (1.0 / (GAMMA - 1.0)) + kinetic
    cons = (density, mass, density * second, density * third, energy)
    flux = (mass, mass * normal + pressure, mass * second, mass * third, normal * (energy + pressure))
    scaled = GAMMA * pressure
    signal = jnp.abs(normal) + scaled * lax.rsqrt(scaled * density)
    return cons, flux, signal


def step_of(level):
    return jnp.where(level == 0, STEP, jnp.where(level == 1, STEP * 2, STEP * 4))


def upper_half():
    return lax.axis_index("by") >= lax.axis_size("by") // 2


def update_kernel(which, half, extra, handed, counts, sends, numbers, sweep, table, *rest):
    received, rest = rest[: sum(counts)], rest[sum(counts) :]
    out, copies = rest[-4 - handed], rest[-3 - handed : -3]
    for source, target in zip(rest, copies):
        target[...] = source[...]

    def body():
        update_body(which, counts, sends, numbers, sweep, table, received, out, *rest[-3:])
        if extra:
            out[BLOCK_ROWS : BLOCK_ROWS + extra, :] = jnp.zeros((extra, 128), jnp.float32)

    if half is None:
        body()
    else:
        pl.when(upper_half() == half)(body)


def update_body(which, counts, sends, numbers, sweep, table, received, out, remote, ghost, change):
    turns = Turns()
    odd_x, odd_y = parities()
    s = numbers[0, 2] if which == 2 else sends[0, 0]
    ratio = step_of(numbers[0, 8 + s])
    first = 0
    for m, count in enumerate(counts):
        for k in range(4):
            remote[m * 4 + k] = sum(array[k] for array in received[first : first + count])
        first += count
    for face in range(6):
        direction, high = face // 2, face % 2
        code = numbers[0, 12 + s * 6 + face]
        far = jnp.maximum(code - 24, 0)
        which = far // 4
        along_x = jnp.where(which == odd_x, 1, 2)
        along_y = jnp.where(which - 2 == odd_y, 0, 3)
        far = jnp.where(which < 2, along_x, along_y) * 4 + far % 4
        near = jnp.minimum(code, 23)
        for layer in range(2):
            i = 2 + layer if high else 1 - layer
            for h in range(2):
                row = i * 8 + direction * 2 + h
                at = (layer * 2 + h) * 5
                moves = [(pl.ds(at, 5), pl.ds(row, 5, stride=GHOST_ROWS))]
                if direction:
                    for field, to in ((1, 1 + direction), (1 + direction, 1)):
                        moves.append((pl.ds(at + field, 1), pl.ds(to * GHOST_ROWS + row, 1)))
                for source, target in moves:
                    ghost[target, :] = jnp.where(
                        code < 24, table[near, source, :], remote[far, source, :]
                    )

    def cells_at(i):
        if 0 <= i < B:
            return [sweep[s, pl.ds(f * FIELD_ROWS + i * 8, 8), :] for f in range(5)]
        k = i + 2 if i < 0 else i - B + 2
        return [ghost[pl.ds(f * GHOST_ROWS + k * 8, 8), :] for f in range(5)]

    here, after = cells_at(-2), cells_at(-1)
    right = [b - a for a, b in zip(here, after)]
    left_face = last_flux = None
    for i in range(-1, B + 1):
        here, after, left = after, cells_at(i + 2 - 1), right
        right = [b - a for a, b in zip(here, after)]
        half = [0.5 * limited(a, b) for a, b in zip(left, right)]
        density, normal, _, _, pressure = here
        carried = ratio * normal
        moved = [carried * a for a in half]
        centre = [
            density - (moved[0] + ratio * density * half[1]),
            normal - (moved[1] + ratio * half[4] / density),
            here[2] - moved[2],
            here[3] - moved[3],
            pressure - (moved[4] + (ratio * GAMMA) * pressure * half[1]),
        ]
        if i >= 0:
            cons, flux, signal = fluxes_of([a - b for a, b in zip(centre, half)])
            old_cons, old_flux, old_signal = left_face
            speed = jnp.maximum(signal, old_signal)
            face_flux = [
                (fa + fb) - speed * (ub - ua)
                for fa, fb, ua, ub in zip(old_flux, flux, old_cons, cons)
            ]
            if i >= 1:
                for f in range(5):
                    change[pl.ds(f * FIELD_ROWS + (i - 1) * 8, 8), :] = face_flux[f] - last_flux[f]
            last_flux = face_flux
        if i < B:
            left_face = fluxes_of([a + b for a, b in zip(centre, half)])

    def in_place(ref, start):
        return ref[pl.ds(start, 8, stride=8), :]

    scale = 0.5 * ratio
    for xh in range(2):
        prims = [
            [sweep[s, pl.ds(f * FIELD_ROWS + HALF * xh * 8 + h, 8, stride=8), :] for h in range(2)]
            for f in range(5)
        ]
        for f in range(5):
            along_y = slot_of(f, 1) * FIELD_ROWS
            along_z = slot_of(f, 2) * FIELD_ROWS
            from_z = turns.from_z(
                *[in_place(change, along_z + HALF * zh * 8 + 4 + xh) for zh in range(2)]
            )
            for h in range(2):
                total = (
                    in_place(change, f * FIELD_ROWS + HALF * xh * 8 + h)
                    + turns.turn(in_place(change, along_y + HALF * h * 8 + 2 + xh))
                    + from_z[h]
                )
                density, u, v, w, pressure = (prims[k][h] for k in range(5))
                if f == 0:
                    initial = density
                elif f < 4:
                    initial = density * prims[f][h]
                else:
                    initial = pressure * (1.0 / (GAMMA - 1.0)) + 0.5 * density * (
                        u * u + v * v + w * w
                    )
                row = f * 2 * B + h * B + HALF * xh
                out[row : row + 8, :] = initial - scale * total


def place_kernel(numbers, from_y0, from_y1, from_x0, from_x1, own, out, slots, staged, sems):
    codes = [numbers[0, 3 + j] for j in range(3)]
    at_x = jnp.where(codes[1] == 4, 1, jnp.where(codes[2] == 4, 2, 0))
    at_y = jnp.where(codes[1] == 5, 1, jnp.where(codes[2] == 5, 2, 0))
    at_own = 3 - at_x - at_y
    empty = codes[0] + codes[1] + codes[2] == 8
    copies = []
    for f in range(5):
        one = pl.ds(f * 2 * B, 2 * B)
        values = (
            (jnp.where(empty, 0.0, own[one, :]), at_own),
            (from_x0[one, :] + from_x1[one, :], at_x),
            (from_y0[one, :] + from_y1[one, :], at_y),
        )
        for v, at in values:
            slots[pl.ds(pl.multiple_of(at * BLOCK_ROWS + f * 2 * B, 2 * B), 2 * B), :] = v
        for t in range(2 * B):
            row = f * 2 * B + (t % 2) * B + t // 2
            staged[f, :, t * 128 : (t + 1) * 128] = slots[pl.ds(row, 3, stride=BLOCK_ROWS), :]
        copies.append(pltpu.make_async_copy(staged.at[f], out.at[f], sems.at[f]))
        copies[-1].start()
    for copy in copies:
        copy.wait()


SMEM = pl.BlockSpec(memory_space=pltpu.SMEM)
VMEM = pl.BlockSpec(memory_space=pltpu.VMEM)
HBM = pl.BlockSpec(memory_space=pltpu.HBM)
ANY = pl.BlockSpec(memory_space=pl.ANY)
LIMIT = 48 << 20


def struct(*shape):
    return jax.ShapeDtypeStruct(shape, jnp.float32)


def in_hbm(array):
    return pltpu.with_memory_space_constraint(array, pltpu.HBM)


def pack(cells, *small):
    return pl.pallas_call(
        pack_kernel,
        out_shape=(
            jax.ShapeDtypeStruct((1, 128), jnp.int32),
            struct(4 * SWEEP_ROWS, 128),
            struct(24, FACE_ROWS, 128),
        )
        + (struct(4, FACE_ROWS, 128),) * 4,
        in_specs=[HBM] * (1 + len(small)),
        out_specs=(VMEM,) * 7,
        scratch_shapes=[
            pltpu.VMEM(cells.shape, jnp.float32),
            *[pltpu.SMEM(array.shape, jnp.int32) for array in small],
            pltpu.SemaphoreType.DMA((5,)),
            pltpu.SemaphoreType.DMA((len(small),)),
        ],
        compiler_params=pltpu.CompilerParams(vmem_limit_bytes=LIMIT),
        name="pack",
    )(*[in_hbm(array) for array in (cells, *small)])


def update(name, which, half, extra, sends, numbers, sweep, table, received, handed=(), after=()):
    counts = tuple(len(arrays) for arrays in received)
    flat = [array for arrays in received for array in arrays]
    message = struct(BLOCK_ROWS + extra, 128)
    return pl.pallas_call(
        functools.partial(update_kernel, which, half, extra, len(handed), counts),
        out_shape=(message, *[struct(*array.shape) for array in handed]) if handed else message,
        in_specs=[SMEM] * 2 + [VMEM] * (2 + len(flat) + len(handed)) + [ANY] * len(after),
        out_specs=(VMEM,) * (1 + len(handed)) if handed else VMEM,
        scratch_shapes=[
            pltpu.VMEM((16, FACE_ROWS, 128), jnp.float32),
            pltpu.VMEM((5 * GHOST_ROWS, 128), jnp.float32),
            pltpu.VMEM((SWEEP_ROWS, 128), jnp.float32),
        ],
        compiler_params=pltpu.CompilerParams(vmem_limit_bytes=LIMIT),
        name=name,
    )(sends, numbers, sweep.reshape(4, SWEEP_ROWS, 128), table, *flat, *handed, *after)


def place(numbers, from_y, from_x, own):
    return pl.pallas_call(
        place_kernel,
        out_shape=struct(5, 3, B * B * B),
        in_specs=[SMEM] + [VMEM] * 5,
        out_specs=HBM,
        scratch_shapes=[
            pltpu.VMEM((3 * BLOCK_ROWS, 128), jnp.float32),
            pltpu.VMEM((5, 3, B * B * B), jnp.float32),
            pltpu.SemaphoreType.DMA((5,)),
        ],
        compiler_params=pltpu.CompilerParams(vmem_limit_bytes=LIMIT),
        name="place",
    )(numbers, *from_y, *from_x, own)


def exchange(values, move, sends):
    count_x, count_y = lax.axis_size("bx"), lax.axis_size("by")
    pairs = []
    for i in range(count_x):
        for j in range(count_y):
            to_i, to_j = move(i, j)
            to_i, to_j = to_i % count_x, to_j % count_y
            if sends(j, to_j):
                pairs.append((i * count_y + j, to_i * count_y + to_j))
    return lax.ppermute(values, ("bx", "by"), pairs)


def on_device(cells_in, block_levels, send_x, send_y, layout, face_out, ghost_src):
    half_x, half_y = lax.axis_size("bx") // 2, lax.axis_size("by") // 2
    pairings = (
        lambda i, j: (i, ((j + 1) ^ 1) - 1),
        lambda i, j: (((i + 1) ^ 1) - 1, j),
        lambda i, j: (i ^ 1, j),
        lambda i, j: (i, j ^ 1),
    )

    def upper(j, to_j):
        return j >= half_y or to_j >= half_y

    def lower(j, to_j):
        return not upper(j, to_j)

    def by_partner(i, j):
        return i, j ^ half_y

    def bx_partner(i, j):
        return i ^ half_x, j

    numbers, sweep, table, *messages = pack(
        cells_in.transpose(1, 0, 2), layout, block_levels, ghost_src, face_out
    )
    common = (numbers, sweep, table)
    early = [exchange(m, pairing, upper) for m, pairing in zip(messages, pairings)]
    y_upper, *messages = update(
        "y_upper", 1, True, 8, send_y, *common, [[r] for r in early], handed=messages
    )
    y_from_upper = exchange(y_upper, by_partner, lambda j, to_j: j >= half_y)
    late = [exchange(m, pairing, lower) for m, pairing in zip(messages, pairings)]
    lower_faces = [[early[0], late[0]], [late[1]], [late[2]], [late[3]]]
    x_lower = update("x_lower", 0, False, 16, send_x, *common, lower_faces, after=(y_upper,))
    x_from_lower = exchange(x_lower, bx_partner, lower)
    y_lower = update("y_lower", 1, False, 8, send_y, *common, lower_faces, after=(x_lower,))
    y_from_lower = exchange(y_lower, by_partner, lambda j, to_j: j < half_y)
    x_upper = update("x_upper", 0, True, 0, send_x, *common, [[r] for r in early], after=(y_lower, y_from_upper))
    x_from_upper = exchange(x_upper, bx_partner, upper)
    own = update("own", 2, None, 0, send_x, *common, [list(p) for p in zip(early, late)], after=(x_upper,))
    from_y, from_x = (y_from_upper, y_from_lower), (x_from_upper, x_from_lower)
    return place(numbers, from_y, from_x, own).transpose(1, 0, 2)


def solution(mesh):
    return jax.shard_map(
        on_device,
        mesh=mesh,
        in_specs=(
            P(("bx", "by"), None, None),
            P(("bx", "by")),
            P(("bx", "by"), None),
            P(("bx", "by"), None),
            P(("bx", "by"), None),
            P(("bx", "by"), None, None),
            P(("bx", "by"), None, None),
        ),
        out_specs=P(("bx", "by"), None, None),
        check_vma=False,
    )
```

```python
import functools

import jax
import jax.numpy as jnp
from jax import lax
from jax.experimental import pallas as pl
from jax.experimental.pallas import tpu as pltpu
from jax.sharding import PartitionSpec as P

B = 16
GAMMA = 1.4
STEP = 0.05
HALF = 8
FIELD_ROWS = B * 8
SWEEP_ROWS = 5 * FIELD_ROWS
BLOCK_ROWS = 5 * 2 * B
FACE_ROWS = 24
GHOST_ROWS = 4 * 8


def slot_of(field, direction):
    if field == 1:
        return 1 + direction
    if field == 1 + direction:
        return 1
    return field


def lanes(shape=(8, 128)):
    return lax.broadcasted_iota(jnp.int32, shape, 1)


def rows(shape=(8, 128)):
    return lax.broadcasted_iota(jnp.int32, shape, 0)


def take(values, index, axis):
    return jnp.take_along_axis(values, index, axis=axis, mode="promise_in_bounds")


class Turns:
    def __init__(self):
        lane, row = lanes(), rows()
        group, inner = lane // 16, lane % 16
        self.low = inner < 8
        self.skew = ((group + row) % 8) * 16 + inner
        self.shift = (row - group) % 8
        self.back = ((row - group) % 8) * 16 + inner
        self.skew_half = ((group + row) % 8) * 16 + (inner + 8) % 16
        self.back_half = ((row - group) % 8) * 16 + (inner + 8) % 16
        source_group = (group + row) % 8
        self.skew_z = (inner % 8) * 16 + (inner // 8) * 8 + source_group
        z_low, z_high = inner % 8, inner // 8
        self.back_z = ((row - z_low) % 8) * 16 + z_high * 8 + group

    def turn(self, v):
        return take(take(take(v, self.skew, 1), self.shift, 0), self.back, 1)

    def to_z(self, v0, v1):
        t0 = take(take(v0, self.skew_z, 1), self.shift, 0)
        t1 = take(take(v1, self.skew_z, 1), self.shift, 0)
        first = jnp.where(self.low, take(t0, self.back, 1), take(t1, self.back_half, 1))
        second = jnp.where(self.low, take(t0, self.back_half, 1), take(t1, self.back, 1))
        return first, second

    def from_z(self, first, second):
        t0 = jnp.where(self.low, take(first, self.skew, 1), take(second, self.skew_half, 1))
        t1 = jnp.where(self.low, take(first, self.skew_half, 1), take(second, self.skew, 1))
        return tuple(take(take(t, self.shift, 0), self.back_z, 1) for t in (t0, t1))


def parities():
    return lax.axis_index("bx") % 2, lax.axis_index("by") % 2


def pack_kernel(
    cells_in, layout_in, levels_in, ghost_src_in, face_out_in, *rest
):
    numbers, sweep, table, *messages = rest[:7]
    cells, layout, levels, ghost_src, face_out, cells_sem, small_sem = rest[7:]
    odd_x, odd_y = parities()
    copies = [
        pltpu.make_async_copy(cells_in.at[f], cells.at[f], cells_sem.at[f]) for f in range(5)
    ]
    small = [
        pltpu.make_async_copy(source, target, small_sem.at[i])
        for i, (source, target) in enumerate(
            (
                (face_out_in, face_out),
                (layout_in, layout),
                (levels_in, levels),
                (ghost_src_in, ghost_src),
            )
        )
    ]
    for copy in copies + small:
        copy.start()
    turns = Turns()
    for field in range(5):
        base = field * FIELD_ROWS
        to_y = slot_of(field, 1) * FIELD_ROWS
        to_z = slot_of(field, 2) * FIELD_ROWS
        copies[field].wait()
        for t in range(2 * B):
            row = base + (t // 2) * 8 + t % 2
            sweep[pl.ds(row, 4, stride=SWEEP_ROWS), :] = cells[
                field, :, t * 128 : (t + 1) * 128
            ]
        for first in range(0, 4 * SWEEP_ROWS, SWEEP_ROWS):
            for xh in range(2):
                v = [
                    sweep[pl.ds(first + base + HALF * xh * 8 + h, 8, stride=8), :]
                    for h in range(2)
                ]
                for h in range(2):
                    start = first + to_y + HALF * h * 8 + 2 + xh
                    sweep[pl.ds(start, 8, stride=8), :] = turns.turn(v[h])
                for zh, value in enumerate(turns.to_z(v[0], v[1])):
                    start = first + to_z + HALF * zh * 8 + 4 + xh
                    sweep[pl.ds(start, 8, stride=8), :] = value
    for s in range(4):
        for face in range(6):
            direction, high = face // 2, face % 2
            for layer in range(2):
                i = B - 1 - layer if high else layer
                for h in range(2):
                    row = s * SWEEP_ROWS + i * 8 + direction * 2 + h
                    to = (layer * 2 + h) * 5
                    table[s * 6 + face, to : to + 5, :] = sweep[
                        pl.ds(row, 5, stride=FIELD_ROWS), :
                    ]
                    if direction:
                        for field, slot in ((1, 1 + direction), (1 + direction, 1)):
                            table[s * 6 + face, to + field : to + field + 1, :] = sweep[
                                pl.ds(slot * FIELD_ROWS + row, 1), :
                            ]
    for copy in small:
        copy.wait()
    for m, one_list in enumerate((2 + (1 - odd_y), 1 - odd_x, odd_x, 2 + odd_y)):
        for k in range(4):
            messages[m][k] = table[face_out[0, one_list, k]]
    codes = [layout[0, j] for j in range(3)]
    kept = functools.reduce(jnp.maximum, [jnp.where(c < 4, c, 0) for c in codes])
    listed = {2: kept}
    listed.update({3 + j: codes[j] for j in range(3)})
    listed.update({8 + j: levels[j] for j in range(4)})
    listed.update({12 + s * 6 + f: ghost_src[0, s, f] for s in range(4) for f in range(6)})
    lane = lanes((1, 128))
    row = jnp.zeros((1, 128), jnp.int32)
    for i, number in listed.items():
        row = jnp.where(lane == i, number, row)
    numbers[...] = row


def limited(left, right):
    return jnp.maximum(jnp.minimum(left, right), 0.0) + jnp.minimum(jnp.maximum(left, right), 0.0)


def fluxes_of(q):
    density, normal, second, third, pressure = q
    mass = density * normal
    kinetic = 0.5 * density * (normal * normal + second * second + third * third)
    energy = pressure * (1.0 / (GAMMA - 1.0)) + kinetic
    cons = (density, mass, density * second, density * third, energy)
    flux = (mass, mass * normal + pressure, mass * second, mass * third, normal * (energy + pressure))
    scaled = GAMMA * pressure
    signal = jnp.abs(normal) + scaled * lax.rsqrt(scaled * density)
    return cons, flux, signal


def step_of(level):
    return jnp.where(level == 0, STEP, jnp.where(level == 1, STEP * 2, STEP * 4))


def upper_half():
    return lax.axis_index("by") >= lax.axis_size("by") // 2


def update_kernel(half, blocks, counts, handed, send_x, send_y, numbers, sweep, table, *rest):
    received, rest = rest[: sum(counts)], rest[sum(counts) :]
    scratch = rest[-3:]
    outs = rest[-3 - len(blocks) - handed : -3 - handed]
    for source, target in zip(rest[:handed], rest[-3 - handed : -3]):
        target[...] = source[...]

    @pl.when(upper_half() == half)
    def _():
        remote = scratch[0]
        first = 0
        for m, count in enumerate(counts):
            for k in range(4):
                remote[m * 4 + k] = sum(array[k] for array in received[first : first + count])
            first += count
        for (which, extra), out in zip(blocks, outs):
            s = (send_x[0, 0], send_y[0, 0], numbers[0, 2])[which]
            update_body(s, numbers, sweep, table, out, *scratch)
            if extra:
                out[BLOCK_ROWS : BLOCK_ROWS + extra, :] = jnp.zeros((extra, 128), jnp.float32)


def update_body(s, numbers, sweep, table, out, remote, ghost, change):
    turns = Turns()
    odd_x, odd_y = parities()
    ratio = step_of(numbers[0, 8 + s])
    for face in range(6):
        direction, high = face // 2, face % 2
        code = numbers[0, 12 + s * 6 + face]
        far = jnp.maximum(code - 24, 0)
        which = far // 4
        along_x = jnp.where(which == odd_x, 1, 2)
        along_y = jnp.where(which - 2 == odd_y, 0, 3)
        far = jnp.where(which < 2, along_x, along_y) * 4 + far % 4
        near = jnp.minimum(code, 23)
        for layer in range(2):
            i = 2 + layer if high else 1 - layer
            for h in range(2):
                row = i * 8 + direction * 2 + h
                at = (layer * 2 + h) * 5
                moves = [(pl.ds(at, 5), pl.ds(row, 5, stride=GHOST_ROWS))]
                if direction:
                    for field, to in ((1, 1 + direction), (1 + direction, 1)):
                        moves.append((pl.ds(at + field, 1), pl.ds(to * GHOST_ROWS + row, 1)))
                for source, target in moves:
                    ghost[target, :] = jnp.where(
                        code < 24, table[near, source, :], remote[far, source, :]
                    )

    def cells_at(i):
        if 0 <= i < B:
            return [sweep[s, pl.ds(f * FIELD_ROWS + i * 8, 8), :] for f in range(5)]
        k = i + 2 if i < 0 else i - B + 2
        return [ghost[pl.ds(f * GHOST_ROWS + k * 8, 8), :] for f in range(5)]

    here, after = cells_at(-2), cells_at(-1)
    right = [b - a for a, b in zip(here, after)]
    left_face = last_flux = None
    for i in range(-1, B + 1):
        here, after, left = after, cells_at(i + 2 - 1), right
        right = [b - a for a, b in zip(here, after)]
        half = [0.5 * limited(a, b) for a, b in zip(left, right)]
        density, normal, _, _, pressure = here
        carried = ratio * normal
        moved = [carried * a for a in half]
        centre = [
            density - (moved[0] + ratio * density * half[1]),
            normal - (moved[1] + ratio * half[4] / density),
            here[2] - moved[2],
            here[3] - moved[3],
            pressure - (moved[4] + (ratio * GAMMA) * pressure * half[1]),
        ]
        if i >= 0:
            cons, flux, signal = fluxes_of([a - b for a, b in zip(centre, half)])
            old_cons, old_flux, old_signal = left_face
            speed = jnp.maximum(signal, old_signal)
            face_flux = [
                (fa + fb) - speed * (ub - ua)
                for fa, fb, ua, ub in zip(old_flux, flux, old_cons, cons)
            ]
            if i >= 1:
                for f in range(5):
                    change[pl.ds(f * FIELD_ROWS + (i - 1) * 8, 8), :] = face_flux[f] - last_flux[f]
            last_flux = face_flux
        if i < B:
            left_face = fluxes_of([a + b for a, b in zip(centre, half)])

    def in_place(ref, start):
        return ref[pl.ds(start, 8, stride=8), :]

    scale = 0.5 * ratio
    for xh in range(2):
        prims = [
            [sweep[s, pl.ds(f * FIELD_ROWS + HALF * xh * 8 + h, 8, stride=8), :] for h in range(2)]
            for f in range(5)
        ]
        for f in range(5):
            along_y = slot_of(f, 1) * FIELD_ROWS
            along_z = slot_of(f, 2) * FIELD_ROWS
            from_z = turns.from_z(
                *[in_place(change, along_z + HALF * zh * 8 + 4 + xh) for zh in range(2)]
            )
            for h in range(2):
                total = (
                    in_place(change, f * FIELD_ROWS + HALF * xh * 8 + h)
                    + turns.turn(in_place(change, along_y + HALF * h * 8 + 2 + xh))
                    + from_z[h]
                )
                density, u, v, w, pressure = (prims[k][h] for k in range(5))
                if f == 0:
                    initial = density
                elif f < 4:
                    initial = density * prims[f][h]
                else:
                    initial = pressure * (1.0 / (GAMMA - 1.0)) + 0.5 * density * (
                        u * u + v * v + w * w
                    )
                row = f * 2 * B + h * B + HALF * xh
                out[row : row + 8, :] = initial - scale * total


def place_kernel(numbers, from_y0, from_y1, from_x0, from_x1, own0, own1, out, slots, staged, sems):
    codes = [numbers[0, 3 + j] for j in range(3)]
    at_x = jnp.where(codes[1] == 4, 1, jnp.where(codes[2] == 4, 2, 0))
    at_y = jnp.where(codes[1] == 5, 1, jnp.where(codes[2] == 5, 2, 0))
    at_own = 3 - at_x - at_y
    upper = upper_half()
    empty = codes[0] + codes[1] + codes[2] == 8
    copies = []
    for f in range(5):
        one = pl.ds(f * 2 * B, 2 * B)
        values = (
            (jnp.where(empty, 0.0, jnp.where(upper, own0[one, :], own1[one, :])), at_own),
            (from_x0[one, :] + from_x1[one, :], at_x),
            (from_y0[one, :] + from_y1[one, :], at_y),
        )
        for v, at in values:
            slots[pl.ds(pl.multiple_of(at * BLOCK_ROWS + f * 2 * B, 2 * B), 2 * B), :] = v
        for t in range(2 * B):
            row = f * 2 * B + (t % 2) * B + t // 2
            staged[f, :, t * 128 : (t + 1) * 128] = slots[pl.ds(row, 3, stride=BLOCK_ROWS), :]
        copies.append(pltpu.make_async_copy(staged.at[f], out.at[f], sems.at[f]))
        copies[-1].start()
    for copy in copies:
        copy.wait()


SMEM = pl.BlockSpec(memory_space=pltpu.SMEM)
VMEM = pl.BlockSpec(memory_space=pltpu.VMEM)
HBM = pl.BlockSpec(memory_space=pltpu.HBM)
ANY = pl.BlockSpec(memory_space=pl.ANY)
LIMIT = 48 << 20


def struct(*shape):
    return jax.ShapeDtypeStruct(shape, jnp.float32)


def in_hbm(array):
    return pltpu.with_memory_space_constraint(array, pltpu.HBM)


def pack(cells, *small):
    return pl.pallas_call(
        pack_kernel,
        out_shape=(
            jax.ShapeDtypeStruct((1, 128), jnp.int32),
            struct(4 * SWEEP_ROWS, 128),
            struct(24, FACE_ROWS, 128),
        )
        + (struct(4, FACE_ROWS, 128),) * 4,
        in_specs=[HBM] * (1 + len(small)),
        out_specs=(VMEM,) * 7,
        scratch_shapes=[
            pltpu.VMEM(cells.shape, jnp.float32),
            *[pltpu.SMEM(array.shape, jnp.int32) for array in small],
            pltpu.SemaphoreType.DMA((5,)),
            pltpu.SemaphoreType.DMA((len(small),)),
        ],
        compiler_params=pltpu.CompilerParams(vmem_limit_bytes=LIMIT),
        name="pack",
    )(*[in_hbm(array) for array in (cells, *small)])


def update(name, half, blocks, send_x, send_y, numbers, sweep, table, received, handed=(), after=()):
    counts = tuple(len(arrays) for arrays in received)
    flat = [array for arrays in received for array in arrays]
    return pl.pallas_call(
        functools.partial(update_kernel, half, blocks, counts, len(handed)),
        out_shape=(
            *[struct(BLOCK_ROWS + extra, 128) for _, extra in blocks],
            *[struct(*array.shape) for array in handed],
        ),
        in_specs=[SMEM] * 3 + [VMEM] * (2 + len(flat) + len(handed)) + [ANY] * len(after),
        out_specs=(VMEM,) * (len(blocks) + len(handed)),
        scratch_shapes=[
            pltpu.VMEM((16, FACE_ROWS, 128), jnp.float32),
            pltpu.VMEM((5 * GHOST_ROWS, 128), jnp.float32),
            pltpu.VMEM((SWEEP_ROWS, 128), jnp.float32),
        ],
        compiler_params=pltpu.CompilerParams(vmem_limit_bytes=LIMIT),
        name=name,
    )(send_x, send_y, numbers, sweep.reshape(4, SWEEP_ROWS, 128), table, *flat, *handed, *after)


def place(numbers, from_y, from_x, own):
    return pl.pallas_call(
        place_kernel,
        out_shape=struct(5, 3, B * B * B),
        in_specs=[SMEM] + [VMEM] * 6,
        out_specs=HBM,
        scratch_shapes=[
            pltpu.VMEM((3 * BLOCK_ROWS, 128), jnp.float32),
            pltpu.VMEM((5, 3, B * B * B), jnp.float32),
            pltpu.SemaphoreType.DMA((5,)),
        ],
        compiler_params=pltpu.CompilerParams(vmem_limit_bytes=LIMIT),
        name="place",
    )(numbers, *from_y, *from_x, *own)


def exchange(values, move, sends):
    count_x, count_y = lax.axis_size("bx"), lax.axis_size("by")
    pairs = []
    for i in range(count_x):
        for j in range(count_y):
            to_i, to_j = move(i, j)
            to_i, to_j = to_i % count_x, to_j % count_y
            if sends(j, to_j):
                pairs.append((i * count_y + j, to_i * count_y + to_j))
    return lax.ppermute(values, ("bx", "by"), pairs)


def on_device(cells_in, block_levels, send_x, send_y, layout, face_out, ghost_src):
    half_x, half_y = lax.axis_size("bx") // 2, lax.axis_size("by") // 2
    pairings = (
        lambda i, j: (i, ((j + 1) ^ 1) - 1),
        lambda i, j: (((i + 1) ^ 1) - 1, j),
        lambda i, j: (i ^ 1, j),
        lambda i, j: (i, j ^ 1),
    )

    def upper(j, to_j):
        return j >= half_y or to_j >= half_y

    def lower(j, to_j):
        return not upper(j, to_j)

    def by_partner(i, j):
        return i, j ^ half_y

    def bx_partner(i, j):
        return i ^ half_x, j

    numbers, sweep, table, *messages = pack(
        cells_in.transpose(1, 0, 2), layout, block_levels, ghost_src, face_out
    )
    common = (send_x, send_y, numbers, sweep, table)
    early = [exchange(m, pairing, upper) for m, pairing in zip(messages, pairings)]
    upper_faces = [[r] for r in early]
    y_upper, *messages = update("upper", True, ((1, 8),), *common, upper_faces, handed=messages)
    y_from_upper = exchange(y_upper, by_partner, lambda j, to_j: j >= half_y)
    late = [exchange(m, pairing, lower) for m, pairing in zip(messages, pairings)]
    lower_faces = [[early[0], late[0]], [late[1]], [late[2]], [late[3]]]
    x_lower, y_lower, own_lower = update(
        "lower", False, ((0, 16), (1, 8), (2, 0)), *common, lower_faces, after=(y_upper,)
    )
    x_from_lower = exchange(x_lower, bx_partner, lower)
    y_from_lower = exchange(y_lower, by_partner, lambda j, to_j: j < half_y)
    x_upper, own_upper = update(
        "rest", True, ((0, 0), (2, 0)), *common, upper_faces, after=(y_lower, y_from_upper)
    )
    x_from_upper = exchange(x_upper, bx_partner, upper)
    from_y, from_x = (y_from_upper, y_from_lower), (x_from_upper, x_from_lower)
    return place(numbers, from_y, from_x, (own_upper, own_lower)).transpose(1, 0, 2)


def solution(mesh):
    return jax.shard_map(
        on_device,
        mesh=mesh,
        in_specs=(
            P(("bx", "by"), None, None),
            P(("bx", "by")),
            P(("bx", "by"), None),
            P(("bx", "by"), None),
            P(("bx", "by"), None),
            P(("bx", "by"), None, None),
            P(("bx", "by"), None, None),
        ),
        out_specs=P(("bx", "by"), None, None),
        check_vma=False,
    )
```

```python
import functools

import jax
import jax.numpy as jnp
from jax import lax
from jax.experimental import pallas as pl
from jax.experimental.pallas import tpu as pltpu
from jax.sharding import PartitionSpec as P

B = 16
GAMMA = 1.4
STEP = 0.05
HALF = 8
FIELD_ROWS = B * 8
SWEEP_ROWS = 5 * FIELD_ROWS
BLOCK_ROWS = 5 * 2 * B
FACE_ROWS = 24
GHOST_ROWS = 4 * 8


def slot_of(field, direction):
    if field == 1:
        return 1 + direction
    if field == 1 + direction:
        return 1
    return field


def lanes(shape=(8, 128)):
    return lax.broadcasted_iota(jnp.int32, shape, 1)


def rows(shape=(8, 128)):
    return lax.broadcasted_iota(jnp.int32, shape, 0)


def take(values, index, axis):
    return jnp.take_along_axis(values, index, axis=axis, mode="promise_in_bounds")


class Turns:
    def __init__(self):
        lane, row = lanes(), rows()
        group, inner = lane // 16, lane % 16
        self.low = inner < 8
        self.skew = ((group + row) % 8) * 16 + inner
        self.shift = (row - group) % 8
        self.back = ((row - group) % 8) * 16 + inner
        self.skew_half = ((group + row) % 8) * 16 + (inner + 8) % 16
        self.back_half = ((row - group) % 8) * 16 + (inner + 8) % 16
        source_group = (group + row) % 8
        self.skew_z = (inner % 8) * 16 + (inner // 8) * 8 + source_group
        z_low, z_high = inner % 8, inner // 8
        self.back_z = ((row - z_low) % 8) * 16 + z_high * 8 + group

    def turn(self, v):
        return take(take(take(v, self.skew, 1), self.shift, 0), self.back, 1)

    def to_z(self, v0, v1):
        t0 = take(take(v0, self.skew_z, 1), self.shift, 0)
        t1 = take(take(v1, self.skew_z, 1), self.shift, 0)
        first = jnp.where(self.low, take(t0, self.back, 1), take(t1, self.back_half, 1))
        second = jnp.where(self.low, take(t0, self.back_half, 1), take(t1, self.back, 1))
        return first, second

    def from_z(self, first, second):
        t0 = jnp.where(self.low, take(first, self.skew, 1), take(second, self.skew_half, 1))
        t1 = jnp.where(self.low, take(first, self.skew_half, 1), take(second, self.skew, 1))
        return tuple(take(take(t, self.shift, 0), self.back_z, 1) for t in (t0, t1))


def parities():
    return lax.axis_index("bx") % 2, lax.axis_index("by") % 2


def pack_kernel(
    cells_in, layout_in, levels_in, ghost_src_in, face_out_in, *rest
):
    numbers, sweep, table, *messages = rest[:7]
    cells, layout, levels, ghost_src, face_out, cells_sem, small_sem = rest[7:]
    odd_x, odd_y = parities()
    copies = [
        pltpu.make_async_copy(cells_in.at[f], cells.at[f], cells_sem.at[f]) for f in range(5)
    ]
    small = [
        pltpu.make_async_copy(source, target, small_sem.at[i])
        for i, (source, target) in enumerate(
            (
                (face_out_in, face_out),
                (layout_in, layout),
                (levels_in, levels),
                (ghost_src_in, ghost_src),
            )
        )
    ]
    for copy in copies + small:
        copy.start()
    turns = Turns()
    for field in range(5):
        base = field * FIELD_ROWS
        to_y = slot_of(field, 1) * FIELD_ROWS
        to_z = slot_of(field, 2) * FIELD_ROWS
        copies[field].wait()
        for t in range(2 * B):
            row = base + (t // 2) * 8 + t % 2
            sweep[pl.ds(row, 4, stride=SWEEP_ROWS), :] = cells[
                field, :, t * 128 : (t + 1) * 128
            ]
        for first in range(0, 4 * SWEEP_ROWS, SWEEP_ROWS):
            for xh in range(2):
                v = [
                    sweep[pl.ds(first + base + HALF * xh * 8 + h, 8, stride=8), :]
                    for h in range(2)
                ]
                for h in range(2):
                    start = first + to_y + HALF * h * 8 + 2 + xh
                    sweep[pl.ds(start, 8, stride=8), :] = turns.turn(v[h])
                for zh, value in enumerate(turns.to_z(v[0], v[1])):
                    start = first + to_z + HALF * zh * 8 + 4 + xh
                    sweep[pl.ds(start, 8, stride=8), :] = value
    for s in range(4):
        for face in range(6):
            direction, high = face // 2, face % 2
            for layer in range(2):
                i = B - 1 - layer if high else layer
                for h in range(2):
                    row = s * SWEEP_ROWS + i * 8 + direction * 2 + h
                    to = (layer * 2 + h) * 5
                    table[s * 6 + face, to : to + 5, :] = sweep[
                        pl.ds(row, 5, stride=FIELD_ROWS), :
                    ]
                    if direction:
                        for field, slot in ((1, 1 + direction), (1 + direction, 1)):
                            table[s * 6 + face, to + field : to + field + 1, :] = sweep[
                                pl.ds(slot * FIELD_ROWS + row, 1), :
                            ]
    for copy in small:
        copy.wait()
    for m, one_list in enumerate((2 + (1 - odd_y), 1 - odd_x, odd_x, 2 + odd_y)):
        for k in range(4):
            messages[m][k] = table[face_out[0, one_list, k]]
    codes = [layout[0, j] for j in range(3)]
    kept = functools.reduce(jnp.maximum, [jnp.where(c < 4, c, 0) for c in codes])
    listed = {2: kept}
    listed.update({3 + j: codes[j] for j in range(3)})
    listed.update({8 + j: levels[j] for j in range(4)})
    listed.update({12 + s * 6 + f: ghost_src[0, s, f] for s in range(4) for f in range(6)})
    lane = lanes((1, 128))
    row = jnp.zeros((1, 128), jnp.int32)
    for i, number in listed.items():
        row = jnp.where(lane == i, number, row)
    numbers[...] = row


def limited(left, right):
    return jnp.maximum(jnp.minimum(left, right), 0.0) + jnp.minimum(jnp.maximum(left, right), 0.0)


def fluxes_of(q):
    density, normal, second, third, pressure = q
    mass = density * normal
    kinetic = 0.5 * density * (normal * normal + second * second + third * third)
    energy = pressure * (1.0 / (GAMMA - 1.0)) + kinetic
    cons = (density, mass, density * second, density * third, energy)
    flux = (mass, mass * normal + pressure, mass * second, mass * third, normal * (energy + pressure))
    scaled = GAMMA * pressure
    signal = jnp.abs(normal) + scaled * lax.rsqrt(scaled * density)
    return cons, flux, signal


def step_of(level):
    return jnp.where(level == 0, STEP, jnp.where(level == 1, STEP * 2, STEP * 4))


def upper_half():
    return lax.axis_index("by") >= lax.axis_size("by") // 2


def update_kernel(half, blocks, counts, handed, send_x, send_y, numbers, sweep, table, *rest):
    received, rest = rest[: sum(counts)], rest[sum(counts) :]
    scratch = rest[-3:]
    outs = rest[-3 - len(blocks) - handed : -3 - handed]
    for source, target in zip(rest[:handed], rest[-3 - handed : -3]):
        target[...] = source[...]

    def body():
        remote = scratch[0]
        first = 0
        for m, count in enumerate(counts):
            for k in range(4):
                remote[m * 4 + k] = sum(array[k] for array in received[first : first + count])
            first += count
        for (which, extra), out in zip(blocks, outs):
            s = (send_x[0, 0], send_y[0, 0], numbers[0, 2])[which]
            update_body(s, numbers, sweep, table, out, *scratch)
            if extra:
                out[BLOCK_ROWS : BLOCK_ROWS + extra, :] = jnp.zeros((extra, 128), jnp.float32)

    if half is None:
        body()
    else:
        pl.when(upper_half() == half)(body)


def update_body(s, numbers, sweep, table, out, remote, ghost, change):
    turns = Turns()
    odd_x, odd_y = parities()
    ratio = step_of(numbers[0, 8 + s])
    for face in range(6):
        direction, high = face // 2, face % 2
        code = numbers[0, 12 + s * 6 + face]
        far = jnp.maximum(code - 24, 0)
        which = far // 4
        along_x = jnp.where(which == odd_x, 1, 2)
        along_y = jnp.where(which - 2 == odd_y, 0, 3)
        far = jnp.where(which < 2, along_x, along_y) * 4 + far % 4
        near = jnp.minimum(code, 23)
        for layer in range(2):
            i = 2 + layer if high else 1 - layer
            for h in range(2):
                row = i * 8 + direction * 2 + h
                at = (layer * 2 + h) * 5
                moves = [(pl.ds(at, 5), pl.ds(row, 5, stride=GHOST_ROWS))]
                if direction:
                    for field, to in ((1, 1 + direction), (1 + direction, 1)):
                        moves.append((pl.ds(at + field, 1), pl.ds(to * GHOST_ROWS + row, 1)))
                for source, target in moves:
                    ghost[target, :] = jnp.where(
                        code < 24, table[near, source, :], remote[far, source, :]
                    )

    def cells_at(i):
        if 0 <= i < B:
            return [sweep[s, pl.ds(f * FIELD_ROWS + i * 8, 8), :] for f in range(5)]
        k = i + 2 if i < 0 else i - B + 2
        return [ghost[pl.ds(f * GHOST_ROWS + k * 8, 8), :] for f in range(5)]

    here, after = cells_at(-2), cells_at(-1)
    right = [b - a for a, b in zip(here, after)]
    left_face = last_flux = None
    for i in range(-1, B + 1):
        here, after, left = after, cells_at(i + 2 - 1), right
        right = [b - a for a, b in zip(here, after)]
        half = [0.5 * limited(a, b) for a, b in zip(left, right)]
        density, normal, _, _, pressure = here
        carried = ratio * normal
        moved = [carried * a for a in half]
        centre = [
            density - (moved[0] + ratio * density * half[1]),
            normal - (moved[1] + ratio * half[4] / density),
            here[2] - moved[2],
            here[3] - moved[3],
            pressure - (moved[4] + (ratio * GAMMA) * pressure * half[1]),
        ]
        if i >= 0:
            cons, flux, signal = fluxes_of([a - b for a, b in zip(centre, half)])
            old_cons, old_flux, old_signal = left_face
            speed = jnp.maximum(signal, old_signal)
            face_flux = [
                (fa + fb) - speed * (ub - ua)
                for fa, fb, ua, ub in zip(old_flux, flux, old_cons, cons)
            ]
            if i >= 1:
                for f in range(5):
                    change[pl.ds(f * FIELD_ROWS + (i - 1) * 8, 8), :] = face_flux[f] - last_flux[f]
            last_flux = face_flux
        if i < B:
            left_face = fluxes_of([a + b for a, b in zip(centre, half)])

    def in_place(ref, start):
        return ref[pl.ds(start, 8, stride=8), :]

    scale = 0.5 * ratio
    for xh in range(2):
        prims = [
            [sweep[s, pl.ds(f * FIELD_ROWS + HALF * xh * 8 + h, 8, stride=8), :] for h in range(2)]
            for f in range(5)
        ]
        for f in range(5):
            along_y = slot_of(f, 1) * FIELD_ROWS
            along_z = slot_of(f, 2) * FIELD_ROWS
            from_z = turns.from_z(
                *[in_place(change, along_z + HALF * zh * 8 + 4 + xh) for zh in range(2)]
            )
            for h in range(2):
                total = (
                    in_place(change, f * FIELD_ROWS + HALF * xh * 8 + h)
                    + turns.turn(in_place(change, along_y + HALF * h * 8 + 2 + xh))
                    + from_z[h]
                )
                density, u, v, w, pressure = (prims[k][h] for k in range(5))
                if f == 0:
                    initial = density
                elif f < 4:
                    initial = density * prims[f][h]
                else:
                    initial = pressure * (1.0 / (GAMMA - 1.0)) + 0.5 * density * (
                        u * u + v * v + w * w
                    )
                row = f * 2 * B + h * B + HALF * xh
                out[row : row + 8, :] = initial - scale * total


def place_kernel(numbers, from_y0, from_y1, from_x0, from_x1, own, out, slots, staged, sems):
    codes = [numbers[0, 3 + j] for j in range(3)]
    at_x = jnp.where(codes[1] == 4, 1, jnp.where(codes[2] == 4, 2, 0))
    at_y = jnp.where(codes[1] == 5, 1, jnp.where(codes[2] == 5, 2, 0))
    at_own = 3 - at_x - at_y
    empty = codes[0] + codes[1] + codes[2] == 8
    copies = []
    for f in range(5):
        one = pl.ds(f * 2 * B, 2 * B)
        values = (
            (jnp.where(empty, 0.0, own[one, :]), at_own),
            (from_x0[one, :] + from_x1[one, :], at_x),
            (from_y0[one, :] + from_y1[one, :], at_y),
        )
        for v, at in values:
            slots[pl.ds(pl.multiple_of(at * BLOCK_ROWS + f * 2 * B, 2 * B), 2 * B), :] = v
        for t in range(2 * B):
            row = f * 2 * B + (t % 2) * B + t // 2
            staged[f, :, t * 128 : (t + 1) * 128] = slots[pl.ds(row, 3, stride=BLOCK_ROWS), :]
        copies.append(pltpu.make_async_copy(staged.at[f], out.at[f], sems.at[f]))
        copies[-1].start()
    for copy in copies:
        copy.wait()


SMEM = pl.BlockSpec(memory_space=pltpu.SMEM)
VMEM = pl.BlockSpec(memory_space=pltpu.VMEM)
HBM = pl.BlockSpec(memory_space=pltpu.HBM)
ANY = pl.BlockSpec(memory_space=pl.ANY)
LIMIT = 48 << 20


def struct(*shape):
    return jax.ShapeDtypeStruct(shape, jnp.float32)


def in_hbm(array):
    return pltpu.with_memory_space_constraint(array, pltpu.HBM)


def pack(cells, *small):
    return pl.pallas_call(
        pack_kernel,
        out_shape=(
            jax.ShapeDtypeStruct((1, 128), jnp.int32),
            struct(4 * SWEEP_ROWS, 128),
            struct(24, FACE_ROWS, 128),
        )
        + (struct(4, FACE_ROWS, 128),) * 4,
        in_specs=[HBM] * (1 + len(small)),
        out_specs=(VMEM,) * 7,
        scratch_shapes=[
            pltpu.VMEM(cells.shape, jnp.float32),
            *[pltpu.SMEM(array.shape, jnp.int32) for array in small],
            pltpu.SemaphoreType.DMA((5,)),
            pltpu.SemaphoreType.DMA((len(small),)),
        ],
        compiler_params=pltpu.CompilerParams(vmem_limit_bytes=LIMIT),
        name="pack",
    )(*[in_hbm(array) for array in (cells, *small)])


def update(name, half, blocks, send_x, send_y, numbers, sweep, table, received, handed=(), after=()):
    counts = tuple(len(arrays) for arrays in received)
    flat = [array for arrays in received for array in arrays]
    return pl.pallas_call(
        functools.partial(update_kernel, half, blocks, counts, len(handed)),
        out_shape=(
            *[struct(BLOCK_ROWS + extra, 128) for _, extra in blocks],
            *[struct(*array.shape) for array in handed],
        ),
        in_specs=[SMEM] * 3 + [VMEM] * (2 + len(flat) + len(handed)) + [ANY] * len(after),
        out_specs=(VMEM,) * (len(blocks) + len(handed)),
        scratch_shapes=[
            pltpu.VMEM((16, FACE_ROWS, 128), jnp.float32),
            pltpu.VMEM((5 * GHOST_ROWS, 128), jnp.float32),
            pltpu.VMEM((SWEEP_ROWS, 128), jnp.float32),
        ],
        compiler_params=pltpu.CompilerParams(vmem_limit_bytes=LIMIT),
        name=name,
    )(send_x, send_y, numbers, sweep.reshape(4, SWEEP_ROWS, 128), table, *flat, *handed, *after)


def place(numbers, from_y, from_x, own):
    return pl.pallas_call(
        place_kernel,
        out_shape=struct(5, 3, B * B * B),
        in_specs=[SMEM] + [VMEM] * 5,
        out_specs=HBM,
        scratch_shapes=[
            pltpu.VMEM((3 * BLOCK_ROWS, 128), jnp.float32),
            pltpu.VMEM((5, 3, B * B * B), jnp.float32),
            pltpu.SemaphoreType.DMA((5,)),
        ],
        compiler_params=pltpu.CompilerParams(vmem_limit_bytes=LIMIT),
        name="place",
    )(numbers, *from_y, *from_x, own)


def exchange(values, move, sends):
    count_x, count_y = lax.axis_size("bx"), lax.axis_size("by")
    pairs = []
    for i in range(count_x):
        for j in range(count_y):
            to_i, to_j = move(i, j)
            to_i, to_j = to_i % count_x, to_j % count_y
            if sends(j, to_j):
                pairs.append((i * count_y + j, to_i * count_y + to_j))
    return lax.ppermute(values, ("bx", "by"), pairs)


def on_device(cells_in, block_levels, send_x, send_y, layout, face_out, ghost_src):
    half_x, half_y = lax.axis_size("bx") // 2, lax.axis_size("by") // 2
    pairings = (
        lambda i, j: (i, ((j + 1) ^ 1) - 1),
        lambda i, j: (((i + 1) ^ 1) - 1, j),
        lambda i, j: (i ^ 1, j),
        lambda i, j: (i, j ^ 1),
    )

    def upper(j, to_j):
        return j >= half_y or to_j >= half_y

    def lower(j, to_j):
        return not upper(j, to_j)

    def anyone(j, to_j):
        return True

    def by_partner(i, j):
        return i, j ^ half_y

    def bx_partner(i, j):
        return i ^ half_x, j

    numbers, sweep, table, *messages = pack(
        cells_in.transpose(1, 0, 2), layout, block_levels, ghost_src, face_out
    )
    common = (send_x, send_y, numbers, sweep, table)
    early = [
        exchange(m, pairing, sends)
        for m, pairing, sends in zip(messages, pairings, (anyone, upper, upper, upper))
    ]
    upper_faces = [[r] for r in early]
    y_upper, *messages = update(
        "y_upper", True, ((1, 8),), *common, upper_faces, handed=messages[1:]
    )
    y_from_upper = exchange(y_upper, by_partner, lambda j, to_j: j >= half_y)
    late = [exchange(m, pairing, lower) for m, pairing in zip(messages, pairings[1:])]
    lower_faces = [[r] for r in (early[0], *late)]
    x_lower, y_lower = update(
        "lower", False, ((0, 16), (1, 8)), *common, lower_faces, after=(y_upper,)
    )
    x_from_lower = exchange(x_lower, bx_partner, lower)
    y_from_lower = exchange(y_lower, by_partner, lambda j, to_j: j < half_y)
    (x_upper,) = update(
        "x_upper", True, ((0, 0),), *common, upper_faces, after=(y_lower, y_from_upper)
    )
    x_from_upper = exchange(x_upper, bx_partner, upper)
    all_faces = [[early[0]], *[list(pair) for pair in zip(early[1:], late)]]
    (own,) = update("own", None, ((2, 0),), *common, all_faces, after=(x_upper,))
    from_y, from_x = (y_from_upper, y_from_lower), (x_from_upper, x_from_lower)
    return place(numbers, from_y, from_x, own).transpose(1, 0, 2)


def solution(mesh):
    return jax.shard_map(
        on_device,
        mesh=mesh,
        in_specs=(
            P(("bx", "by"), None, None),
            P(("bx", "by")),
            P(("bx", "by"), None),
            P(("bx", "by"), None),
            P(("bx", "by"), None),
            P(("bx", "by"), None, None),
            P(("bx", "by"), None, None),
        ),
        out_specs=P(("bx", "by"), None, None),
        check_vma=False,
    )
```

```python
import functools

import jax
import jax.numpy as jnp
from jax import lax
from jax.experimental import pallas as pl
from jax.experimental.pallas import tpu as pltpu
from jax.sharding import PartitionSpec as P

B = 16
GAMMA = 1.4
STEP = 0.05
HALF = 8
FIELD_ROWS = B * 8
SWEEP_ROWS = 5 * FIELD_ROWS
BLOCK_ROWS = 5 * 2 * B
FACE_ROWS = 24
GHOST_ROWS = 4 * 8


def slot_of(field, direction):
    if field == 1:
        return 1 + direction
    if field == 1 + direction:
        return 1
    return field


def lanes(shape=(8, 128)):
    return lax.broadcasted_iota(jnp.int32, shape, 1)


def rows(shape=(8, 128)):
    return lax.broadcasted_iota(jnp.int32, shape, 0)


def take(values, index, axis):
    return jnp.take_along_axis(values, index, axis=axis, mode="promise_in_bounds")


class Turns:
    def __init__(self):
        lane, row = lanes(), rows()
        group, inner = lane // 16, lane % 16
        self.low = inner < 8
        self.skew = ((group + row) % 8) * 16 + inner
        self.shift = (row - group) % 8
        self.back = ((row - group) % 8) * 16 + inner
        self.skew_half = ((group + row) % 8) * 16 + (inner + 8) % 16
        self.back_half = ((row - group) % 8) * 16 + (inner + 8) % 16
        source_group = (group + row) % 8
        self.skew_z = (inner % 8) * 16 + (inner // 8) * 8 + source_group
        z_low, z_high = inner % 8, inner // 8
        self.back_z = ((row - z_low) % 8) * 16 + z_high * 8 + group

    def turn(self, v):
        return take(take(take(v, self.skew, 1), self.shift, 0), self.back, 1)

    def to_z(self, v0, v1):
        t0 = take(take(v0, self.skew_z, 1), self.shift, 0)
        t1 = take(take(v1, self.skew_z, 1), self.shift, 0)
        first = jnp.where(self.low, take(t0, self.back, 1), take(t1, self.back_half, 1))
        second = jnp.where(self.low, take(t0, self.back_half, 1), take(t1, self.back, 1))
        return first, second

    def from_z(self, first, second):
        t0 = jnp.where(self.low, take(first, self.skew, 1), take(second, self.skew_half, 1))
        t1 = jnp.where(self.low, take(first, self.skew_half, 1), take(second, self.skew, 1))
        return tuple(take(take(t, self.shift, 0), self.back_z, 1) for t in (t0, t1))


def parities():
    return lax.axis_index("bx") % 2, lax.axis_index("by") % 2


def pack_kernel(
    cells_in, layout_in, levels_in, ghost_src_in, face_out_in, *rest
):
    numbers, sweep, table, *messages = rest[:7]
    cells, layout, levels, ghost_src, face_out, cells_sem, small_sem = rest[7:]
    odd_x, odd_y = parities()
    copies = [
        pltpu.make_async_copy(cells_in.at[f], cells.at[f], cells_sem.at[f]) for f in range(5)
    ]
    small = [
        pltpu.make_async_copy(source, target, small_sem.at[i])
        for i, (source, target) in enumerate(
            (
                (face_out_in, face_out),
                (layout_in, layout),
                (levels_in, levels),
                (ghost_src_in, ghost_src),
            )
        )
    ]
    for copy in copies + small:
        copy.start()
    turns = Turns()
    for field in range(5):
        base = field * FIELD_ROWS
        to_y = slot_of(field, 1) * FIELD_ROWS
        to_z = slot_of(field, 2) * FIELD_ROWS
        copies[field].wait()
        for t in range(2 * B):
            row = base + (t // 2) * 8 + t % 2
            sweep[pl.ds(row, 4, stride=SWEEP_ROWS), :] = cells[
                field, :, t * 128 : (t + 1) * 128
            ]
        for first in range(0, 4 * SWEEP_ROWS, SWEEP_ROWS):
            for xh in range(2):
                v = [
                    sweep[pl.ds(first + base + HALF * xh * 8 + h, 8, stride=8), :]
                    for h in range(2)
                ]
                for h in range(2):
                    start = first + to_y + HALF * h * 8 + 2 + xh
                    sweep[pl.ds(start, 8, stride=8), :] = turns.turn(v[h])
                for zh, value in enumerate(turns.to_z(v[0], v[1])):
                    start = first + to_z + HALF * zh * 8 + 4 + xh
                    sweep[pl.ds(start, 8, stride=8), :] = value
    for s in range(4):
        for face in range(6):
            direction, high = face // 2, face % 2
            for layer in range(2):
                i = B - 1 - layer if high else layer
                for h in range(2):
                    row = s * SWEEP_ROWS + i * 8 + direction * 2 + h
                    to = (layer * 2 + h) * 5
                    table[s * 6 + face, to : to + 5, :] = sweep[
                        pl.ds(row, 5, stride=FIELD_ROWS), :
                    ]
                    if direction:
                        for field, slot in ((1, 1 + direction), (1 + direction, 1)):
                            table[s * 6 + face, to + field : to + field + 1, :] = sweep[
                                pl.ds(slot * FIELD_ROWS + row, 1), :
                            ]
    for copy in small:
        copy.wait()
    for m, one_list in enumerate((2 + (1 - odd_y), 1 - odd_x, odd_x, 2 + odd_y)):
        for k in range(4):
            messages[m][k] = table[face_out[0, one_list, k]]
    codes = [layout[0, j] for j in range(3)]
    kept = functools.reduce(jnp.maximum, [jnp.where(c < 4, c, 0) for c in codes])
    listed = {}
    listed.update({3 + j: codes[j] for j in range(3)})
    listed.update({8 + j: levels[j] for j in range(4)})
    listed.update({12 + s * 6 + f: ghost_src[0, s, f] for s in range(4) for f in range(6)})
    for i in range(3, 40):
        numbers[0, i] = listed.get(i, 0)
    numbers[0, 2] = kept


def limited(left, right):
    return jnp.maximum(jnp.minimum(left, right), 0.0) + jnp.minimum(jnp.maximum(left, right), 0.0)


def fluxes_of(q):
    density, normal, second, third, pressure = q
    mass = density * normal
    kinetic = 0.5 * density * (normal * normal + second * second + third * third)
    energy = pressure * (1.0 / (GAMMA - 1.0)) + kinetic
    cons = (density, mass, density * second, density * third, energy)
    flux = (mass, mass * normal + pressure, mass * second, mass * third, normal * (energy + pressure))
    scaled = GAMMA * pressure
    signal = jnp.abs(normal) + scaled * lax.rsqrt(scaled * density)
    return cons, flux, signal


def step_of(level):
    return jnp.where(level == 0, STEP, jnp.where(level == 1, STEP * 2, STEP * 4))


def upper_half():
    return lax.axis_index("by") >= lax.axis_size("by") // 2


def update_kernel(half, blocks, counts, handed, send_x, send_y, numbers, sweep, table, *rest):
    received, rest = rest[: sum(counts)], rest[sum(counts) :]
    scratch = rest[-3:]
    outs = rest[-3 - len(blocks) - handed : -3 - handed]
    for source, target in zip(rest[:handed], rest[-3 - handed : -3]):
        target[...] = source[...]

    def body():
        remote = scratch[0]
        first = 0
        for m, count in enumerate(counts):
            for k in range(4):
                remote[m * 4 + k] = sum(array[k] for array in received[first : first + count])
            first += count
        for (which, extra), out in zip(blocks, outs):
            s = (send_x[0, 0], send_y[0, 0], numbers[0, 2])[which]
            update_body(s, numbers, sweep, table, out, *scratch)
            if extra:
                out[BLOCK_ROWS : BLOCK_ROWS + extra, :] = jnp.zeros((extra, 128), jnp.float32)

    if half is None:
        body()
    else:
        pl.when(upper_half() == half)(body)


def update_body(s, numbers, sweep, table, out, remote, ghost, change):
    turns = Turns()
    odd_x, odd_y = parities()
    ratio = step_of(numbers[0, 8 + s])
    for face in range(6):
        direction, high = face // 2, face % 2
        code = numbers[0, 12 + s * 6 + face]
        far = jnp.maximum(code - 24, 0)
        which = far // 4
        along_x = jnp.where(which == odd_x, 1, 2)
        along_y = jnp.where(which - 2 == odd_y, 0, 3)
        far = jnp.where(which < 2, along_x, along_y) * 4 + far % 4
        near = jnp.minimum(code, 23)
        for layer in range(2):
            i = 2 + layer if high else 1 - layer
            for h in range(2):
                row = i * 8 + direction * 2 + h
                at = (layer * 2 + h) * 5
                moves = [(pl.ds(at, 5), pl.ds(row, 5, stride=GHOST_ROWS))]
                if direction:
                    for field, to in ((1, 1 + direction), (1 + direction, 1)):
                        moves.append((pl.ds(at + field, 1), pl.ds(to * GHOST_ROWS + row, 1)))
                for source, target in moves:
                    ghost[target, :] = jnp.where(
                        code < 24, table[near, source, :], remote[far, source, :]
                    )

    def cells_at(i):
        if 0 <= i < B:
            return [sweep[s, pl.ds(f * FIELD_ROWS + i * 8, 8), :] for f in range(5)]
        k = i + 2 if i < 0 else i - B + 2
        return [ghost[pl.ds(f * GHOST_ROWS + k * 8, 8), :] for f in range(5)]

    here, after = cells_at(-2), cells_at(-1)
    right = [b - a for a, b in zip(here, after)]
    left_face = last_flux = None
    for i in range(-1, B + 1):
        here, after, left = after, cells_at(i + 2 - 1), right
        right = [b - a for a, b in zip(here, after)]
        half = [0.5 * limited(a, b) for a, b in zip(left, right)]
        density, normal, _, _, pressure = here
        carried = ratio * normal
        moved = [carried * a for a in half]
        centre = [
            density - (moved[0] + ratio * density * half[1]),
            normal - (moved[1] + ratio * half[4] / density),
            here[2] - moved[2],
            here[3] - moved[3],
            pressure - (moved[4] + (ratio * GAMMA) * pressure * half[1]),
        ]
        if i >= 0:
            cons, flux, signal = fluxes_of([a - b for a, b in zip(centre, half)])
            old_cons, old_flux, old_signal = left_face
            speed = jnp.maximum(signal, old_signal)
            face_flux = [
                (fa + fb) - speed * (ub - ua)
                for fa, fb, ua, ub in zip(old_flux, flux, old_cons, cons)
            ]
            if i >= 1:
                for f in range(5):
                    change[pl.ds(f * FIELD_ROWS + (i - 1) * 8, 8), :] = face_flux[f] - last_flux[f]
            last_flux = face_flux
        if i < B:
            left_face = fluxes_of([a + b for a, b in zip(centre, half)])

    def in_place(ref, start):
        return ref[pl.ds(start, 8, stride=8), :]

    scale = 0.5 * ratio
    for xh in range(2):
        prims = [
            [sweep[s, pl.ds(f * FIELD_ROWS + HALF * xh * 8 + h, 8, stride=8), :] for h in range(2)]
            for f in range(5)
        ]
        for f in range(5):
            along_y = slot_of(f, 1) * FIELD_ROWS
            along_z = slot_of(f, 2) * FIELD_ROWS
            from_z = turns.from_z(
                *[in_place(change, along_z + HALF * zh * 8 + 4 + xh) for zh in range(2)]
            )
            for h in range(2):
                total = (
                    in_place(change, f * FIELD_ROWS + HALF * xh * 8 + h)
                    + turns.turn(in_place(change, along_y + HALF * h * 8 + 2 + xh))
                    + from_z[h]
                )
                density, u, v, w, pressure = (prims[k][h] for k in range(5))
                if f == 0:
                    initial = density
                elif f < 4:
                    initial = density * prims[f][h]
                else:
                    initial = pressure * (1.0 / (GAMMA - 1.0)) + 0.5 * density * (
                        u * u + v * v + w * w
                    )
                row = f * 2 * B + h * B + HALF * xh
                out[row : row + 8, :] = initial - scale * total


def place_kernel(numbers, from_y0, from_y1, from_x0, from_x1, own, out, slots, staged, sems):
    codes = [numbers[0, 3 + j] for j in range(3)]
    at_x = jnp.where(codes[1] == 4, 1, jnp.where(codes[2] == 4, 2, 0))
    at_y = jnp.where(codes[1] == 5, 1, jnp.where(codes[2] == 5, 2, 0))
    at_own = 3 - at_x - at_y
    empty = codes[0] + codes[1] + codes[2] == 8
    copies = []
    for f in range(5):
        one = pl.ds(f * 2 * B, 2 * B)
        values = (
            (jnp.where(empty, 0.0, own[one, :]), at_own),
            (from_x0[one, :] + from_x1[one, :], at_x),
            (from_y0[one, :] + from_y1[one, :], at_y),
        )
        for v, at in values:
            slots[pl.ds(pl.multiple_of(at * BLOCK_ROWS + f * 2 * B, 2 * B), 2 * B), :] = v
        for t in range(2 * B):
            row = f * 2 * B + (t % 2) * B + t // 2
            staged[f, :, t * 128 : (t + 1) * 128] = slots[pl.ds(row, 3, stride=BLOCK_ROWS), :]
        copies.append(pltpu.make_async_copy(staged.at[f], out.at[f], sems.at[f]))
        copies[-1].start()
    for copy in copies:
        copy.wait()


SMEM = pl.BlockSpec(memory_space=pltpu.SMEM)
VMEM = pl.BlockSpec(memory_space=pltpu.VMEM)
HBM = pl.BlockSpec(memory_space=pltpu.HBM)
ANY = pl.BlockSpec(memory_space=pl.ANY)
LIMIT = 48 << 20


def struct(*shape):
    return jax.ShapeDtypeStruct(shape, jnp.float32)


def in_hbm(array):
    return pltpu.with_memory_space_constraint(array, pltpu.HBM)


def pack(cells, *small):
    return pl.pallas_call(
        pack_kernel,
        out_shape=(
            pltpu.SMEM((1, 40), jnp.int32),
            struct(4 * SWEEP_ROWS, 128),
            struct(24, FACE_ROWS, 128),
        )
        + (struct(4, FACE_ROWS, 128),) * 4,
        in_specs=[HBM] * (1 + len(small)),
        out_specs=(SMEM,) + (VMEM,) * 6,
        scratch_shapes=[
            pltpu.VMEM(cells.shape, jnp.float32),
            *[pltpu.SMEM(array.shape, jnp.int32) for array in small],
            pltpu.SemaphoreType.DMA((5,)),
            pltpu.SemaphoreType.DMA((len(small),)),
        ],
        compiler_params=pltpu.CompilerParams(vmem_limit_bytes=LIMIT),
        name="pack",
    )(*[in_hbm(array) for array in (cells, *small)])


def update(name, half, blocks, send_x, send_y, numbers, sweep, table, received, handed=(), after=()):
    counts = tuple(len(arrays) for arrays in received)
    flat = [array for arrays in received for array in arrays]
    return pl.pallas_call(
        functools.partial(update_kernel, half, blocks, counts, len(handed)),
        out_shape=(
            *[struct(BLOCK_ROWS + extra, 128) for _, extra in blocks],
            *[struct(*array.shape) for array in handed],
        ),
        in_specs=[SMEM] * 3 + [VMEM] * (2 + len(flat) + len(handed)) + [ANY] * len(after),
        out_specs=(VMEM,) * (len(blocks) + len(handed)),
        scratch_shapes=[
            pltpu.VMEM((16, FACE_ROWS, 128), jnp.float32),
            pltpu.VMEM((5 * GHOST_ROWS, 128), jnp.float32),
            pltpu.VMEM((SWEEP_ROWS, 128), jnp.float32),
        ],
        compiler_params=pltpu.CompilerParams(vmem_limit_bytes=LIMIT),
        name=name,
    )(send_x, send_y, numbers, sweep.reshape(4, SWEEP_ROWS, 128), table, *flat, *handed, *after)


def place(numbers, from_y, from_x, own):
    return pl.pallas_call(
        place_kernel,
        out_shape=struct(5, 3, B * B * B),
        in_specs=[SMEM] + [VMEM] * 5,
        out_specs=HBM,
        scratch_shapes=[
            pltpu.VMEM((3 * BLOCK_ROWS, 128), jnp.float32),
            pltpu.VMEM((5, 3, B * B * B), jnp.float32),
            pltpu.SemaphoreType.DMA((5,)),
        ],
        compiler_params=pltpu.CompilerParams(vmem_limit_bytes=LIMIT),
        name="place",
    )(numbers, *from_y, *from_x, own)


def exchange(values, move, sends):
    count_x, count_y = lax.axis_size("bx"), lax.axis_size("by")
    pairs = []
    for i in range(count_x):
        for j in range(count_y):
            to_i, to_j = move(i, j)
            to_i, to_j = to_i % count_x, to_j % count_y
            if sends(j, to_j):
                pairs.append((i * count_y + j, to_i * count_y + to_j))
    return lax.ppermute(values, ("bx", "by"), pairs)


def on_device(cells_in, block_levels, send_x, send_y, layout, face_out, ghost_src):
    half_x, half_y = lax.axis_size("bx") // 2, lax.axis_size("by") // 2
    pairings = (
        lambda i, j: (i, ((j + 1) ^ 1) - 1),
        lambda i, j: (((i + 1) ^ 1) - 1, j),
        lambda i, j: (i ^ 1, j),
        lambda i, j: (i, j ^ 1),
    )

    def upper(j, to_j):
        return j >= half_y or to_j >= half_y

    def lower(j, to_j):
        return not upper(j, to_j)

    def anyone(j, to_j):
        return True

    def by_partner(i, j):
        return i, j ^ half_y

    def bx_partner(i, j):
        return i ^ half_x, j

    numbers, sweep, table, *messages = pack(
        cells_in.transpose(1, 0, 2), layout, block_levels, ghost_src, face_out
    )
    common = (send_x, send_y, numbers, sweep, table)
    early = [
        exchange(m, pairing, sends)
        for m, pairing, sends in zip(messages, pairings, (anyone, upper, upper, upper))
    ]
    upper_faces = [[r] for r in early]
    y_upper, *messages = update(
        "y_upper", True, ((1, 0),), *common, upper_faces, handed=messages[1:]
    )
    y_from_upper = exchange(y_upper, by_partner, lambda j, to_j: j >= half_y)
    late = [exchange(m, pairing, lower) for m, pairing in zip(messages, pairings[1:])]
    lower_faces = [[r] for r in (early[0], *late)]
    (x_lower,) = update("x_lower", False, ((0, 8),), *common, lower_faces, after=(y_upper,))
    x_from_lower = exchange(x_lower, bx_partner, lower)
    (y_lower,) = update("y_lower", False, ((1, 0),), *common, lower_faces, after=(x_lower,))
    y_from_lower = exchange(y_lower, by_partner, lambda j, to_j: j < half_y)
    (x_upper,) = update(
        "x_upper", True, ((0, 0),), *common, upper_faces, after=(y_lower, y_from_upper)
    )
    x_from_upper = exchange(x_upper, bx_partner, upper)
    all_faces = [[early[0]], *[list(pair) for pair in zip(early[1:], late)]]
    (own,) = update("own", None, ((2, 0),), *common, all_faces, after=(x_upper,))
    from_y, from_x = (y_from_upper, y_from_lower), (x_from_upper, x_from_lower)
    return place(numbers, from_y, from_x, own).transpose(1, 0, 2)


def solution(mesh):
    return jax.shard_map(
        on_device,
        mesh=mesh,
        in_specs=(
            P(("bx", "by"), None, None),
            P(("bx", "by")),
            P(("bx", "by"), None),
            P(("bx", "by"), None),
            P(("bx", "by"), None),
            P(("bx", "by"), None, None),
            P(("bx", "by"), None, None),
        ),
        out_specs=P(("bx", "by"), None, None),
        check_vma=False,
    )
```

```python
import functools

import jax
import jax.numpy as jnp
from jax import lax
from jax.experimental import pallas as pl
from jax.experimental.pallas import tpu as pltpu
from jax.sharding import PartitionSpec as P

B = 16
GAMMA = 1.4
STEP = 0.05
HALF = 8
FIELD_ROWS = B * 8
SWEEP_ROWS = 5 * FIELD_ROWS
BLOCK_ROWS = 5 * 2 * B
FACE_ROWS = 24
GHOST_ROWS = 4 * 8


def slot_of(field, direction):
    if field == 1:
        return 1 + direction
    if field == 1 + direction:
        return 1
    return field


def lanes(shape=(8, 128)):
    return lax.broadcasted_iota(jnp.int32, shape, 1)


def rows(shape=(8, 128)):
    return lax.broadcasted_iota(jnp.int32, shape, 0)


def take(values, index, axis):
    return jnp.take_along_axis(values, index, axis=axis, mode="promise_in_bounds")


class Turns:
    def __init__(self):
        lane, row = lanes(), rows()
        group, inner = lane // 16, lane % 16
        self.low = inner < 8
        self.skew = ((group + row) % 8) * 16 + inner
        self.shift = (row - group) % 8
        self.back = ((row - group) % 8) * 16 + inner
        self.skew_half = ((group + row) % 8) * 16 + (inner + 8) % 16
        self.back_half = ((row - group) % 8) * 16 + (inner + 8) % 16
        source_group = (group + row) % 8
        self.skew_z = (inner % 8) * 16 + (inner // 8) * 8 + source_group
        self.skew_z_half = (inner % 8) * 16 + (1 - inner // 8) * 8 + source_group
        z_low, z_high = inner % 8, inner // 8
        self.back_z = ((row - z_low) % 8) * 16 + z_high * 8 + group
        self.back_z_half = ((row - z_low) % 8) * 16 + (1 - z_high) * 8 + group

    def turn(self, v):
        return take(take(take(v, self.skew, 1), self.shift, 0), self.back, 1)

    def from_z(self, first, second):
        a, b = take(first, self.skew, 1), take(second, self.skew_half, 1)
        t0 = take(jnp.where(self.low, a, b), self.shift, 0)
        t1 = take(jnp.where(self.low, b, a), self.shift, 0)
        return take(t0, self.back_z, 1), take(t1, self.back_z_half, 1)


def parities():
    return lax.axis_index("bx") % 2, lax.axis_index("by") % 2


def pack_kernel(
    cells_in, layout_in, levels_in, ghost_src_in, face_out_in, *rest
):
    numbers, sweep, table, *messages = rest[:7]
    cells, layout, levels, ghost_src, face_out, cells_sem, small_sem = rest[7:]
    odd_x, odd_y = parities()
    copies = [
        pltpu.make_async_copy(cells_in.at[f], cells.at[f], cells_sem.at[f]) for f in range(5)
    ]
    small = [
        pltpu.make_async_copy(source, target, small_sem.at[i])
        for i, (source, target) in enumerate(
            (
                (face_out_in, face_out),
                (layout_in, layout),
                (levels_in, levels),
                (ghost_src_in, ghost_src),
            )
        )
    ]
    for copy in copies + small:
        copy.start()
    turns = Turns()
    for field in range(5):
        base = field * FIELD_ROWS
        to_y = slot_of(field, 1) * FIELD_ROWS
        to_z = slot_of(field, 2) * FIELD_ROWS
        copies[field].wait()
        for t in range(2 * B):
            row = base + (t // 2) * 8 + t % 2
            sweep[pl.ds(row, 4, stride=SWEEP_ROWS), :] = cells[
                field, :, t * 128 : (t + 1) * 128
            ]
        places = [(s * SWEEP_ROWS, xh) for s in range(4) for xh in range(2)]
        v = [
            sweep[pl.ds(first + base + HALF * xh * 8 + h, 8, stride=8), :]
            for first, xh in places
            for h in range(2)
        ]
        y = [take(a, turns.skew, 1) for a in v]
        z = [take(a, (turns.skew_z, turns.skew_z_half)[k % 2], 1) for k, a in enumerate(v)]
        y = [take(a, turns.shift, 0) for a in y]
        z = [take(a, turns.shift, 0) for a in z]
        y = [take(a, turns.back, 1) for a in y]
        pairs = list(zip(z[::2], z[1::2]))
        ones = [take(jnp.where(turns.low, a, b), turns.back, 1) for a, b in pairs]
        twos = [take(jnp.where(turns.low, b, a), turns.back_half, 1) for a, b in pairs]
        for k, (first, xh) in enumerate(places):
            for h in range(2):
                start = first + to_y + HALF * h * 8 + 2 + xh
                sweep[pl.ds(start, 8, stride=8), :] = y[2 * k + h]
            for zh, value in enumerate((ones[k], twos[k])):
                start = first + to_z + HALF * zh * 8 + 4 + xh
                sweep[pl.ds(start, 8, stride=8), :] = value
    for s in range(4):
        for face in range(6):
            direction, high = face // 2, face % 2
            for layer in range(2):
                i = B - 1 - layer if high else layer
                for h in range(2):
                    row = s * SWEEP_ROWS + i * 8 + direction * 2 + h
                    to = (layer * 2 + h) * 5
                    table[s * 6 + face, to : to + 5, :] = sweep[
                        pl.ds(row, 5, stride=FIELD_ROWS), :
                    ]
                    if direction:
                        for field, slot in ((1, 1 + direction), (1 + direction, 1)):
                            table[s * 6 + face, to + field : to + field + 1, :] = sweep[
                                pl.ds(slot * FIELD_ROWS + row, 1), :
                            ]
    for copy in small:
        copy.wait()
    for m, one_list in enumerate((2 + (1 - odd_y), 1 - odd_x, odd_x, 2 + odd_y)):
        for k in range(4):
            messages[m][k] = table[face_out[0, one_list, k]]
    codes = [layout[0, j] for j in range(3)]
    kept = functools.reduce(jnp.maximum, [jnp.where(c < 4, c, 0) for c in codes])
    listed = {}
    listed.update({3 + j: codes[j] for j in range(3)})
    listed.update({8 + j: levels[j] for j in range(4)})
    listed.update({12 + s * 6 + f: ghost_src[0, s, f] for s in range(4) for f in range(6)})
    for i in range(3, 40):
        numbers[0, i] = listed.get(i, 0)
    numbers[0, 2] = kept


def limited(left, right):
    return jnp.maximum(jnp.minimum(left, right), 0.0) + jnp.minimum(jnp.maximum(left, right), 0.0)


def fluxes_of(q):
    density, normal, second, third, pressure = q
    mass = density * normal
    kinetic = 0.5 * density * (normal * normal + second * second + third * third)
    energy = pressure * (1.0 / (GAMMA - 1.0)) + kinetic
    cons = (density, mass, density * second, density * third, energy)
    flux = (mass, mass * normal + pressure, mass * second, mass * third, normal * (energy + pressure))
    scaled = GAMMA * pressure
    signal = jnp.abs(normal) + scaled * lax.rsqrt(scaled * density)
    return cons, flux, signal


def step_of(level):
    return jnp.where(level == 0, STEP, jnp.where(level == 1, STEP * 2, STEP * 4))


def upper_half():
    return lax.axis_index("by") >= lax.axis_size("by") // 2


def update_kernel(half, blocks, counts, handed, send_x, send_y, numbers, sweep, table, *rest):
    received, rest = rest[: sum(counts)], rest[sum(counts) :]
    scratch = rest[-3:]
    outs = rest[-3 - len(blocks) - handed : -3 - handed]
    for source, target in zip(rest[:handed], rest[-3 - handed : -3]):
        target[...] = source[...]

    def body():
        remote = scratch[0]
        first = 0
        for m, count in enumerate(counts):
            for k in range(4):
                remote[m * 4 + k] = sum(array[k] for array in received[first : first + count])
            first += count
        for (which, extra), out in zip(blocks, outs):
            s = (send_x[0, 0], send_y[0, 0], numbers[0, 2])[which]
            update_body(s, numbers, sweep, table, out, *scratch)
            if extra:
                out[BLOCK_ROWS : BLOCK_ROWS + extra, :] = jnp.zeros((extra, 128), jnp.float32)

    if half is None:
        body()
    else:
        pl.when(upper_half() == half)(body)


def update_body(s, numbers, sweep, table, out, remote, ghost, change):
    turns = Turns()
    odd_x, odd_y = parities()
    ratio = step_of(numbers[0, 8 + s])
    for face in range(6):
        direction, high = face // 2, face % 2
        code = numbers[0, 12 + s * 6 + face]
        far = jnp.maximum(code - 24, 0)
        which = far // 4
        along_x = jnp.where(which == odd_x, 1, 2)
        along_y = jnp.where(which - 2 == odd_y, 0, 3)
        far = jnp.where(which < 2, along_x, along_y) * 4 + far % 4
        near = jnp.minimum(code, 23)
        for layer in range(2):
            i = 2 + layer if high else 1 - layer
            for h in range(2):
                row = i * 8 + direction * 2 + h
                at = (layer * 2 + h) * 5
                moves = [(pl.ds(at, 5), pl.ds(row, 5, stride=GHOST_ROWS))]
                if direction:
                    for field, to in ((1, 1 + direction), (1 + direction, 1)):
                        moves.append((pl.ds(at + field, 1), pl.ds(to * GHOST_ROWS + row, 1)))
                for source, target in moves:
                    ghost[target, :] = jnp.where(
                        code < 24, table[near, source, :], remote[far, source, :]
                    )

    def cells_at(i):
        if 0 <= i < B:
            return [sweep[s, pl.ds(f * FIELD_ROWS + i * 8, 8), :] for f in range(5)]
        k = i + 2 if i < 0 else i - B + 2
        return [ghost[pl.ds(f * GHOST_ROWS + k * 8, 8), :] for f in range(5)]

    here, after = cells_at(-2), cells_at(-1)
    right = [b - a for a, b in zip(here, after)]
    left_face = last_flux = None
    for i in range(-1, B + 1):
        here, after, left = after, cells_at(i + 2 - 1), right
        right = [b - a for a, b in zip(here, after)]
        half = [0.5 * limited(a, b) for a, b in zip(left, right)]
        density, normal, _, _, pressure = here
        carried = ratio * normal
        moved = [carried * a for a in half]
        centre = [
            density - (moved[0] + ratio * density * half[1]),
            normal - (moved[1] + ratio * half[4] / density),
            here[2] - moved[2],
            here[3] - moved[3],
            pressure - (moved[4] + (ratio * GAMMA) * pressure * half[1]),
        ]
        if i >= 0:
            cons, flux, signal = fluxes_of([a - b for a, b in zip(centre, half)])
            old_cons, old_flux, old_signal = left_face
            speed = jnp.maximum(signal, old_signal)
            face_flux = [
                (fa + fb) - speed * (ub - ua)
                for fa, fb, ua, ub in zip(old_flux, flux, old_cons, cons)
            ]
            if i >= 1:
                for f in range(5):
                    change[pl.ds(f * FIELD_ROWS + (i - 1) * 8, 8), :] = face_flux[f] - last_flux[f]
            last_flux = face_flux
        if i < B:
            left_face = fluxes_of([a + b for a, b in zip(centre, half)])

    def in_place(ref, start):
        return ref[pl.ds(start, 8, stride=8), :]

    scale = 0.5 * ratio
    for xh in range(2):
        prims = [
            [sweep[s, pl.ds(f * FIELD_ROWS + HALF * xh * 8 + h, 8, stride=8), :] for h in range(2)]
            for f in range(5)
        ]
        for f in range(5):
            along_y = slot_of(f, 1) * FIELD_ROWS
            along_z = slot_of(f, 2) * FIELD_ROWS
            from_z = turns.from_z(
                *[in_place(change, along_z + HALF * zh * 8 + 4 + xh) for zh in range(2)]
            )
            for h in range(2):
                total = (
                    in_place(change, f * FIELD_ROWS + HALF * xh * 8 + h)
                    + turns.turn(in_place(change, along_y + HALF * h * 8 + 2 + xh))
                    + from_z[h]
                )
                density, u, v, w, pressure = (prims[k][h] for k in range(5))
                if f == 0:
                    initial = density
                elif f < 4:
                    initial = density * prims[f][h]
                else:
                    initial = pressure * (1.0 / (GAMMA - 1.0)) + 0.5 * density * (
                        u * u + v * v + w * w
                    )
                row = f * 2 * B + h * B + HALF * xh
                out[row : row + 8, :] = initial - scale * total


def place_kernel(numbers, from_y0, from_y1, from_x0, from_x1, own, out, slots, staged, sems):
    codes = [numbers[0, 3 + j] for j in range(3)]
    at_x = jnp.where(codes[1] == 4, 1, jnp.where(codes[2] == 4, 2, 0))
    at_y = jnp.where(codes[1] == 5, 1, jnp.where(codes[2] == 5, 2, 0))
    at_own = 3 - at_x - at_y
    empty = codes[0] + codes[1] + codes[2] == 8
    copies = []
    for f in range(5):
        one = pl.ds(f * 2 * B, 2 * B)
        values = (
            (jnp.where(empty, 0.0, own[one, :]), at_own),
            (from_x0[one, :] + from_x1[one, :], at_x),
            (from_y0[one, :] + from_y1[one, :], at_y),
        )
        for v, at in values:
            slots[pl.ds(pl.multiple_of(at * BLOCK_ROWS + f * 2 * B, 2 * B), 2 * B), :] = v
        for t in range(2 * B):
            row = f * 2 * B + (t % 2) * B + t // 2
            staged[f, :, t * 128 : (t + 1) * 128] = slots[pl.ds(row, 3, stride=BLOCK_ROWS), :]
        copies.append(pltpu.make_async_copy(staged.at[f], out.at[f], sems.at[f]))
        copies[-1].start()
    for copy in copies:
        copy.wait()


SMEM = pl.BlockSpec(memory_space=pltpu.SMEM)
VMEM = pl.BlockSpec(memory_space=pltpu.VMEM)
HBM = pl.BlockSpec(memory_space=pltpu.HBM)
ANY = pl.BlockSpec(memory_space=pl.ANY)
LIMIT = 48 << 20


def struct(*shape):
    return jax.ShapeDtypeStruct(shape, jnp.float32)


def in_hbm(array):
    return pltpu.with_memory_space_constraint(array, pltpu.HBM)


def pack(cells, *small):
    return pl.pallas_call(
        pack_kernel,
        out_shape=(
            pltpu.SMEM((1, 40), jnp.int32),
            struct(4 * SWEEP_ROWS, 128),
            struct(24, FACE_ROWS, 128),
        )
        + (struct(4, FACE_ROWS, 128),) * 4,
        in_specs=[HBM] * (1 + len(small)),
        out_specs=(SMEM,) + (VMEM,) * 6,
        scratch_shapes=[
            pltpu.VMEM(cells.shape, jnp.float32),
            *[pltpu.SMEM(array.shape, jnp.int32) for array in small],
            pltpu.SemaphoreType.DMA((5,)),
            pltpu.SemaphoreType.DMA((len(small),)),
        ],
        compiler_params=pltpu.CompilerParams(vmem_limit_bytes=LIMIT),
        name="pack",
    )(*[in_hbm(array) for array in (cells, *small)])


def update(name, half, blocks, send_x, send_y, numbers, sweep, table, received, handed=(), after=()):
    counts = tuple(len(arrays) for arrays in received)
    flat = [array for arrays in received for array in arrays]
    return pl.pallas_call(
        functools.partial(update_kernel, half, blocks, counts, len(handed)),
        out_shape=(
            *[struct(BLOCK_ROWS + extra, 128) for _, extra in blocks],
            *[struct(*array.shape) for array in handed],
        ),
        in_specs=[SMEM] * 3 + [VMEM] * (2 + len(flat) + len(handed)) + [ANY] * len(after),
        out_specs=(VMEM,) * (len(blocks) + len(handed)),
        scratch_shapes=[
            pltpu.VMEM((16, FACE_ROWS, 128), jnp.float32),
            pltpu.VMEM((5 * GHOST_ROWS, 128), jnp.float32),
            pltpu.VMEM((SWEEP_ROWS, 128), jnp.float32),
        ],
        compiler_params=pltpu.CompilerParams(vmem_limit_bytes=LIMIT),
        name=name,
    )(send_x, send_y, numbers, sweep.reshape(4, SWEEP_ROWS, 128), table, *flat, *handed, *after)


def place(numbers, from_y, from_x, own):
    return pl.pallas_call(
        place_kernel,
        out_shape=struct(5, 3, B * B * B),
        in_specs=[SMEM] + [VMEM] * 5,
        out_specs=HBM,
        scratch_shapes=[
            pltpu.VMEM((3 * BLOCK_ROWS, 128), jnp.float32),
            pltpu.VMEM((5, 3, B * B * B), jnp.float32),
            pltpu.SemaphoreType.DMA((5,)),
        ],
        compiler_params=pltpu.CompilerParams(vmem_limit_bytes=LIMIT),
        name="place",
    )(numbers, *from_y, *from_x, own)


def exchange(values, move, sends):
    count_x, count_y = lax.axis_size("bx"), lax.axis_size("by")
    pairs = []
    for i in range(count_x):
        for j in range(count_y):
            to_i, to_j = move(i, j)
            to_i, to_j = to_i % count_x, to_j % count_y
            if sends(j, to_j):
                pairs.append((i * count_y + j, to_i * count_y + to_j))
    return lax.ppermute(values, ("bx", "by"), pairs)


def on_device(cells_in, block_levels, send_x, send_y, layout, face_out, ghost_src):
    half_x, half_y = lax.axis_size("bx") // 2, lax.axis_size("by") // 2
    pairings = (
        lambda i, j: (i, ((j + 1) ^ 1) - 1),
        lambda i, j: (((i + 1) ^ 1) - 1, j),
        lambda i, j: (i ^ 1, j),
        lambda i, j: (i, j ^ 1),
    )

    def upper(j, to_j):
        return j >= half_y or to_j >= half_y

    def lower(j, to_j):
        return not upper(j, to_j)

    def anyone(j, to_j):
        return True

    def by_partner(i, j):
        return i, j ^ half_y

    def bx_partner(i, j):
        return i ^ half_x, j

    numbers, sweep, table, *messages = pack(
        cells_in.transpose(1, 0, 2), layout, block_levels, ghost_src, face_out
    )
    common = (send_x, send_y, numbers, sweep, table)
    early = [
        exchange(m, pairing, sends)
        for m, pairing, sends in zip(messages, pairings, (anyone, upper, upper, upper))
    ]
    upper_faces = [[r] for r in early]
    y_upper, *messages = update(
        "y_upper", True, ((1, 0),), *common, upper_faces, handed=messages[1:]
    )
    y_from_upper = exchange(y_upper, by_partner, lambda j, to_j: j >= half_y)
    late = [exchange(m, pairing, lower) for m, pairing in zip(messages, pairings[1:])]
    lower_faces = [[r] for r in (early[0], *late)]
    (x_lower,) = update("x_lower", False, ((0, 8),), *common, lower_faces, after=(y_upper,))
    x_from_lower = exchange(x_lower, bx_partner, lower)
    (y_lower,) = update("y_lower", False, ((1, 0),), *common, lower_faces, after=(x_lower,))
    y_from_lower = exchange(y_lower, by_partner, lambda j, to_j: j < half_y)
    (x_upper,) = update(
        "x_upper", True, ((0, 0),), *common, upper_faces, after=(y_lower, y_from_upper)
    )
    x_from_upper = exchange(x_upper, bx_partner, upper)
    all_faces = [[early[0]], *[list(pair) for pair in zip(early[1:], late)]]
    (own,) = update("own", None, ((2, 0),), *common, all_faces, after=(x_upper,))
    from_y, from_x = (y_from_upper, y_from_lower), (x_from_upper, x_from_lower)
    return place(numbers, from_y, from_x, own).transpose(1, 0, 2)


def solution(mesh):
    return jax.shard_map(
        on_device,
        mesh=mesh,
        in_specs=(
            P(("bx", "by"), None, None),
            P(("bx", "by")),
            P(("bx", "by"), None),
            P(("bx", "by"), None),
            P(("bx", "by"), None),
            P(("bx", "by"), None, None),
            P(("bx", "by"), None, None),
        ),
        out_specs=P(("bx", "by"), None, None),
        check_vma=False,
    )
```

```python
import functools

import jax
import jax.numpy as jnp
from jax import lax
from jax.experimental import pallas as pl
from jax.experimental.pallas import tpu as pltpu
from jax.sharding import PartitionSpec as P

B = 16
GAMMA = 1.4
STEP = 0.05
HALF = 8
FIELD_ROWS = B * 8
SWEEP_ROWS = 5 * FIELD_ROWS
BLOCK_ROWS = 5 * 2 * B
FACE_ROWS = 24
GHOST_ROWS = 4 * 8


def slot_of(field, direction):
    if field == 1:
        return 1 + direction
    if field == 1 + direction:
        return 1
    return field


def lanes(shape=(8, 128)):
    return lax.broadcasted_iota(jnp.int32, shape, 1)


def rows(shape=(8, 128)):
    return lax.broadcasted_iota(jnp.int32, shape, 0)


def take(values, index, axis):
    return jnp.take_along_axis(values, index, axis=axis, mode="promise_in_bounds")


class Turns:
    def __init__(self):
        lane, row = lanes(), rows()
        group, inner = lane // 16, lane % 16
        self.low = inner < 8
        self.skew = ((group + row) % 8) * 16 + inner
        self.shift = (row - group) % 8
        self.back = ((row - group) % 8) * 16 + inner
        self.skew_half = ((group + row) % 8) * 16 + (inner + 8) % 16
        self.back_half = ((row - group) % 8) * 16 + (inner + 8) % 16
        source_group = (group + row) % 8
        self.skew_z = (inner % 8) * 16 + (inner // 8) * 8 + source_group
        self.skew_z_half = (inner % 8) * 16 + (1 - inner // 8) * 8 + source_group
        z_low, z_high = inner % 8, inner // 8
        self.back_z = ((row - z_low) % 8) * 16 + z_high * 8 + group
        self.back_z_half = ((row - z_low) % 8) * 16 + (1 - z_high) * 8 + group

    def turn(self, v):
        return take(take(take(v, self.skew, 1), self.shift, 0), self.back, 1)

    def from_z(self, first, second):
        a, b = take(first, self.skew, 1), take(second, self.skew_half, 1)
        t0 = take(jnp.where(self.low, a, b), self.shift, 0)
        t1 = take(jnp.where(self.low, b, a), self.shift, 0)
        return take(t0, self.back_z, 1), take(t1, self.back_z_half, 1)


def parities():
    return lax.axis_index("bx") % 2, lax.axis_index("by") % 2


def pack_kernel(
    cells_in, layout_in, levels_in, ghost_src_in, face_out_in, *rest
):
    numbers, sweep, table, *messages = rest[:7]
    cells, layout, levels, ghost_src, face_out, cells_sem, small_sem = rest[7:]
    odd_x, odd_y = parities()
    copies = [
        pltpu.make_async_copy(cells_in.at[f], cells.at[f], cells_sem.at[f]) for f in range(5)
    ]
    small = [
        pltpu.make_async_copy(source, target, small_sem.at[i])
        for i, (source, target) in enumerate(
            (
                (face_out_in, face_out),
                (layout_in, layout),
                (levels_in, levels),
                (ghost_src_in, ghost_src),
            )
        )
    ]
    for copy in copies + small:
        copy.start()
    turns = Turns()
    for field in range(5):
        base = field * FIELD_ROWS
        to_y = slot_of(field, 1) * FIELD_ROWS
        to_z = slot_of(field, 2) * FIELD_ROWS
        copies[field].wait()
        for t in range(2 * B):
            row = base + (t // 2) * 8 + t % 2
            sweep[pl.ds(row, 4, stride=SWEEP_ROWS), :] = cells[
                field, :, t * 128 : (t + 1) * 128
            ]
        places = [(s * SWEEP_ROWS, xh) for s in range(4) for xh in range(2)]
        v = [
            sweep[pl.ds(first + base + HALF * xh * 8 + h, 8, stride=8), :]
            for first, xh in places
            for h in range(2)
        ]
        y = [take(a, turns.skew, 1) for a in v]
        z = [take(a, (turns.skew_z, turns.skew_z_half)[k % 2], 1) for k, a in enumerate(v)]
        y = [take(a, turns.shift, 0) for a in y]
        z = [take(a, turns.shift, 0) for a in z]
        y = [take(a, turns.back, 1) for a in y]
        pairs = list(zip(z[::2], z[1::2]))
        ones = [take(jnp.where(turns.low, a, b), turns.back, 1) for a, b in pairs]
        twos = [take(jnp.where(turns.low, b, a), turns.back_half, 1) for a, b in pairs]
        for k, (first, xh) in enumerate(places):
            for h in range(2):
                start = first + to_y + HALF * h * 8 + 2 + xh
                sweep[pl.ds(start, 8, stride=8), :] = y[2 * k + h]
            for zh, value in enumerate((ones[k], twos[k])):
                start = first + to_z + HALF * zh * 8 + 4 + xh
                sweep[pl.ds(start, 8, stride=8), :] = value
    for s in range(4):
        for face in range(6):
            direction, high = face // 2, face % 2
            for layer in range(2):
                i = B - 1 - layer if high else layer
                for h in range(2):
                    row = s * SWEEP_ROWS + i * 8 + direction * 2 + h
                    to = (layer * 2 + h) * 5
                    table[s * 6 + face, to : to + 5, :] = sweep[
                        pl.ds(row, 5, stride=FIELD_ROWS), :
                    ]
                    if direction:
                        for field, slot in ((1, 1 + direction), (1 + direction, 1)):
                            table[s * 6 + face, to + field : to + field + 1, :] = sweep[
                                pl.ds(slot * FIELD_ROWS + row, 1), :
                            ]
    for copy in small:
        copy.wait()
    for m, one_list in enumerate((2 + (1 - odd_y), 1 - odd_x, odd_x, 2 + odd_y)):
        for k in range(4):
            messages[m][k] = table[face_out[0, one_list, k]]
    codes = [layout[0, j] for j in range(3)]
    kept = functools.reduce(jnp.maximum, [jnp.where(c < 4, c, 0) for c in codes])
    listed = {}
    listed.update({3 + j: codes[j] for j in range(3)})
    listed.update({8 + j: levels[j] for j in range(4)})
    listed.update({12 + s * 6 + f: ghost_src[0, s, f] for s in range(4) for f in range(6)})
    for i in range(3, 40):
        numbers[0, i] = listed.get(i, 0)
    numbers[0, 2] = kept


def limited(left, right):
    return jnp.maximum(jnp.minimum(left, right), 0.0) + jnp.minimum(jnp.maximum(left, right), 0.0)


def fluxes_of(q):
    density, normal, second, third, pressure = q
    mass = density * normal
    kinetic = 0.5 * density * (normal * normal + second * second + third * third)
    energy = pressure * (1.0 / (GAMMA - 1.0)) + kinetic
    cons = (density, mass, density * second, density * third, energy)
    flux = (mass, mass * normal + pressure, mass * second, mass * third, normal * (energy + pressure))
    scaled = GAMMA * pressure
    signal = jnp.abs(normal) + scaled * lax.rsqrt(scaled * density)
    return cons, flux, signal


def step_of(level):
    return jnp.where(level == 0, STEP, jnp.where(level == 1, STEP * 2, STEP * 4))


def upper_half():
    return lax.axis_index("by") >= lax.axis_size("by") // 2


def update_kernel(half, blocks, counts, handed, send_x, send_y, numbers, sweep, table, *rest):
    received, rest = rest[: sum(counts)], rest[sum(counts) :]
    scratch = rest[-3:]
    outs = rest[-3 - len(blocks) - handed : -3 - handed]
    for source, target in zip(rest[:handed], rest[-3 - handed : -3]):
        target[...] = source[...]

    def body():
        remote = scratch[0]
        first = 0
        for m, count in enumerate(counts):
            for k in range(4):
                remote[m * 4 + k] = sum(array[k] for array in received[first : first + count])
            first += count
        for (which, extra), out in zip(blocks, outs):
            s = (send_x[0, 0], send_y[0, 0], numbers[0, 2])[which]
            update_body(s, numbers, sweep, table, out, *scratch)
            if extra:
                out[BLOCK_ROWS : BLOCK_ROWS + extra, :] = jnp.zeros((extra, 128), jnp.float32)

    if half is None:
        body()
    else:
        pl.when(upper_half() == half)(body)


def update_body(s, numbers, sweep, table, out, remote, ghost, change):
    turns = Turns()
    odd_x, odd_y = parities()
    ratio = step_of(numbers[0, 8 + s])
    for face in range(6):
        direction, high = face // 2, face % 2
        code = numbers[0, 12 + s * 6 + face]
        far = jnp.maximum(code - 24, 0)
        which = far // 4
        along_x = jnp.where(which == odd_x, 1, 2)
        along_y = jnp.where(which - 2 == odd_y, 0, 3)
        far = jnp.where(which < 2, along_x, along_y) * 4 + far % 4
        near = jnp.minimum(code, 23)
        for layer in range(2):
            i = 2 + layer if high else 1 - layer
            for h in range(2):
                row = i * 8 + direction * 2 + h
                at = (layer * 2 + h) * 5
                moves = [(pl.ds(at, 5), pl.ds(row, 5, stride=GHOST_ROWS))]
                if direction:
                    for field, to in ((1, 1 + direction), (1 + direction, 1)):
                        moves.append((pl.ds(at + field, 1), pl.ds(to * GHOST_ROWS + row, 1)))
                for source, target in moves:
                    ghost[target, :] = jnp.where(
                        code < 24, table[near, source, :], remote[far, source, :]
                    )

    def cells_at(i):
        if 0 <= i < B:
            return [sweep[s, pl.ds(f * FIELD_ROWS + i * 8, 8), :] for f in range(5)]
        k = i + 2 if i < 0 else i - B + 2
        return [ghost[pl.ds(f * GHOST_ROWS + k * 8, 8), :] for f in range(5)]

    here, after = cells_at(-2), cells_at(-1)
    right = [b - a for a, b in zip(here, after)]
    left_face = last_flux = None
    for i in range(-1, B + 1):
        here, after, left = after, cells_at(i + 2 - 1), right
        right = [b - a for a, b in zip(here, after)]
        half = [0.5 * limited(a, b) for a, b in zip(left, right)]
        density, normal, _, _, pressure = here
        carried = ratio * normal
        moved = [carried * a for a in half]
        centre = [
            density - (moved[0] + ratio * density * half[1]),
            normal - (moved[1] + ratio * half[4] / density),
            here[2] - moved[2],
            here[3] - moved[3],
            pressure - (moved[4] + (ratio * GAMMA) * pressure * half[1]),
        ]
        if i >= 0:
            cons, flux, signal = fluxes_of([a - b for a, b in zip(centre, half)])
            old_cons, old_flux, old_signal = left_face
            speed = jnp.maximum(signal, old_signal)
            face_flux = [
                (fa + fb) - speed * (ub - ua)
                for fa, fb, ua, ub in zip(old_flux, flux, old_cons, cons)
            ]
            if i >= 1:
                for f in range(5):
                    change[pl.ds(f * FIELD_ROWS + (i - 1) * 8, 8), :] = face_flux[f] - last_flux[f]
            last_flux = face_flux
        if i < B:
            left_face = fluxes_of([a + b for a, b in zip(centre, half)])

    def in_place(ref, start):
        return ref[pl.ds(start, 8, stride=8), :]

    scale = 0.5 * ratio
    for xh in range(2):
        prims = [
            [sweep[s, pl.ds(f * FIELD_ROWS + HALF * xh * 8 + h, 8, stride=8), :] for h in range(2)]
            for f in range(5)
        ]
        for f in range(5):
            along_y = slot_of(f, 1) * FIELD_ROWS
            along_z = slot_of(f, 2) * FIELD_ROWS
            from_z = turns.from_z(
                *[in_place(change, along_z + HALF * zh * 8 + 4 + xh) for zh in range(2)]
            )
            for h in range(2):
                total = (
                    in_place(change, f * FIELD_ROWS + HALF * xh * 8 + h)
                    + turns.turn(in_place(change, along_y + HALF * h * 8 + 2 + xh))
                    + from_z[h]
                )
                density, u, v, w, pressure = (prims[k][h] for k in range(5))
                if f == 0:
                    initial = density
                elif f < 4:
                    initial = density * prims[f][h]
                else:
                    initial = pressure * (1.0 / (GAMMA - 1.0)) + 0.5 * density * (
                        u * u + v * v + w * w
                    )
                row = f * 2 * B + h * B + HALF * xh
                out[row : row + 8, :] = initial - scale * total


def place_kernel(half, numbers, from_y, from_x, own, *rest):
    @pl.when(upper_half() == half)
    def _():
        place_body(numbers, from_y, from_x, own, *rest[-4:])


def place_body(numbers, from_y, from_x, own, out, slots, staged, sems):
    codes = [numbers[0, 3 + j] for j in range(3)]
    at_x = jnp.where(codes[1] == 4, 1, jnp.where(codes[2] == 4, 2, 0))
    at_y = jnp.where(codes[1] == 5, 1, jnp.where(codes[2] == 5, 2, 0))
    at_own = 3 - at_x - at_y
    empty = codes[0] + codes[1] + codes[2] == 8
    copies = []
    for f in range(5):
        one = pl.ds(f * 2 * B, 2 * B)
        values = (
            (jnp.where(empty, 0.0, own[one, :]), at_own),
            (from_x[one, :], at_x),
            (from_y[one, :], at_y),
        )
        for v, at in values:
            slots[pl.ds(pl.multiple_of(at * BLOCK_ROWS + f * 2 * B, 2 * B), 2 * B), :] = v
        for t in range(2 * B):
            row = f * 2 * B + (t % 2) * B + t // 2
            staged[f, :, t * 128 : (t + 1) * 128] = slots[pl.ds(row, 3, stride=BLOCK_ROWS), :]
        copies.append(pltpu.make_async_copy(staged.at[f], out.at[f], sems.at[f]))
        copies[-1].start()
    for copy in copies:
        copy.wait()


SMEM = pl.BlockSpec(memory_space=pltpu.SMEM)
VMEM = pl.BlockSpec(memory_space=pltpu.VMEM)
HBM = pl.BlockSpec(memory_space=pltpu.HBM)
ANY = pl.BlockSpec(memory_space=pl.ANY)
LIMIT = 48 << 20


def struct(*shape):
    return jax.ShapeDtypeStruct(shape, jnp.float32)


def in_hbm(array):
    return pltpu.with_memory_space_constraint(array, pltpu.HBM)


def pack(cells, *small):
    return pl.pallas_call(
        pack_kernel,
        out_shape=(
            pltpu.SMEM((1, 40), jnp.int32),
            struct(4 * SWEEP_ROWS, 128),
            struct(24, FACE_ROWS, 128),
        )
        + (struct(4, FACE_ROWS, 128),) * 4,
        in_specs=[HBM] * (1 + len(small)),
        out_specs=(SMEM,) + (VMEM,) * 6,
        scratch_shapes=[
            pltpu.VMEM(cells.shape, jnp.float32),
            *[pltpu.SMEM(array.shape, jnp.int32) for array in small],
            pltpu.SemaphoreType.DMA((5,)),
            pltpu.SemaphoreType.DMA((len(small),)),
        ],
        compiler_params=pltpu.CompilerParams(vmem_limit_bytes=LIMIT),
        name="pack",
    )(*[in_hbm(array) for array in (cells, *small)])


def update(name, half, blocks, send_x, send_y, numbers, sweep, table, received, handed=(), after=()):
    counts = tuple(len(arrays) for arrays in received)
    flat = [array for arrays in received for array in arrays]
    return pl.pallas_call(
        functools.partial(update_kernel, half, blocks, counts, len(handed)),
        out_shape=(
            *[struct(BLOCK_ROWS + extra, 128) for _, extra in blocks],
            *[struct(*array.shape) for array in handed],
        ),
        in_specs=[SMEM] * 3 + [VMEM] * (2 + len(flat) + len(handed)) + [ANY] * len(after),
        out_specs=(VMEM,) * (len(blocks) + len(handed)),
        scratch_shapes=[
            pltpu.VMEM((16, FACE_ROWS, 128), jnp.float32),
            pltpu.VMEM((5 * GHOST_ROWS, 128), jnp.float32),
            pltpu.VMEM((SWEEP_ROWS, 128), jnp.float32),
        ],
        compiler_params=pltpu.CompilerParams(vmem_limit_bytes=LIMIT),
        name=name,
    )(send_x, send_y, numbers, sweep.reshape(4, SWEEP_ROWS, 128), table, *flat, *handed, *after)


def place(name, half, numbers, from_y, from_x, own, *before):
    return pl.pallas_call(
        functools.partial(place_kernel, half),
        out_shape=struct(5, 3, B * B * B),
        in_specs=[SMEM] + [VMEM] * 3 + [HBM] * len(before),
        out_specs=HBM,
        scratch_shapes=[
            pltpu.VMEM((3 * BLOCK_ROWS, 128), jnp.float32),
            pltpu.VMEM((5, 3, B * B * B), jnp.float32),
            pltpu.SemaphoreType.DMA((5,)),
        ],
        input_output_aliases={4: 0} if before else {},
        compiler_params=pltpu.CompilerParams(vmem_limit_bytes=LIMIT),
        name=name,
    )(numbers, from_y, from_x, own, *before)


def exchange(values, move, sends):
    count_x, count_y = lax.axis_size("bx"), lax.axis_size("by")
    pairs = []
    for i in range(count_x):
        for j in range(count_y):
            to_i, to_j = move(i, j)
            to_i, to_j = to_i % count_x, to_j % count_y
            if sends(j, to_j):
                pairs.append((i * count_y + j, to_i * count_y + to_j))
    return lax.ppermute(values, ("bx", "by"), pairs)


def on_device(cells_in, block_levels, send_x, send_y, layout, face_out, ghost_src):
    half_x, half_y = lax.axis_size("bx") // 2, lax.axis_size("by") // 2
    pairings = (
        lambda i, j: (i, ((j + 1) ^ 1) - 1),
        lambda i, j: (((i + 1) ^ 1) - 1, j),
        lambda i, j: (i ^ 1, j),
        lambda i, j: (i, j ^ 1),
    )

    def upper(j, to_j):
        return j >= half_y or to_j >= half_y

    def lower(j, to_j):
        return not upper(j, to_j)

    def anyone(j, to_j):
        return True

    def by_partner(i, j):
        return i, j ^ half_y

    def bx_partner(i, j):
        return i ^ half_x, j

    numbers, sweep, table, *messages = pack(
        cells_in.transpose(1, 0, 2), layout, block_levels, ghost_src, face_out
    )
    common = (send_x, send_y, numbers, sweep, table)
    early = [
        exchange(m, pairing, sends)
        for m, pairing, sends in zip(messages, pairings, (anyone, upper, upper, upper))
    ]
    upper_faces = [[r] for r in early]
    y_upper, *messages = update(
        "y_upper", True, ((1, 0),), *common, upper_faces, handed=messages[1:]
    )
    y_from_upper = exchange(y_upper, by_partner, lambda j, to_j: j >= half_y)
    late = [exchange(m, pairing, lower) for m, pairing in zip(messages, pairings[1:])]
    lower_faces = [[r] for r in (early[0], *late)]
    (x_lower,) = update("x_lower", False, ((0, 8),), *common, lower_faces, after=(y_upper,))
    x_from_lower = exchange(x_lower, bx_partner, lower)
    (y_lower,) = update("y_lower", False, ((1, 0),), *common, lower_faces, after=(x_lower,))
    y_from_lower = exchange(y_lower, by_partner, lambda j, to_j: j < half_y)
    (x_upper,) = update(
        "x_upper", True, ((0, 0),), *common, upper_faces, after=(y_lower, y_from_upper)
    )
    x_from_upper = exchange(x_upper, bx_partner, upper)
    all_faces = [[early[0]], *[list(pair) for pair in zip(early[1:], late)]]
    (own,) = update("own", None, ((2, 0),), *common, all_faces, after=(x_upper,))
    out = place("place_lower", False, numbers, y_from_upper, x_from_lower, own)
    out = place("place_upper", True, numbers, y_from_lower, x_from_upper, own, out)
    return out.transpose(1, 0, 2)


def solution(mesh):
    return jax.shard_map(
        on_device,
        mesh=mesh,
        in_specs=(
            P(("bx", "by"), None, None),
            P(("bx", "by")),
            P(("bx", "by"), None),
            P(("bx", "by"), None),
            P(("bx", "by"), None),
            P(("bx", "by"), None, None),
            P(("bx", "by"), None, None),
        ),
        out_specs=P(("bx", "by"), None, None),
        check_vma=False,
    )
```

```python
import functools

import jax
import jax.numpy as jnp
from jax import lax
from jax.experimental import pallas as pl
from jax.experimental.pallas import tpu as pltpu
from jax.sharding import PartitionSpec as P

B = 16
GAMMA = 1.4
STEP = 0.05
HALF = 8
FIELD_ROWS = B * 8
SWEEP_ROWS = 5 * FIELD_ROWS
BLOCK_ROWS = 5 * 2 * B
FACE_ROWS = 24
GHOST_ROWS = 4 * 8


def slot_of(field, direction):
    if field == 1:
        return 1 + direction
    if field == 1 + direction:
        return 1
    return field


def lanes(shape=(8, 128)):
    return lax.broadcasted_iota(jnp.int32, shape, 1)


def rows(shape=(8, 128)):
    return lax.broadcasted_iota(jnp.int32, shape, 0)


def take(values, index, axis):
    return jnp.take_along_axis(values, index, axis=axis, mode="promise_in_bounds")


class Turns:
    def __init__(self):
        lane, row = lanes(), rows()
        group, inner = lane // 16, lane % 16
        self.low = inner < 8
        self.skew = ((group + row) % 8) * 16 + inner
        self.shift = (row - group) % 8
        self.back = ((row - group) % 8) * 16 + inner
        self.skew_half = ((group + row) % 8) * 16 + (inner + 8) % 16
        self.back_half = ((row - group) % 8) * 16 + (inner + 8) % 16
        source_group = (group + row) % 8
        self.skew_z = (inner % 8) * 16 + (inner // 8) * 8 + source_group
        self.skew_z_half = (inner % 8) * 16 + (1 - inner // 8) * 8 + source_group
        z_low, z_high = inner % 8, inner // 8
        self.back_z = ((row - z_low) % 8) * 16 + z_high * 8 + group
        self.back_z_half = ((row - z_low) % 8) * 16 + (1 - z_high) * 8 + group

    def turn(self, v):
        return take(take(take(v, self.skew, 1), self.shift, 0), self.back, 1)

    def from_z(self, first, second):
        a, b = take(first, self.skew, 1), take(second, self.skew_half, 1)
        t0 = take(jnp.where(self.low, a, b), self.shift, 0)
        t1 = take(jnp.where(self.low, b, a), self.shift, 0)
        return take(t0, self.back_z, 1), take(t1, self.back_z_half, 1)


def parities():
    return lax.axis_index("bx") % 2, lax.axis_index("by") % 2


def pack_kernel(
    cells_in, layout_in, levels_in, ghost_src_in, face_out_in, *rest
):
    numbers, sweep, table, *messages = rest[:7]
    cells, layout, levels, ghost_src, face_out, cells_sem, small_sem = rest[7:]
    odd_x, odd_y = parities()
    copies = [
        pltpu.make_async_copy(cells_in.at[f], cells.at[f], cells_sem.at[f]) for f in range(5)
    ]
    small = [
        pltpu.make_async_copy(source, target, small_sem.at[i])
        for i, (source, target) in enumerate(
            (
                (face_out_in, face_out),
                (layout_in, layout),
                (levels_in, levels),
                (ghost_src_in, ghost_src),
            )
        )
    ]
    for copy in copies + small:
        copy.start()
    turns = Turns()
    for field in range(5):
        base = field * FIELD_ROWS
        to_y = slot_of(field, 1) * FIELD_ROWS
        to_z = slot_of(field, 2) * FIELD_ROWS
        copies[field].wait()
        for t in range(2 * B):
            row = base + (t // 2) * 8 + t % 2
            sweep[pl.ds(row, 4, stride=SWEEP_ROWS), :] = cells[
                field, :, t * 128 : (t + 1) * 128
            ]
        places = [(s * SWEEP_ROWS, xh) for s in range(4) for xh in range(2)]
        v = [
            sweep[pl.ds(first + base + HALF * xh * 8 + h, 8, stride=8), :]
            for first, xh in places
            for h in range(2)
        ]
        y = [take(a, turns.skew, 1) for a in v]
        z = [take(a, (turns.skew_z, turns.skew_z_half)[k % 2], 1) for k, a in enumerate(v)]
        y = [take(a, turns.shift, 0) for a in y]
        z = [take(a, turns.shift, 0) for a in z]
        y = [take(a, turns.back, 1) for a in y]
        pairs = list(zip(z[::2], z[1::2]))
        ones = [take(jnp.where(turns.low, a, b), turns.back, 1) for a, b in pairs]
        twos = [take(jnp.where(turns.low, b, a), turns.back_half, 1) for a, b in pairs]
        for k, (first, xh) in enumerate(places):
            for h in range(2):
                start = first + to_y + HALF * h * 8 + 2 + xh
                sweep[pl.ds(start, 8, stride=8), :] = y[2 * k + h]
            for zh, value in enumerate((ones[k], twos[k])):
                start = first + to_z + HALF * zh * 8 + 4 + xh
                sweep[pl.ds(start, 8, stride=8), :] = value
    for s in range(4):
        for face in range(6):
            direction, high = face // 2, face % 2
            for layer in range(2):
                i = B - 1 - layer if high else layer
                for h in range(2):
                    row = s * SWEEP_ROWS + i * 8 + direction * 2 + h
                    to = (layer * 2 + h) * 5
                    table[s * 6 + face, to : to + 5, :] = sweep[
                        pl.ds(row, 5, stride=FIELD_ROWS), :
                    ]
                    if direction:
                        for field, slot in ((1, 1 + direction), (1 + direction, 1)):
                            table[s * 6 + face, to + field : to + field + 1, :] = sweep[
                                pl.ds(slot * FIELD_ROWS + row, 1), :
                            ]
    for copy in small:
        copy.wait()
    for m, one_list in enumerate((2 + (1 - odd_y), 1 - odd_x, odd_x, 2 + odd_y)):
        for k in range(4):
            messages[m][k] = table[face_out[0, one_list, k]]
    codes = [layout[0, j] for j in range(3)]
    kept = functools.reduce(jnp.maximum, [jnp.where(c < 4, c, 0) for c in codes])
    listed = {}
    listed.update({3 + j: codes[j] for j in range(3)})
    listed.update({8 + j: levels[j] for j in range(4)})
    listed.update({12 + s * 6 + f: ghost_src[0, s, f] for s in range(4) for f in range(6)})
    for i in range(3, 40):
        numbers[0, i] = listed.get(i, 0)
    numbers[0, 2] = kept


def limited(left, right):
    return jnp.maximum(jnp.minimum(left, right), 0.0) + jnp.minimum(jnp.maximum(left, right), 0.0)


def fluxes_of(q):
    density, normal, second, third, pressure = q
    mass = density * normal
    kinetic = 0.5 * density * (normal * normal + second * second + third * third)
    energy = pressure * (1.0 / (GAMMA - 1.0)) + kinetic
    cons = (density, mass, density * second, density * third, energy)
    flux = (mass, mass * normal + pressure, mass * second, mass * third, normal * (energy + pressure))
    scaled = GAMMA * pressure
    signal = jnp.abs(normal) + scaled * lax.rsqrt(scaled * density)
    return cons, flux, signal


def step_of(level):
    return jnp.where(level == 0, STEP, jnp.where(level == 1, STEP * 2, STEP * 4))


def upper_half():
    return lax.axis_index("by") >= lax.axis_size("by") // 2


def update_kernel(half, blocks, counts, handed, send_x, send_y, numbers, sweep, table, *rest):
    received, rest = rest[: sum(counts)], rest[sum(counts) :]
    scratch = rest[-3:]
    outs = rest[-3 - len(blocks) - handed : -3 - handed]
    for source, target in zip(rest[:handed], rest[-3 - handed : -3]):
        target[...] = source[...]

    def body():
        remote = scratch[0]
        first = 0
        for m, count in enumerate(counts):
            for k in range(4):
                remote[m * 4 + k] = sum(array[k] for array in received[first : first + count])
            first += count
        for (which, extra), out in zip(blocks, outs):
            s = (send_x[0, 0], send_y[0, 0], numbers[0, 2])[which]
            update_body(s, numbers, sweep, table, out, *scratch)
            if extra:
                out[BLOCK_ROWS : BLOCK_ROWS + extra, :] = jnp.zeros((extra, 128), jnp.float32)

    if half is None:
        body()
    else:
        pl.when(upper_half() == half)(body)


def update_body(s, numbers, sweep, table, out, remote, ghost, change):
    turns = Turns()
    odd_x, odd_y = parities()
    ratio = step_of(numbers[0, 8 + s])
    for face in range(6):
        direction, high = face // 2, face % 2
        code = numbers[0, 12 + s * 6 + face]
        far = jnp.maximum(code - 24, 0)
        which = far // 4
        along_x = jnp.where(which == odd_x, 1, 2)
        along_y = jnp.where(which - 2 == odd_y, 0, 3)
        far = jnp.where(which < 2, along_x, along_y) * 4 + far % 4
        near = jnp.minimum(code, 23)
        for layer in range(2):
            i = 2 + layer if high else 1 - layer
            for h in range(2):
                row = i * 8 + direction * 2 + h
                at = (layer * 2 + h) * 5
                moves = [(pl.ds(at, 5), pl.ds(row, 5, stride=GHOST_ROWS))]
                if direction:
                    for field, to in ((1, 1 + direction), (1 + direction, 1)):
                        moves.append((pl.ds(at + field, 1), pl.ds(to * GHOST_ROWS + row, 1)))
                for source, target in moves:
                    ghost[target, :] = jnp.where(
                        code < 24, table[near, source, :], remote[far, source, :]
                    )

    def cells_at(i):
        if 0 <= i < B:
            return [sweep[s, pl.ds(f * FIELD_ROWS + i * 8, 8), :] for f in range(5)]
        k = i + 2 if i < 0 else i - B + 2
        return [ghost[pl.ds(f * GHOST_ROWS + k * 8, 8), :] for f in range(5)]

    here, after = cells_at(-2), cells_at(-1)
    right = [b - a for a, b in zip(here, after)]
    left_face = last_flux = None
    for i in range(-1, B + 1):
        here, after, left = after, cells_at(i + 2 - 1), right
        right = [b - a for a, b in zip(here, after)]
        half = [0.5 * limited(a, b) for a, b in zip(left, right)]
        density, normal, _, _, pressure = here
        carried = ratio * normal
        moved = [carried * a for a in half]
        centre = [
            density - (moved[0] + ratio * density * half[1]),
            normal - (moved[1] + ratio * half[4] / density),
            here[2] - moved[2],
            here[3] - moved[3],
            pressure - (moved[4] + (ratio * GAMMA) * pressure * half[1]),
        ]
        if i >= 0:
            cons, flux, signal = fluxes_of([a - b for a, b in zip(centre, half)])
            old_cons, old_flux, old_signal = left_face
            speed = jnp.maximum(signal, old_signal)
            face_flux = [
                (fa + fb) - speed * (ub - ua)
                for fa, fb, ua, ub in zip(old_flux, flux, old_cons, cons)
            ]
            if i >= 1:
                for f in range(5):
                    change[pl.ds(f * FIELD_ROWS + (i - 1) * 8, 8), :] = face_flux[f] - last_flux[f]
            last_flux = face_flux
        if i < B:
            left_face = fluxes_of([a + b for a, b in zip(centre, half)])

    def in_place(ref, start):
        return ref[pl.ds(start, 8, stride=8), :]

    scale = 0.5 * ratio
    for xh in range(2):
        prims = [
            [sweep[s, pl.ds(f * FIELD_ROWS + HALF * xh * 8 + h, 8, stride=8), :] for h in range(2)]
            for f in range(5)
        ]
        for f in range(5):
            along_y = slot_of(f, 1) * FIELD_ROWS
            along_z = slot_of(f, 2) * FIELD_ROWS
            from_z = turns.from_z(
                *[in_place(change, along_z + HALF * zh * 8 + 4 + xh) for zh in range(2)]
            )
            for h in range(2):
                total = (
                    in_place(change, f * FIELD_ROWS + HALF * xh * 8 + h)
                    + turns.turn(in_place(change, along_y + HALF * h * 8 + 2 + xh))
                    + from_z[h]
                )
                density, u, v, w, pressure = (prims[k][h] for k in range(5))
                if f == 0:
                    initial = density
                elif f < 4:
                    initial = density * prims[f][h]
                else:
                    initial = pressure * (1.0 / (GAMMA - 1.0)) + 0.5 * density * (
                        u * u + v * v + w * w
                    )
                row = f * 2 * B + h * B + HALF * xh
                out[row : row + 8, :] = initial - scale * total


def place_kernel(half, numbers, from_y, from_x, own, *rest):
    @pl.when(upper_half() == half)
    def _():
        place_body(numbers, from_y, from_x, own, *rest[-4:])


def place_body(numbers, from_y, from_x, own, out, slots, staged, sems):
    codes = [numbers[0, 3 + j] for j in range(3)]
    at_x = jnp.where(codes[1] == 4, 1, jnp.where(codes[2] == 4, 2, 0))
    at_y = jnp.where(codes[1] == 5, 1, jnp.where(codes[2] == 5, 2, 0))
    at_own = 3 - at_x - at_y
    empty = codes[0] + codes[1] + codes[2] == 8
    copies = []
    for f in range(5):
        one = pl.ds(f * 2 * B, 2 * B)
        values = (
            (jnp.where(empty, 0.0, own[one, :]), at_own),
            (from_x[one, :], at_x),
            (from_y[one, :], at_y),
        )
        for v, at in values:
            slots[pl.ds(pl.multiple_of(at * BLOCK_ROWS + f * 2 * B, 2 * B), 2 * B), :] = v
        for t in range(2 * B):
            row = f * 2 * B + (t % 2) * B + t // 2
            staged[f, :, t * 128 : (t + 1) * 128] = slots[pl.ds(row, 3, stride=BLOCK_ROWS), :]
        copies.append(pltpu.make_async_copy(staged.at[f], out.at[f], sems.at[f]))
        copies[-1].start()
    for copy in copies:
        copy.wait()


SMEM = pl.BlockSpec(memory_space=pltpu.SMEM)
VMEM = pl.BlockSpec(memory_space=pltpu.VMEM)
HBM = pl.BlockSpec(memory_space=pltpu.HBM)
ANY = pl.BlockSpec(memory_space=pl.ANY)
LIMIT = 48 << 20


def struct(*shape):
    return jax.ShapeDtypeStruct(shape, jnp.float32)


def in_hbm(array):
    return pltpu.with_memory_space_constraint(array, pltpu.HBM)


def pack(cells, *small):
    return pl.pallas_call(
        pack_kernel,
        out_shape=(
            pltpu.SMEM((1, 40), jnp.int32),
            struct(4 * SWEEP_ROWS, 128),
            struct(24, FACE_ROWS, 128),
        )
        + (struct(4, FACE_ROWS, 128),) * 4,
        in_specs=[HBM] * (1 + len(small)),
        out_specs=(SMEM,) + (VMEM,) * 6,
        scratch_shapes=[
            pltpu.VMEM(cells.shape, jnp.float32),
            *[pltpu.SMEM(array.shape, jnp.int32) for array in small],
            pltpu.SemaphoreType.DMA((5,)),
            pltpu.SemaphoreType.DMA((len(small),)),
        ],
        compiler_params=pltpu.CompilerParams(vmem_limit_bytes=LIMIT),
        name="pack",
    )(*[in_hbm(array) for array in (cells, *small)])


def update(name, half, blocks, send_x, send_y, numbers, sweep, table, received, handed=(), after=()):
    counts = tuple(len(arrays) for arrays in received)
    flat = [array for arrays in received for array in arrays]
    return pl.pallas_call(
        functools.partial(update_kernel, half, blocks, counts, len(handed)),
        out_shape=(
            *[struct(BLOCK_ROWS + extra, 128) for _, extra in blocks],
            *[struct(*array.shape) for array in handed],
        ),
        in_specs=[SMEM] * 3 + [VMEM] * (2 + len(flat) + len(handed)) + [ANY] * len(after),
        out_specs=(VMEM,) * (len(blocks) + len(handed)),
        scratch_shapes=[
            pltpu.VMEM((16, FACE_ROWS, 128), jnp.float32),
            pltpu.VMEM((5 * GHOST_ROWS, 128), jnp.float32),
            pltpu.VMEM((SWEEP_ROWS, 128), jnp.float32),
        ],
        compiler_params=pltpu.CompilerParams(vmem_limit_bytes=LIMIT),
        name=name,
    )(send_x, send_y, numbers, sweep.reshape(4, SWEEP_ROWS, 128), table, *flat, *handed, *after)


def place(name, half, numbers, from_y, from_x, own, *before):
    return pl.pallas_call(
        functools.partial(place_kernel, half),
        out_shape=struct(5, 3, B * B * B),
        in_specs=[SMEM] + [VMEM] * 3 + [HBM] * len(before),
        out_specs=HBM,
        scratch_shapes=[
            pltpu.VMEM((3 * BLOCK_ROWS, 128), jnp.float32),
            pltpu.VMEM((5, 3, B * B * B), jnp.float32),
            pltpu.SemaphoreType.DMA((5,)),
        ],
        input_output_aliases={4: 0} if before else {},
        compiler_params=pltpu.CompilerParams(vmem_limit_bytes=LIMIT),
        name=name,
    )(numbers, from_y, from_x, own, *before)


def exchange(values, move, sends):
    count_x, count_y = lax.axis_size("bx"), lax.axis_size("by")
    pairs = []
    for i in range(count_x):
        for j in range(count_y):
            to_i, to_j = move(i, j)
            to_i, to_j = to_i % count_x, to_j % count_y
            if sends(j, to_j):
                pairs.append((i * count_y + j, to_i * count_y + to_j))
    return lax.ppermute(values, ("bx", "by"), pairs)


def on_device(cells_in, block_levels, send_x, send_y, layout, face_out, ghost_src):
    half_x, half_y = lax.axis_size("bx") // 2, lax.axis_size("by") // 2
    pairings = (
        lambda i, j: (i, ((j + 1) ^ 1) - 1),
        lambda i, j: (((i + 1) ^ 1) - 1, j),
        lambda i, j: (i ^ 1, j),
        lambda i, j: (i, j ^ 1),
    )

    def upper(j, to_j):
        return j >= half_y or to_j >= half_y

    def lower(j, to_j):
        return not upper(j, to_j)

    def anyone(j, to_j):
        return True

    def by_partner(i, j):
        return i, j ^ half_y

    def bx_partner(i, j):
        return i ^ half_x, j

    numbers, sweep, table, *messages = pack(
        cells_in.transpose(1, 0, 2), layout, block_levels, ghost_src, face_out
    )
    common = (send_x, send_y, numbers, sweep, table)
    early = [
        exchange(m, pairing, sends)
        for m, pairing, sends in zip(messages, pairings, (anyone, upper, upper, upper))
    ]
    upper_faces = [[r] for r in early]
    y_upper, *messages = update(
        "y_upper", True, ((1, 0),), *common, upper_faces, handed=messages[1:]
    )
    y_from_upper = exchange(y_upper, by_partner, lambda j, to_j: j >= half_y)
    late = [exchange(m, pairing, lower) for m, pairing in zip(messages, pairings[1:])]
    lower_faces = [[r] for r in (early[0], *late)]
    (y_lower,) = update("y_lower", False, ((1, 8),), *common, lower_faces, after=(y_upper,))
    y_from_lower = exchange(y_lower, by_partner, lambda j, to_j: j < half_y)
    (x_lower,) = update("x_lower", False, ((0, 0),), *common, lower_faces, after=(y_lower,))
    x_from_lower = exchange(x_lower, bx_partner, lower)
    (x_upper,) = update(
        "x_upper", True, ((0, 0),), *common, upper_faces, after=(x_lower, y_from_upper)
    )
    x_from_upper = exchange(x_upper, bx_partner, upper)
    all_faces = [[early[0]], *[list(pair) for pair in zip(early[1:], late)]]
    (own,) = update("own", None, ((2, 0),), *common, all_faces, after=(x_upper,))
    out = place("place_lower", False, numbers, y_from_upper, x_from_lower, own)
    out = place("place_upper", True, numbers, y_from_lower, x_from_upper, own, out)
    return out.transpose(1, 0, 2)


def solution(mesh):
    return jax.shard_map(
        on_device,
        mesh=mesh,
        in_specs=(
            P(("bx", "by"), None, None),
            P(("bx", "by")),
            P(("bx", "by"), None),
            P(("bx", "by"), None),
            P(("bx", "by"), None),
            P(("bx", "by"), None, None),
            P(("bx", "by"), None, None),
        ),
        out_specs=P(("bx", "by"), None, None),
        check_vma=False,
    )
```

```python
import functools

import jax
import jax.numpy as jnp
from jax import lax
from jax.experimental import pallas as pl
from jax.experimental.pallas import tpu as pltpu
from jax.sharding import PartitionSpec as P

B = 16
GAMMA = 1.4
STEP = 0.05
HALF = 8
FIELD_ROWS = B * 8
SWEEP_ROWS = 5 * FIELD_ROWS
BLOCK_ROWS = 5 * 2 * B
FACE_ROWS = 24
GHOST_ROWS = 4 * 8


def slot_of(field, direction):
    if field == 1:
        return 1 + direction
    if field == 1 + direction:
        return 1
    return field


def lanes(shape=(8, 128)):
    return lax.broadcasted_iota(jnp.int32, shape, 1)


def rows(shape=(8, 128)):
    return lax.broadcasted_iota(jnp.int32, shape, 0)


def take(values, index, axis):
    return jnp.take_along_axis(values, index, axis=axis, mode="promise_in_bounds")


class Turns:
    def __init__(self):
        lane, row = lanes(), rows()
        group, inner = lane // 16, lane % 16
        self.low = inner < 8
        self.skew = ((group + row) % 8) * 16 + inner
        self.shift = (row - group) % 8
        self.back = ((row - group) % 8) * 16 + inner
        self.skew_half = ((group + row) % 8) * 16 + (inner + 8) % 16
        self.back_half = ((row - group) % 8) * 16 + (inner + 8) % 16
        source_group = (group + row) % 8
        self.skew_z = (inner % 8) * 16 + (inner // 8) * 8 + source_group
        self.skew_z_half = (inner % 8) * 16 + (1 - inner // 8) * 8 + source_group
        z_low, z_high = inner % 8, inner // 8
        self.back_z = ((row - z_low) % 8) * 16 + z_high * 8 + group
        self.back_z_half = ((row - z_low) % 8) * 16 + (1 - z_high) * 8 + group

    def turn(self, v):
        return take(take(take(v, self.skew, 1), self.shift, 0), self.back, 1)

    def from_z(self, first, second):
        a, b = take(first, self.skew, 1), take(second, self.skew_half, 1)
        t0 = take(jnp.where(self.low, a, b), self.shift, 0)
        t1 = take(jnp.where(self.low, b, a), self.shift, 0)
        return take(t0, self.back_z, 1), take(t1, self.back_z_half, 1)


def parities():
    return lax.axis_index("bx") % 2, lax.axis_index("by") % 2


def pack_kernel(
    cells_in, layout_in, levels_in, ghost_src_in, face_out_in, *rest
):
    numbers, sweep, table, *messages = rest[:7]
    cells, layout, levels, ghost_src, face_out, cells_sem, small_sem = rest[7:]
    odd_x, odd_y = parities()
    copies = [
        pltpu.make_async_copy(cells_in.at[f], cells.at[f], cells_sem.at[f]) for f in range(5)
    ]
    small = [
        pltpu.make_async_copy(source, target, small_sem.at[i])
        for i, (source, target) in enumerate(
            (
                (face_out_in, face_out),
                (layout_in, layout),
                (levels_in, levels),
                (ghost_src_in, ghost_src),
            )
        )
    ]
    for copy in copies + small:
        copy.start()
    turns = Turns()
    for field in range(5):
        base = field * FIELD_ROWS
        to_y = slot_of(field, 1) * FIELD_ROWS
        to_z = slot_of(field, 2) * FIELD_ROWS
        copies[field].wait()
        for t in range(2 * B):
            row = base + (t // 2) * 8 + t % 2
            sweep[pl.ds(row, 4, stride=SWEEP_ROWS), :] = cells[
                field, :, t * 128 : (t + 1) * 128
            ]
        places = [(s * SWEEP_ROWS, xh) for s in range(4) for xh in range(2)]
        v = [
            sweep[pl.ds(first + base + HALF * xh * 8 + h, 8, stride=8), :]
            for first, xh in places
            for h in range(2)
        ]
        y = [take(a, turns.skew, 1) for a in v]
        z = [take(a, (turns.skew_z, turns.skew_z_half)[k % 2], 1) for k, a in enumerate(v)]
        y = [take(a, turns.shift, 0) for a in y]
        z = [take(a, turns.shift, 0) for a in z]
        y = [take(a, turns.back, 1) for a in y]
        pairs = list(zip(z[::2], z[1::2]))
        ones = [take(jnp.where(turns.low, a, b), turns.back, 1) for a, b in pairs]
        twos = [take(jnp.where(turns.low, b, a), turns.back_half, 1) for a, b in pairs]
        for k, (first, xh) in enumerate(places):
            for h in range(2):
                start = first + to_y + HALF * h * 8 + 2 + xh
                sweep[pl.ds(start, 8, stride=8), :] = y[2 * k + h]
            for zh, value in enumerate((ones[k], twos[k])):
                start = first + to_z + HALF * zh * 8 + 4 + xh
                sweep[pl.ds(start, 8, stride=8), :] = value
    for s in range(4):
        for face in range(6):
            direction, high = face // 2, face % 2
            for layer in range(2):
                i = B - 1 - layer if high else layer
                for h in range(2):
                    row = s * SWEEP_ROWS + i * 8 + direction * 2 + h
                    to = (layer * 2 + h) * 5
                    table[s * 6 + face, to : to + 5, :] = sweep[
                        pl.ds(row, 5, stride=FIELD_ROWS), :
                    ]
                    if direction:
                        for field, slot in ((1, 1 + direction), (1 + direction, 1)):
                            table[s * 6 + face, to + field : to + field + 1, :] = sweep[
                                pl.ds(slot * FIELD_ROWS + row, 1), :
                            ]
    for copy in small:
        copy.wait()
    upper = upper_half()
    other, same = 1 - odd_x, odd_x
    second, third = jnp.where(upper, other, same), jnp.where(upper, same, other)
    for m, one_list in enumerate((2 + (1 - odd_y), second, third, 2 + odd_y)):
        for k in range(4):
            messages[m][k] = table[face_out[0, one_list, k]]
    codes = [layout[0, j] for j in range(3)]
    kept = functools.reduce(jnp.maximum, [jnp.where(c < 4, c, 0) for c in codes])
    listed = {}
    listed.update({3 + j: codes[j] for j in range(3)})
    listed.update({8 + j: levels[j] for j in range(4)})
    listed.update({12 + s * 6 + f: ghost_src[0, s, f] for s in range(4) for f in range(6)})
    for i in range(3, 40):
        numbers[0, i] = listed.get(i, 0)
    numbers[0, 2] = kept


def limited(left, right):
    return jnp.maximum(jnp.minimum(left, right), 0.0) + jnp.minimum(jnp.maximum(left, right), 0.0)


def fluxes_of(q):
    density, normal, second, third, pressure = q
    mass = density * normal
    kinetic = 0.5 * density * (normal * normal + second * second + third * third)
    energy = pressure * (1.0 / (GAMMA - 1.0)) + kinetic
    cons = (density, mass, density * second, density * third, energy)
    flux = (mass, mass * normal + pressure, mass * second, mass * third, normal * (energy + pressure))
    scaled = GAMMA * pressure
    signal = jnp.abs(normal) + scaled * lax.rsqrt(scaled * density)
    return cons, flux, signal


def step_of(level):
    return jnp.where(level == 0, STEP, jnp.where(level == 1, STEP * 2, STEP * 4))


def upper_half():
    return lax.axis_index("by") >= lax.axis_size("by") // 2


def update_kernel(half, blocks, counts, handed, send_x, send_y, numbers, sweep, table, *rest):
    received, rest = rest[: sum(counts)], rest[sum(counts) :]
    scratch = rest[-3:]
    outs = rest[-3 - len(blocks) - handed : -3 - handed]
    for source, target in zip(rest[:handed], rest[-3 - handed : -3]):
        target[...] = source[...]

    def body():
        remote = scratch[0]
        first = 0
        for m, count in enumerate(counts):
            for k in range(4):
                remote[m * 4 + k] = sum(array[k] for array in received[first : first + count])
            first += count
        for (which, extra), out in zip(blocks, outs):
            s = (send_x[0, 0], send_y[0, 0], numbers[0, 2])[which]
            update_body(s, numbers, sweep, table, out, *scratch)
            if extra:
                out[BLOCK_ROWS : BLOCK_ROWS + extra, :] = jnp.zeros((extra, 128), jnp.float32)

    if half is None:
        body()
    else:
        pl.when(upper_half() == half)(body)


def update_body(s, numbers, sweep, table, out, remote, ghost, change):
    turns = Turns()
    odd_x, odd_y = parities()
    ratio = step_of(numbers[0, 8 + s])
    for face in range(6):
        direction, high = face // 2, face % 2
        code = numbers[0, 12 + s * 6 + face]
        far = jnp.maximum(code - 24, 0)
        which = far // 4
        along_x = jnp.where(which == odd_x, 1, 2)
        along_y = jnp.where(which - 2 == odd_y, 0, 3)
        far = jnp.where(which < 2, along_x, along_y) * 4 + far % 4
        near = jnp.minimum(code, 23)
        for layer in range(2):
            i = 2 + layer if high else 1 - layer
            for h in range(2):
                row = i * 8 + direction * 2 + h
                at = (layer * 2 + h) * 5
                moves = [(pl.ds(at, 5), pl.ds(row, 5, stride=GHOST_ROWS))]
                if direction:
                    for field, to in ((1, 1 + direction), (1 + direction, 1)):
                        moves.append((pl.ds(at + field, 1), pl.ds(to * GHOST_ROWS + row, 1)))
                for source, target in moves:
                    ghost[target, :] = jnp.where(
                        code < 24, table[near, source, :], remote[far, source, :]
                    )

    def cells_at(i):
        if 0 <= i < B:
            return [sweep[s, pl.ds(f * FIELD_ROWS + i * 8, 8), :] for f in range(5)]
        k = i + 2 if i < 0 else i - B + 2
        return [ghost[pl.ds(f * GHOST_ROWS + k * 8, 8), :] for f in range(5)]

    here, after = cells_at(-2), cells_at(-1)
    right = [b - a for a, b in zip(here, after)]
    left_face = last_flux = None
    for i in range(-1, B + 1):
        here, after, left = after, cells_at(i + 2 - 1), right
        right = [b - a for a, b in zip(here, after)]
        half = [0.5 * limited(a, b) for a, b in zip(left, right)]
        density, normal, _, _, pressure = here
        carried = ratio * normal
        moved = [carried * a for a in half]
        centre = [
            density - (moved[0] + ratio * density * half[1]),
            normal - (moved[1] + ratio * half[4] / density),
            here[2] - moved[2],
            here[3] - moved[3],
            pressure - (moved[4] + (ratio * GAMMA) * pressure * half[1]),
        ]
        if i >= 0:
            cons, flux, signal = fluxes_of([a - b for a, b in zip(centre, half)])
            old_cons, old_flux, old_signal = left_face
            speed = jnp.maximum(signal, old_signal)
            face_flux = [
                (fa + fb) - speed * (ub - ua)
                for fa, fb, ua, ub in zip(old_flux, flux, old_cons, cons)
            ]
            if i >= 1:
                for f in range(5):
                    change[pl.ds(f * FIELD_ROWS + (i - 1) * 8, 8), :] = face_flux[f] - last_flux[f]
            last_flux = face_flux
        if i < B:
            left_face = fluxes_of([a + b for a, b in zip(centre, half)])

    def in_place(ref, start):
        return ref[pl.ds(start, 8, stride=8), :]

    scale = 0.5 * ratio
    for xh in range(2):
        prims = [
            [sweep[s, pl.ds(f * FIELD_ROWS + HALF * xh * 8 + h, 8, stride=8), :] for h in range(2)]
            for f in range(5)
        ]
        for f in range(5):
            along_y = slot_of(f, 1) * FIELD_ROWS
            along_z = slot_of(f, 2) * FIELD_ROWS
            from_z = turns.from_z(
                *[in_place(change, along_z + HALF * zh * 8 + 4 + xh) for zh in range(2)]
            )
            for h in range(2):
                total = (
                    in_place(change, f * FIELD_ROWS + HALF * xh * 8 + h)
                    + turns.turn(in_place(change, along_y + HALF * h * 8 + 2 + xh))
                    + from_z[h]
                )
                density, u, v, w, pressure = (prims[k][h] for k in range(5))
                if f == 0:
                    initial = density
                elif f < 4:
                    initial = density * prims[f][h]
                else:
                    initial = pressure * (1.0 / (GAMMA - 1.0)) + 0.5 * density * (
                        u * u + v * v + w * w
                    )
                row = f * 2 * B + h * B + HALF * xh
                out[row : row + 8, :] = initial - scale * total


def place_kernel(half, numbers, from_y, from_x, own, *rest):
    @pl.when(upper_half() == half)
    def _():
        place_body(numbers, from_y, from_x, own, *rest[-4:])


def place_body(numbers, from_y, from_x, own, out, slots, staged, sems):
    codes = [numbers[0, 3 + j] for j in range(3)]
    at_x = jnp.where(codes[1] == 4, 1, jnp.where(codes[2] == 4, 2, 0))
    at_y = jnp.where(codes[1] == 5, 1, jnp.where(codes[2] == 5, 2, 0))
    at_own = 3 - at_x - at_y
    empty = codes[0] + codes[1] + codes[2] == 8
    copies = []
    for f in range(5):
        one = pl.ds(f * 2 * B, 2 * B)
        values = (
            (jnp.where(empty, 0.0, own[one, :]), at_own),
            (from_x[one, :], at_x),
            (from_y[one, :], at_y),
        )
        for v, at in values:
            slots[pl.ds(pl.multiple_of(at * BLOCK_ROWS + f * 2 * B, 2 * B), 2 * B), :] = v
        for t in range(2 * B):
            row = f * 2 * B + (t % 2) * B + t // 2
            staged[f, :, t * 128 : (t + 1) * 128] = slots[pl.ds(row, 3, stride=BLOCK_ROWS), :]
        copies.append(pltpu.make_async_copy(staged.at[f], out.at[f], sems.at[f]))
        copies[-1].start()
    for copy in copies:
        copy.wait()


SMEM = pl.BlockSpec(memory_space=pltpu.SMEM)
VMEM = pl.BlockSpec(memory_space=pltpu.VMEM)
HBM = pl.BlockSpec(memory_space=pltpu.HBM)
ANY = pl.BlockSpec(memory_space=pl.ANY)
LIMIT = 48 << 20


def struct(*shape):
    return jax.ShapeDtypeStruct(shape, jnp.float32)


def in_hbm(array):
    return pltpu.with_memory_space_constraint(array, pltpu.HBM)


def pack(cells, *small):
    return pl.pallas_call(
        pack_kernel,
        out_shape=(
            pltpu.SMEM((1, 40), jnp.int32),
            struct(4 * SWEEP_ROWS, 128),
            struct(24, FACE_ROWS, 128),
        )
        + (struct(4, FACE_ROWS, 128),) * 4,
        in_specs=[HBM] * (1 + len(small)),
        out_specs=(SMEM,) + (VMEM,) * 6,
        scratch_shapes=[
            pltpu.VMEM(cells.shape, jnp.float32),
            *[pltpu.SMEM(array.shape, jnp.int32) for array in small],
            pltpu.SemaphoreType.DMA((5,)),
            pltpu.SemaphoreType.DMA((len(small),)),
        ],
        compiler_params=pltpu.CompilerParams(vmem_limit_bytes=LIMIT),
        name="pack",
    )(*[in_hbm(array) for array in (cells, *small)])


def update(name, half, blocks, send_x, send_y, numbers, sweep, table, received, handed=(), after=()):
    counts = tuple(len(arrays) for arrays in received)
    flat = [array for arrays in received for array in arrays]
    return pl.pallas_call(
        functools.partial(update_kernel, half, blocks, counts, len(handed)),
        out_shape=(
            *[struct(BLOCK_ROWS + extra, 128) for _, extra in blocks],
            *[struct(*array.shape) for array in handed],
        ),
        in_specs=[SMEM] * 3 + [VMEM] * (2 + len(flat) + len(handed)) + [ANY] * len(after),
        out_specs=(VMEM,) * (len(blocks) + len(handed)),
        scratch_shapes=[
            pltpu.VMEM((16, FACE_ROWS, 128), jnp.float32),
            pltpu.VMEM((5 * GHOST_ROWS, 128), jnp.float32),
            pltpu.VMEM((SWEEP_ROWS, 128), jnp.float32),
        ],
        compiler_params=pltpu.CompilerParams(vmem_limit_bytes=LIMIT),
        name=name,
    )(send_x, send_y, numbers, sweep.reshape(4, SWEEP_ROWS, 128), table, *flat, *handed, *after)


def place(name, half, numbers, from_y, from_x, own, *before):
    return pl.pallas_call(
        functools.partial(place_kernel, half),
        out_shape=struct(5, 3, B * B * B),
        in_specs=[SMEM] + [VMEM] * 3 + [HBM] * len(before),
        out_specs=HBM,
        scratch_shapes=[
            pltpu.VMEM((3 * BLOCK_ROWS, 128), jnp.float32),
            pltpu.VMEM((5, 3, B * B * B), jnp.float32),
            pltpu.SemaphoreType.DMA((5,)),
        ],
        input_output_aliases={4: 0} if before else {},
        compiler_params=pltpu.CompilerParams(vmem_limit_bytes=LIMIT),
        name=name,
    )(numbers, from_y, from_x, own, *before)


def exchange(values, move, sends):
    count_x, count_y = lax.axis_size("bx"), lax.axis_size("by")
    pairs = []
    for i in range(count_x):
        for j in range(count_y):
            to_i, to_j = move(i, j)
            to_i, to_j = to_i % count_x, to_j % count_y
            if sends(j, to_j):
                pairs.append((i * count_y + j, to_i * count_y + to_j))
    return lax.ppermute(values, ("bx", "by"), pairs)


def on_device(cells_in, block_levels, send_x, send_y, layout, face_out, ghost_src):
    half_x, half_y = lax.axis_size("bx") // 2, lax.axis_size("by") // 2
    pairings = (
        lambda i, j: (i, ((j + 1) ^ 1) - 1),
        lambda i, j: (((i + 1) ^ 1) - 1, j),
        lambda i, j: (i ^ 1, j),
        lambda i, j: (i, j ^ 1),
    )

    def upper(j, to_j):
        return j >= half_y or to_j >= half_y

    def lower(j, to_j):
        return not upper(j, to_j)

    def anyone(j, to_j):
        return True

    def by_partner(i, j):
        return i, j ^ half_y

    def bx_partner(i, j):
        return i ^ half_x, j

    numbers, sweep, table, *messages = pack(
        cells_in.transpose(1, 0, 2), layout, block_levels, ghost_src, face_out
    )
    common = (send_x, send_y, numbers, sweep, table)
    odd_by, odd_bx, even_bx, even_by = pairings

    def mixed(i, j):
        return (odd_bx if j >= half_y else even_bx)(i, j)

    first = exchange(messages[0], odd_by, anyone)
    second = exchange(messages[1], mixed, anyone)
    third = exchange(messages[2], even_bx, upper)
    fourth = exchange(messages[3], even_by, upper)
    upper_faces = [[first], [second], [third], [fourth]]
    y_upper, *messages = update(
        "y_upper", True, ((1, 0),), *common, upper_faces, handed=messages[2:]
    )
    y_from_upper = exchange(y_upper, by_partner, lambda j, to_j: j >= half_y)
    third = exchange(messages[0], odd_bx, lower)
    fourth = exchange(messages[1], even_by, lower)
    lower_faces = [[first], [third], [second], [fourth]]
    (x_lower,) = update("x_lower", False, ((0, 8),), *common, lower_faces, after=(y_upper,))
    x_from_lower = exchange(x_lower, bx_partner, lower)
    (y_lower,) = update("y_lower", False, ((1, 0),), *common, lower_faces, after=(x_lower,))
    y_from_lower = exchange(y_lower, by_partner, lambda j, to_j: j < half_y)
    (x_upper,) = update(
        "x_upper", True, ((0, 0),), *common, upper_faces, after=(y_lower, y_from_upper)
    )
    x_from_upper = exchange(x_upper, bx_partner, upper)
    (own_upper,) = update("own_upper", True, ((2, 0),), *common, upper_faces, after=(x_upper,))
    (own_lower,) = update("own_lower", False, ((2, 0),), *common, lower_faces, after=(x_upper,))
    out = place("place_lower", False, numbers, y_from_upper, x_from_lower, own_lower)
    out = place("place_upper", True, numbers, y_from_lower, x_from_upper, own_upper, out)
    return out.transpose(1, 0, 2)


def solution(mesh):
    return jax.shard_map(
        on_device,
        mesh=mesh,
        in_specs=(
            P(("bx", "by"), None, None),
            P(("bx", "by")),
            P(("bx", "by"), None),
            P(("bx", "by"), None),
            P(("bx", "by"), None),
            P(("bx", "by"), None, None),
            P(("bx", "by"), None, None),
        ),
        out_specs=P(("bx", "by"), None, None),
        check_vma=False,
    )
```
